32 devices in a mesh: groups: 2 (over x), gs: 8 (over z, y), sub: 2 (over core).
Axes of the slice: x: 2, y: 2, z: 4, core: 2. Of those that a mesh axis runs over, the one named last changes fastest.
Arguments:
- centres: float32 [3, 131072], P(None, ('groups', 'gs', 'sub')), parts along dimension 1, may hold values from -3 to 3
- log_scales: float32 [3, 131072], P(None, ('groups', 'gs', 'sub')), parts along dimension 1, may hold values from -3.7 to -1.4
- rotations: float32 [4, 131072], P(None, ('groups', 'gs', 'sub')), parts along dimension 1, may hold values from -1 to 2, as said below
- opacity_logits: float32 [131072], P(('groups', 'gs', 'sub')), parts along dimension 0, may hold values from -7 to -6.5
- colours: float32 [3, 131072], P(None, ('groups', 'gs', 'sub')), parts along dimension 1, may hold values from -6 to 6
- view_shift: float32 [8, 3], P('groups'), parts along dimension 0, may hold values from -0.2 to 0.2
- tile_ids: int32 [512], P(('groups', 'gs', 'sub')), parts along dimension 0, may hold values from 0 to 255, as said below
- tile_counts: int32 [512], P(('groups', 'gs', 'sub')), parts along dimension 0, may hold values from 256 to 512
- tile_lists: int32 [512, 512], P(('groups', 'gs', 'sub')), parts along dimension 0, may hold values from 0 to 4095, as said below
- send_index: int32 [32, 16, 256], P(('groups', 'gs', 'sub')), parts along dimension 0, may hold values from 0 to 16383, as said below
- image_cot: float32 [3, 131072], P(None, ('groups', 'gs', 'sub')), parts along dimension 1, may hold values from -6 to 6
Outputs:
- rendered: float32 [3, 131072], P(None, ('groups', 'gs', 'sub')), parts along dimension 1
- centre_grad: float32 [3, 131072], P(None, ('groups', 'gs', 'sub')), parts along dimension 1
- scale_grad: float32 [3, 131072], P(None, ('groups', 'gs', 'sub')), parts along dimension 1
- rotation_grad: float32 [4, 131072], P(None, ('groups', 'gs', 'sub')), parts along dimension 1
- opacity_grad: float32 [131072], P(('groups', 'gs', 'sub')), parts along dimension 0
- colour_grad: float32 [3, 131072], P(None, ('groups', 'gs', 'sub')), parts along dimension 1
The draws below stay inside these ranges and needn't reach their ends.
There are 2 independent parts, one for each index of `groups`. The reference program is written for one: setup_inputs(seed, part) draws one part's arguments, and reference() takes and returns one part's arrays. A program takes and returns all parts, laid end to end along the dimension named above; each array names one. Nothing has to cross between parts.
Inputs may be any that keep to these rules, and one draw needn't show every extreme that they name: `send_index`: entries are view * 4096 + g; a Gaussian g of a source appears at most once among all its sends. `tile_ids`: A permutation of all tiles. `tile_lists`: slot numbers s * 256 + j of the owning device's received Gaussians; the live entries of one list are distinct, and every slot is named by some live entry of its device. `rotations`: first component 1 to 2, the others -1 to 1.
All inputs are finite; a program needn't handle non-finite values.
Results may differ from the reference program's by a relative error of at most 0.0003.
Values sent between devices are 32-bit elements; how exact they have to be, the bound alone decides.
No kernel may reach another device: no remote copies, remote signals or barrier semaphores. Data moves between devices by JAX's collectives and lax.ppermute only.
A program may use at most 64 MiB of HBM per device.

```python
from functools import partial
import jax
import jax.numpy as jnp
from jax import lax

VIEWS = 4
TILES_X = 32
LIST = 512
TILE_DEV = 16
G_DEV = 4096
GROUP = 16
GAUSS = 65536
SLOTS = 4096
CAP = 256
TILES = 256
TILES_VIEW = 64
TILE_ROWS = 2
PIXELS = 65536


FOCAL = 512.0


def draw_shift(key):
    return jax.random.uniform(jax.random.fold_in(key, 101), (VIEWS, 3), jnp.float32, -0.2, 0.2)


def routing(key):
    key = jax.random.fold_in(key, 202)
    keys = jax.random.split(key, 5)
    pool_size = 2 * LIST
    quads_x = TILES_X // 2
    quads_view = TILES_VIEW // 4
    quad_dev = TILE_DEV // 4
    quad_order = jax.random.permutation(keys[0], TILES // 4).astype(jnp.int32)
    quad_view = quad_order // quads_view
    quad_rest = quad_order % quads_view
    quad_row = quad_rest // quads_x
    quad_col = quad_rest % quads_x
    corner = jnp.arange(4, dtype=jnp.int32)
    tile_order = (quad_view[:, None] * TILES_VIEW + (2 * quad_row[:, None] + corner[None, :] // 2) * TILES_X + 2 * quad_col[:, None] + corner[None, :] % 2).reshape(TILES)
    counts = jax.random.randint(keys[1], (GROUP, TILE_DEV), LIST // 2, LIST + 1).astype(jnp.int32)
    devices = jnp.arange(GROUP, dtype=jnp.int32)
    counts = jnp.where((devices < max(GROUP // 8, 1))[:, None], LIST, counts)
    counts = counts.at[GROUP - 1, 0].set(LIST // 2)
    positions = jnp.arange(LIST, dtype=jnp.int32)
    local = jnp.arange(TILE_DEV, dtype=jnp.int32)
    start = local % 4 * (pool_size // 4)
    wrap = jnp.maximum(start[None, :] + counts - pool_size, 0)
    is_live = positions[None, None, :] < counts[:, :, None]
    pool_idx = jnp.where(positions[None, None, :] < wrap[:, :, None], positions[None, None, :], start[None, :, None] + positions[None, None, :] - wrap[:, :, None])
    flat = jnp.where(is_live, (local // 4)[None, :, None] * pool_size + pool_idx, 0).reshape(GROUP, TILE_DEV * LIST)
    slot_perm = jax.vmap(lambda sub_key: jax.random.permutation(sub_key, SLOTS))(jax.random.split(keys[2], GROUP)).astype(jnp.int32)
    chosen = jnp.take_along_axis(slot_perm, flat, axis=1)
    filler = jax.random.randint(keys[3], (GROUP, TILE_DEV * LIST), 0, SLOTS).astype(jnp.int32)
    lists = jnp.where(is_live.reshape(GROUP, TILE_DEV * LIST), chosen, filler).reshape(TILES, LIST)
    inverse = jnp.zeros((GROUP, SLOTS), jnp.int32).at[devices[:, None], slot_perm].set(jnp.arange(SLOTS, dtype=jnp.int32)[None, :])
    home_quad = jnp.take_along_axis(quad_order.reshape(GROUP, quad_dev), inverse // pool_size, axis=1)
    pool_pos = inverse % pool_size
    home_quad = jnp.transpose(home_quad.reshape(GROUP, GROUP, CAP), (1, 0, 2))
    pool_pos = jnp.transpose(pool_pos.reshape(GROUP, GROUP, CAP), (1, 0, 2))
    gauss_perm = jax.vmap(lambda sub_key: jax.random.permutation(sub_key, G_DEV))(jax.random.split(keys[4], GROUP)).astype(jnp.int32)
    chosen_gauss = gauss_perm[:, :SLOTS].reshape(GROUP, GROUP, CAP)
    sends = home_quad // quads_view * G_DEV + chosen_gauss
    return (tile_order, counts.reshape(TILES), lists, sends, home_quad, pool_pos)


def draw_view_shift(key, part):
    return draw_shift(key)


def draw_tile_ids(key, part):
    return routing(key)[0]


def draw_tile_counts(key, part):
    return routing(key)[1]


def draw_tile_lists(key, part):
    return routing(key)[2]


def draw_send_index(key, part):
    return routing(key)[3]


def draw_rotations(key, part):
    key = jax.random.fold_in(key, 5)
    keys = jax.random.split(key, 2)
    first = jax.random.uniform(keys[0], (1, GAUSS), jnp.float32, 1.0, 2.0)
    others = jax.random.uniform(keys[1], (3, GAUSS), jnp.float32, -1.0, 1.0)
    return jnp.concatenate([first, others], axis=0)


def draw_centres(key, part):
    tile_order, counts, lists, sends, home_quad, pool_pos = routing(key)
    shift = draw_shift(key)
    key = jax.random.fold_in(key, 3)
    keys = jax.random.split(key, 4)
    base = jax.random.uniform(keys[0], (3, GROUP, G_DEV), jnp.float32, -1.0, 1.0)
    quads_x = TILES_X // 2
    quads_view = TILES_VIEW // 4
    view_of = home_quad // quads_view
    quad_rest = home_quad % quads_view
    pixel_u = (32 * (quad_rest % quads_x) + 16).astype(jnp.float32) + jax.random.uniform(keys[1], home_quad.shape, jnp.float32, -3.0, 3.0)
    pixel_v = (32 * (quad_rest // quads_x) + 16).astype(jnp.float32) + jax.random.uniform(keys[2], home_quad.shape, jnp.float32, -3.0, 3.0)
    depth = 3.0 + 2.0 * (pool_pos.astype(jnp.float32) + jax.random.uniform(keys[3], home_quad.shape, jnp.float32, 0.0, 1.0)) / (2 * LIST)
    world_x = (pixel_u - 8.0 * TILES_X) * depth / FOCAL - shift[view_of, 0]
    world_y = (pixel_v - 8.0 * TILE_ROWS) * depth / FOCAL - shift[view_of, 1]
    world_z = depth - 4.0 - shift[view_of, 2]
    source = jnp.broadcast_to(jnp.arange(GROUP, dtype=jnp.int32)[:, None, None], home_quad.shape)
    gauss_idx = sends % G_DEV
    base = base.at[0, source, gauss_idx].set(world_x)
    base = base.at[1, source, gauss_idx].set(world_y)
    base = base.at[2, source, gauss_idx].set(world_z)
    return base.reshape(3, GAUSS)


def block_scale(own_key, dims, pieces, least, top_value):
    def one(dim, blocks):
        steps = jax.random.uniform(jax.random.fold_in(jax.random.fold_in(own_key, 6), dim), (blocks,), jnp.float32, least / len(pieces), top_value / len(pieces))
        return jnp.repeat(jnp.exp(steps), dims[dim] // blocks).reshape((-1,) + (1,) * (len(dims) - dim - 1))

    level = one(*pieces[0])
    for cut in pieces[1:]:
        level = level * one(*cut)
    return level


def normal_values(key, shape, width, reach, cuts=(), kind=jnp.bfloat16):
    level = block_scale(key, shape, cuts, -0.22, 0.18) if cuts else 1.0
    drawn = jax.random.normal(key, shape, jnp.float32) * width * level
    return jnp.minimum(jnp.maximum(drawn, -reach), reach).astype(kind)


def setup_inputs(seed: int = 0, part: int = 0) -> dict:
    key_of = jax.random.split(jax.random.key(seed), 12)
    part_keys = jax.random.split(jax.random.fold_in(key_of[11], part), 12)
    return {
        "centres": draw_centres(jax.random.fold_in(jax.random.fold_in(key_of[11], part), 71), part),
        "log_scales": jnp.clip(-3.7 + 2.3000001 * jax.random.uniform(part_keys[1], (3, GAUSS), jnp.float32) ** block_scale(part_keys[1], (3, GAUSS), ((1, 16),), -0.2, 0.2), -3.7, -1.4),
        "rotations": draw_rotations(jax.random.fold_in(jax.random.fold_in(key_of[11], part), 71), part),
        "opacity_logits": jnp.clip(-7.0 + 0.5 * jax.random.uniform(part_keys[3], (GAUSS,), jnp.float32) ** block_scale(part_keys[3], (GAUSS,), ((0, 16),), -0.2, 0.2), -7.0, -6.5),
        "colours": normal_values(part_keys[4], (3, GAUSS), 1.0, 6.0, ((1, 16),), jnp.float32),
        "view_shift": draw_view_shift(jax.random.fold_in(jax.random.fold_in(key_of[11], part), 71), part),
        "tile_ids": draw_tile_ids(jax.random.fold_in(jax.random.fold_in(key_of[11], part), 71), part),
        "tile_counts": draw_tile_counts(jax.random.fold_in(jax.random.fold_in(key_of[11], part), 71), part),
        "tile_lists": draw_tile_lists(jax.random.fold_in(jax.random.fold_in(key_of[11], part), 71), part),
        "send_index": draw_send_index(jax.random.fold_in(jax.random.fold_in(key_of[11], part), 71), part),
        "image_cot": normal_values(part_keys[10], (3, PIXELS), 1.0, 6.0, ((1, 16),), jnp.float32),
    }


FOCAL = 512.0
SH_ZERO = 0.28209479177387814
DILATION = 0.3
BACKGROUND = 1.0
DEPTH_OFFSET = 4.0

def project(centres, log_scales, rotations, opacity_logits, colours, view_shift, half_height):
    half_width = 8.0 * TILES_X
    camera_x = centres[0][None, :] + view_shift[:, 0:1]
    camera_y = centres[1][None, :] + view_shift[:, 1:2]
    camera_z = centres[2][None, :] + view_shift[:, 2:3] + DEPTH_OFFSET
    quat_norm = jnp.sqrt(lax.optimization_barrier(jnp.sum(rotations * rotations, axis=0)))
    quat_w = rotations[0] / quat_norm
    quat_x = rotations[1] / quat_norm
    quat_y = rotations[2] / quat_norm
    quat_z = rotations[3] / quat_norm
    rotation = [[1.0 - 2.0 * (quat_y * quat_y + quat_z * quat_z), 2.0 * (quat_x * quat_y - quat_w * quat_z), 2.0 * (quat_x * quat_z + quat_w * quat_y)], [2.0 * (quat_x * quat_y + quat_w * quat_z), 1.0 - 2.0 * (quat_x * quat_x + quat_z * quat_z), 2.0 * (quat_y * quat_z - quat_w * quat_x)], [2.0 * (quat_x * quat_z - quat_w * quat_y), 2.0 * (quat_y * quat_z + quat_w * quat_x), 1.0 - 2.0 * (quat_x * quat_x + quat_y * quat_y)]]
    scales = jnp.exp(log_scales)
    stretched = [[rotation[row_idx][col_idx] * scales[col_idx] for col_idx in range(3)] for row_idx in range(3)]
    covariance = [[sum((stretched[row_idx][mid_idx] * stretched[col_idx][mid_idx] for mid_idx in range(3))) for col_idx in range(3)] for row_idx in range(3)]
    focal_z = FOCAL / camera_z
    shear_x = -FOCAL * camera_x / (camera_z * camera_z)
    shear_y = -FOCAL * camera_y / (camera_z * camera_z)
    screen_xx = focal_z * focal_z * covariance[0][0] + 2.0 * focal_z * shear_x * covariance[0][2] + shear_x * shear_x * covariance[2][2] + DILATION
    screen_yy = focal_z * focal_z * covariance[1][1] + 2.0 * focal_z * shear_y * covariance[1][2] + shear_y * shear_y * covariance[2][2] + DILATION
    screen_xy = focal_z * focal_z * covariance[0][1] + focal_z * shear_y * covariance[0][2] + shear_x * focal_z * covariance[1][2] + shear_x * shear_y * covariance[2][2]
    determinant = screen_xx * screen_yy - screen_xy * screen_xy
    mean_u = FOCAL * camera_x / camera_z + half_width
    mean_v = FOCAL * camera_y / camera_z + half_height
    opacity = jnp.broadcast_to(jax.nn.sigmoid(opacity_logits)[None, :], camera_z.shape)
    tints = [jnp.broadcast_to(0.5 + SH_ZERO * colours[channel][None, :], camera_z.shape) for channel in range(3)]
    return jnp.stack([mean_u, mean_v, screen_yy / determinant, -screen_xy / determinant, screen_xx / determinant, opacity] + tints)

def render_tile(params, tile_count, tile_id, tile_cot, tiles_view):
    local_id = tile_id % tiles_view
    anchor_x = (16 * (local_id % TILES_X)).astype(jnp.float32)
    anchor_y = (16 * (local_id // TILES_X)).astype(jnp.float32)
    within = jnp.arange(256, dtype=jnp.int32)
    pixel_x = anchor_x + (within % 16).astype(jnp.float32) + 0.5
    pixel_y = anchor_y + (within // 16).astype(jnp.float32) + 0.5
    is_live = jnp.arange(params.shape[1], dtype=jnp.int32) < tile_count

    def shade_tile(gathered):
        offset_x = pixel_x[:, None] - gathered[0][None, :]
        offset_y = pixel_y[:, None] - gathered[1][None, :]
        exponent = -0.5 * (gathered[2][None, :] * offset_x * offset_x + gathered[4][None, :] * offset_y * offset_y) - gathered[3][None, :] * offset_x * offset_y
        coverage = jnp.where(is_live[None, :], gathered[5][None, :] * jnp.exp(exponent), 0.0)
        log_keep = jnp.log1p(-coverage)
        running = jnp.cumsum(log_keep, axis=1)
        weights = coverage * jnp.exp(running - log_keep)
        shaded = jnp.einsum('pl,cl->cp', weights, gathered[6:9], precision=lax.Precision.HIGHEST)
        return shaded + BACKGROUND * jnp.exp(running[:, -1])[None, :]
    shaded, pullback = jax.vjp(shade_tile, params)
    params_grad, = pullback(tile_cot)
    return (shaded, params_grad)

def reference(centres, log_scales, rotations, opacity_logits, colours, view_shift, tile_ids, tile_counts, tile_lists, send_index, image_cot):

    def projector(centre_arg, scale_arg, rotation_arg, logit_arg, colour_arg):
        return project(centre_arg, scale_arg, rotation_arg, logit_arg, colour_arg, view_shift, 8.0 * TILE_ROWS).reshape(9, VIEWS * GAUSS)
    projected, pull_raw = jax.vjp(projector, centres, log_scales, rotations, opacity_logits, colours)
    source = jnp.arange(GROUP, dtype=jnp.int32)[:, None, None]
    columns = send_index // G_DEV * GAUSS + source * G_DEV + send_index % G_DEV
    slot_cols = jnp.transpose(columns, (1, 0, 2)).reshape(GROUP, SLOTS)
    received = jnp.moveaxis(projected[:, slot_cols], 1, 0)
    shade_fn = jax.vmap(partial(render_tile, tiles_view=TILES_VIEW))

    def per_device(inputs):
        received_dev, owned_ids, owned_counts, owned_lists, owned_cot = inputs
        gathered = jnp.moveaxis(received_dev[:, owned_lists], 1, 0)
        cot_tiles = jnp.moveaxis(owned_cot.reshape(3, TILE_DEV, 256), 0, 1)
        shaded, tile_grads = shade_fn(gathered, owned_counts, owned_ids, cot_tiles)
        flat_grads = jnp.moveaxis(tile_grads, 1, 0).reshape(9, TILE_DEV * LIST)
        slot_grads = jnp.zeros((9, SLOTS), jnp.float32).at[:, owned_lists.reshape(-1)].add(flat_grads)
        return (jnp.moveaxis(shaded, 1, 0).reshape(3, TILE_DEV * 256), slot_grads)
    images, slot_grads = lax.map(per_device, (received, tile_ids.reshape(GROUP, TILE_DEV), tile_counts.reshape(GROUP, TILE_DEV), tile_lists.reshape(GROUP, TILE_DEV, LIST), jnp.moveaxis(image_cot.reshape(3, GROUP, TILE_DEV * 256), 1, 0)))
    rendered = jnp.moveaxis(images, 1, 0).reshape(3, PIXELS)
    proj_grad = jnp.zeros((9, VIEWS * GAUSS), jnp.float32).at[:, slot_cols.reshape(-1)].add(jnp.moveaxis(slot_grads, 1, 0).reshape(9, GROUP * SLOTS))
    raw_grads = pull_raw(proj_grad)
    return (rendered, raw_grads[0], raw_grads[1], raw_grads[2], raw_grads[3], raw_grads[4])
```

```python
import math

import jax
import jax.numpy as jnp
from jax import lax
from jax.experimental import pallas as pl
from jax.experimental.pallas import tpu as pltpu
from jax.sharding import PartitionSpec as P

TILES_X = 32
FOCAL = 512.0
SH_ZERO = 0.28209479177387814
DILATION = 0.3
BACKGROUND = 1.0
DEPTH_OFFSET = 4.0
LOG2E = math.log2(math.e)
PARAMS = 9
ROW = PARAMS * 128
AXES = ("groups", "gs", "sub")
PEERS = ("gs", "sub")

BF16 = jnp.bfloat16
F32 = jnp.float32
NN = (((1,), (0,)), ((), ()))
NT = (((1,), (1,)), ((), ()))
TN = (((0,), (0,)), ((), ()))


def dot(lhs, rhs, dims=NN):
    return lax.dot_general(lhs, rhs, dims, preferred_element_type=F32)


def iota(shape, dim):
    return lax.broadcasted_iota(jnp.int32, shape, dim)


def halves(value):
    high = value.astype(BF16)
    return high, (value - high.astype(F32)).astype(BF16)


def lookup(row_of, low, high, rows):
    found = [jnp.zeros(low[0].shape, F32) for _ in low]
    for row in range(rows):
        spread = jnp.broadcast_to(row_of(row), low[0].shape)
        for pos in range(len(low)):
            taken = jnp.take_along_axis(spread, low[pos], axis=1, mode="promise_in_bounds")
            found[pos] = jnp.where(high[pos] == row, taken, found[pos])
    return found


def project(raw, shift):
    centres, log_scales, rotations, logit, colours, half_height = raw
    half_width = 8.0 * TILES_X
    camera_x = centres[0] + shift[0]
    camera_y = centres[1] + shift[1]
    camera_z = centres[2] + shift[2] + DEPTH_OFFSET
    inv_norm = 1.0 / jnp.sqrt(sum(part * part for part in rotations))
    quat_w, quat_x, quat_y, quat_z = [part * inv_norm for part in rotations]
    rotation = [
        [
            1.0 - 2.0 * (quat_y * quat_y + quat_z * quat_z),
            2.0 * (quat_x * quat_y - quat_w * quat_z),
            2.0 * (quat_x * quat_z + quat_w * quat_y),
        ],
        [
            2.0 * (quat_x * quat_y + quat_w * quat_z),
            1.0 - 2.0 * (quat_x * quat_x + quat_z * quat_z),
            2.0 * (quat_y * quat_z - quat_w * quat_x),
        ],
        [
            2.0 * (quat_x * quat_z - quat_w * quat_y),
            2.0 * (quat_y * quat_z + quat_w * quat_x),
            1.0 - 2.0 * (quat_x * quat_x + quat_y * quat_y),
        ],
    ]
    scales = [jnp.exp(part) for part in log_scales]
    stretched = [[rotation[i][j] * scales[j] for j in range(3)] for i in range(3)]

    def covariance(i, j):
        return sum(stretched[i][mid] * stretched[j][mid] for mid in range(3))

    cov_xx, cov_xy, cov_xz = covariance(0, 0), covariance(0, 1), covariance(0, 2)
    cov_yy, cov_yz, cov_zz = covariance(1, 1), covariance(1, 2), covariance(2, 2)
    inv_z = 1.0 / camera_z
    focal_z = FOCAL * inv_z
    ratio_x = camera_x * inv_z
    ratio_y = camera_y * inv_z
    shear_x = -focal_z * ratio_x
    shear_y = -focal_z * ratio_y
    screen_xx = (
        focal_z * focal_z * cov_xx
        + 2.0 * focal_z * shear_x * cov_xz
        + shear_x * shear_x * cov_zz
        + DILATION
    )
    screen_yy = (
        focal_z * focal_z * cov_yy
        + 2.0 * focal_z * shear_y * cov_yz
        + shear_y * shear_y * cov_zz
        + DILATION
    )
    screen_xy = (
        focal_z * focal_z * cov_xy
        + focal_z * shear_y * cov_xz
        + shear_x * focal_z * cov_yz
        + shear_x * shear_y * cov_zz
    )
    inv_det = 1.0 / (screen_xx * screen_yy - screen_xy * screen_xy)
    return [
        FOCAL * ratio_x + half_width,
        FOCAL * ratio_y + half_height,
        screen_yy * inv_det,
        -screen_xy * inv_det,
        screen_xx * inv_det,
        1.0 / (1.0 + jnp.exp(-logit)),
    ] + [0.5 + SH_ZERO * part for part in colours]


def load_dense(ref, scratch, first, rows):
    count = ref.shape[0]
    for row in range(rows):
        scratch[pl.ds(first + row, count, stride=rows), :] = ref[:, row * 128 : row * 128 + 128]


def view_shifts(view, shift_ref):
    chosen = []
    for axis in range(3):
        value = jnp.full(view.shape, shift_ref[0, axis], F32)
        for other in range(1, shift_ref.shape[0]):
            value = jnp.where(view == other, shift_ref[other, axis], value)
        chosen.append(value)
    return chosen


def raw_rows(scratch, logit_ref, rows, chunk):
    def part(index):
        return scratch[index * rows + chunk * 8 : index * rows + chunk * 8 + 8, :]

    return (
        [part(i) for i in range(3)],
        [part(i) for i in range(3, 6)],
        [part(i) for i in range(6, 10)],
        logit_ref[chunk * 8 : chunk * 8 + 8, :],
        [part(i) for i in range(10, 13)],
    )


def load_raw(refs, scratch, rows):
    first = 0
    for ref in refs:
        load_dense(ref, scratch, first, rows)
        first += ref.shape[0] * rows


def pre_kernel(
    half_height,
    shift_ref,
    centre_ref,
    scale_ref,
    rotation_ref,
    logit_ref,
    colour_ref,
    send_ref,
    out_ref,
    inverse_ref,
    view_ref,
    raw,
    index,
    table,
):
    rows = logit_ref.shape[0]
    owned = rows * 128
    load_raw((centre_ref, scale_ref, rotation_ref, colour_ref), raw, rows)
    per = send_ref.shape[1] // 128
    peers = send_ref.shape[0]
    for part in range(per):
        index[pl.ds(part, peers, stride=per), :] = send_ref[:, part * 128 : part * 128 + 128]
    total = jnp.zeros((2 * rows, 128), F32)
    group = 8
    for start in range(0, rows, group):
        lefts, rights = [], []
        for row in range(start, start + group):
            entry = index[row : row + 1, :]
            local = entry % owned
            slot = row * 128 + iota((1, 128), 1)
            first = (slot >> 6).astype(F32)
            second = ((slot & 63) + 64 * (entry // owned)).astype(F32)
            match = jnp.broadcast_to(local >> 7, (rows, 128)) == iota((rows, 128), 0)
            lefts.append(
                jnp.concatenate([jnp.where(match, first, 0.0), jnp.where(match, second, 0.0)], 0)
            )
            rights.append(
                jnp.where(
                    jnp.broadcast_to(local & 127, (128, 128)) == iota((128, 128), 0), 1.0, 0.0
                )
            )
        left = jnp.concatenate(lefts, 1).astype(BF16)
        right = jnp.concatenate(rights, 1).astype(BF16)
        total = total + dot(left, right, NT)
    whole = (total + 0.5).astype(jnp.int32)
    second = whole[rows:]
    inverse_ref[...] = whole[:rows] * 64 + (second & 63)
    view_ref[...] = second >> 6
    for chunk in range(rows // 8):
        parts = raw_rows(raw, logit_ref, rows, chunk)
        shift = view_shifts(view_ref[chunk * 8 : chunk * 8 + 8, :], shift_ref)
        for c, value in enumerate(project(parts + (half_height,), shift)):
            table[c * rows + chunk * 8 : c * rows + chunk * 8 + 8, :] = value
    local = [index[i * 8 : i * 8 + 8, :] % owned for i in range(rows // 8)]
    low = [value & 127 for value in local]
    high = [value >> 7 for value in local]

    def gather(c, carry):
        found = lookup(lambda row: table[pl.ds(c * rows + row, 1), :], low, high, rows)
        lane = pl.multiple_of(c * 128, 128)
        for i in range(rows // 8):
            for s in range(8):
                out_ref[i * 8 + s, :, pl.ds(lane, 128)] = found[i][s : s + 1, :]
        return carry

    lax.fori_loop(0, PARAMS, gather, 0)


def render_kernel(
    tiles_view,
    count_ref,
    id_ref,
    table_ref,
    list_ref,
    cot_ref,
    image_ref,
    grad_ref,
    gathered,
    coefs,
    moments,
    grads,
    exclusive,
    inclusive,
    partial_ref,
    beta_ref,
    slot_ref,
    slots,
):
    tiles, length = list_ref.shape
    blocks = length // 128
    rows = table_ref.shape[0]
    vregs = [(8 * i, 128 * b) for i in range(tiles // 8) for b in range(blocks)]
    stride = 16 * blocks

    def dense(ref, first, lane):
        return ref[first : first + 8, lane : lane + 128]

    def spot(first, lane, k):
        return pl.ds((first * blocks + lane // 128) * 16 + k, 8, stride=stride)

    index = [dense(list_ref, *pos) for pos in vregs]
    low = [value & 127 for value in index]
    high = [value >> 7 for value in index]

    def gather(c, carry):
        offset = pl.multiple_of(c * 128, 128)
        found = lookup(lambda row: table_ref[row, :, pl.ds(offset, 128)], low, high, rows)
        for (first, lane), value in zip(vregs, found):
            gathered[c, first : first + 8, lane : lane + 128] = value
        return carry

    lax.fori_loop(0, PARAMS, gather, 0)
    for (first, lane), value in zip(vregs, index):
        slots[pl.ds(first * blocks + lane // 128, 8, stride=blocks), :] = value

    sublane = iota((8, 128), 0)
    mid_x, mid_y, live = [], [], []
    for i in range(tiles // 8):
        x = jnp.zeros((8, 128), jnp.int32)
        y = x
        n = x
        for s in range(8):
            local = lax.rem(id_ref[i * 8 + s], tiles_view)
            x = jnp.where(sublane == s, 16 * lax.rem(local, TILES_X) + 8, x)
            y = jnp.where(sublane == s, 16 * lax.div(local, TILES_X) + 8, y)
            n = jnp.where(sublane == s, count_ref[i * 8 + s], n)
        mid_x.append(x.astype(F32))
        mid_y.append(y.astype(F32))
        live.append(n)

    def entry(first, lane):
        u, w, a, b, e, o = [gathered[c, first : first + 8, lane : lane + 128] for c in range(6)]
        return u - mid_x[first // 8], w - mid_y[first // 8], a, b, e, o

    coefs[...] = jnp.zeros(coefs.shape, F32)
    for first, lane in vregs:
        du, dw, a, b, e, o = entry(first, lane)
        is_live = iota((8, 128), 1) + lane < live[first // 8]
        slope_x = a * du + b * dw
        slope_y = e * dw + b * du
        level = -0.5 * (du * slope_x + dw * slope_y) + jnp.log(o)
        values = [-0.5 * a, -0.5 * e, -b, slope_x, slope_y, level]
        for k, value in enumerate(values):
            dead = -1000.0 if k == 5 else 0.0
            coefs[spot(first, lane, k), :] = jnp.where(is_live, value * LOG2E, dead)
        for k in range(3):
            tint = gathered[6 + k, first : first + 8, lane : lane + 128]
            coefs[spot(first, lane, 8 + k), :] = tint - BACKGROUND

    before = iota((256, 256), 0) & 127
    after = iota((256, 256), 1)
    is_sum = after >= 128
    exclusive[...] = jnp.where(is_sum | (before < after), 1.0, 0.0).astype(BF16)
    inclusive[...] = jnp.where(is_sum | (before <= after), 1.0, 0.0).astype(BF16)
    feature = iota((8, 256), 0)
    pixel = iota((8, 256), 1)
    px = (pixel & 15).astype(F32) - 7.5
    py = (pixel >> 4).astype(F32) - 7.5
    features = jnp.where(feature == 0, px * px, 0.0)
    for k, value in enumerate([py * py, px * py, px, py, jnp.ones_like(px)]):
        features = jnp.where(feature == k + 1, value, features)
    no_rows = jnp.zeros((8, 256), F32)
    moment_rows = jnp.concatenate([features, no_rows], 0).astype(BF16)
    blank = jnp.zeros((24, 128), F32)

    def render(t, carry):
        lanes = pl.ds(pl.multiple_of(t * 256, 256), 256)
        cot = jnp.concatenate([cot_ref[:, lanes], jnp.zeros((5, 256), F32)], 0)
        cot_high = cot.astype(BF16).astype(F32)
        cot_low = cot - cot_high
        left = jnp.concatenate(
            [features, features, features, cot_high, cot_high, cot_low], 0
        ).astype(BF16)
        left = left.T
        cot_rows = jnp.concatenate([cot_high, cot_low], 0).astype(BF16)
        run = None
        run_grad = None
        image = jnp.zeros((16, 256), F32)
        for b in range(blocks):
            base = pl.multiple_of((t * blocks + b) * 16, 16)
            coef = coefs[pl.ds(base, 8), :]
            tint = coefs[pl.ds(base + 8, 8), :]
            coef_high = coef.astype(BF16).astype(F32)
            rest = coef - coef_high
            coef_mid = rest.astype(BF16).astype(F32)
            coef_low = rest - coef_mid
            tint_high = tint.astype(BF16).astype(F32)
            tint_low = tint - tint_high
            shape_rows = jnp.concatenate([coef_high, coef_mid, coef_low], 0)
            tint_rows = jnp.concatenate([tint_high, tint_low, tint_high], 0)
            right = jnp.concatenate(
                [
                    jnp.concatenate([shape_rows, blank], 1),
                    jnp.concatenate([blank, tint_rows], 1),
                ],
                0,
            ).astype(BF16)
            both = dot(left, right)
            alpha = jnp.exp2(both[:, :128])
            shade = both[:, 128:]
            keep = alpha * (-LOG2E + alpha * (-LOG2E / 2.0 + alpha * (-LOG2E / 3.0)))
            sums = dot(jnp.concatenate(halves(keep), 1), exclusive[...])
            logs = sums[:, :128]
            if b == 0:
                run = sums[:, 128:]
            else:
                logs = logs + run
                run = run + sums[:, 128:]
            weight = alpha * jnp.exp2(logs)
            share = weight * shade
            weights = jnp.concatenate(halves(weight), 1)
            tints = jnp.concatenate([tint_high, tint_low], 0).astype(BF16)
            image = image + dot(jnp.concatenate([tints, tints], 1), weights, NT)
            tint_grad = dot(cot_rows, weights)
            tint_grad = tint_grad[:8] + tint_grad[8:]
            moments[pl.ds(base + 8, 8), :] = tint_grad[:, :128] + tint_grad[:, 128:]
            sums = dot(jnp.concatenate(halves(share), 1), inclusive[...])
            prefix = sums[:, :128]
            if b == 0:
                run_grad = sums[:, 128:]
            else:
                prefix = prefix + run_grad
                run_grad = run_grad + sums[:, 128:]
            beta = alpha * (1.0 + alpha * (1.0 + alpha))
            beta_ref[:, b * 128 : b * 128 + 128] = beta
            partial_ref[:, b * 128 : b * 128 + 128] = share + prefix * beta
        image_ref[:, lanes] = BACKGROUND + (image[:8] + image[8:])[:3]
        for b in range(blocks):
            base = pl.multiple_of((t * blocks + b) * 16, 16)
            here = slice(b * 128, b * 128 + 128)
            slope = partial_ref[:, here] - run_grad * beta_ref[:, here]
            summed = dot(moment_rows, jnp.concatenate(halves(slope), 1))
            moments[pl.ds(base, 8), :] = summed[:8, :128] + summed[:8, 128:]
        return carry

    lax.fori_loop(0, tiles, render, 0)

    for first, lane in vregs:
        du, dw, a, b, e, o = entry(first, lane)
        m_xx, m_yy, m_xy, m_x, m_y, m_one = [moments[spot(first, lane, k), :] for k in range(6)]
        d_x = m_x - du * m_one
        d_y = m_y - dw * m_one
        values = [
            a * d_x + b * d_y,
            e * d_y + b * d_x,
            -0.5 * (m_xx - du * (m_x + d_x)),
            -(m_xy - dw * m_x - du * d_y),
            -0.5 * (m_yy - dw * (m_y + d_y)),
            m_one / o,
        ] + [moments[spot(first, lane, 8 + k), :] for k in range(3)]
        for k, value in enumerate(values):
            grads[spot(first, lane, k), :] = value

    slot_ref[...] = jnp.zeros(slot_ref.shape, F32)

    def scatter(t, carry):
        lefts, rights = [], []
        for b in range(blocks):
            base = pl.multiple_of((t * blocks + b) * 16, 16)
            entry_slot = slots[pl.ds(t * blocks + b, 1), :]
            match = jnp.broadcast_to(entry_slot >> 7, (rows, 128)) == iota((rows, 128), 0)
            where = jnp.broadcast_to(entry_slot & 127, (128, 128)) == iota((128, 128), 0)
            right = jnp.where(where, 1.0, 0.0).astype(BF16)
            high_rows, low_rows = [], []
            for c in range(PARAMS):
                value = grads[pl.ds(base + c, 1), :]
                value_high = value.astype(BF16).astype(F32)
                high_rows.append(jnp.where(match, value_high, 0.0))
                low_rows.append(jnp.where(match, value - value_high, 0.0))
            lefts.append(jnp.concatenate(high_rows, 0).astype(BF16))
            lefts.append(jnp.concatenate(low_rows, 0).astype(BF16))
            rights += [right, right]
        slot_ref[...] += dot(jnp.concatenate(lefts, 1), jnp.concatenate(rights, 1), NT)
        return carry

    lax.fori_loop(0, tiles, scatter, 0)

    for c in range(PARAMS):
        for row in range(rows):
            grad_ref[row, :, c * 128 : c * 128 + 128] = slot_ref[
                c * rows + row : c * rows + row + 1, :
            ]


def post_kernel(
    half_height,
    shift_ref,
    centre_ref,
    scale_ref,
    rotation_ref,
    logit_ref,
    colour_ref,
    inverse_ref,
    view_ref,
    table_ref,
    centre_out,
    scale_out,
    rotation_out,
    logit_out,
    colour_out,
    raw,
    grads,
    dense_out,
):
    rows = logit_ref.shape[0]
    load_raw((centre_ref, scale_ref, rotation_ref, colour_ref), raw, rows)
    index = [inverse_ref[i * 8 : i * 8 + 8, :] for i in range(rows // 8)]
    low = [value & 127 for value in index]
    high = [value >> 7 for value in index]

    def gather(c, carry):
        offset = pl.multiple_of(c * 128, 128)
        found = lookup(lambda row: table_ref[row, :, pl.ds(offset, 128)], low, high, rows)
        for i in range(rows // 8):
            grads[c, i * 8 : i * 8 + 8, :] = found[i]
        return carry

    lax.fori_loop(0, PARAMS, gather, 0)
    for chunk in range(rows // 8):
        parts = raw_rows(raw, logit_ref, rows, chunk)
        shift = view_shifts(view_ref[chunk * 8 : chunk * 8 + 8, :], shift_ref)
        _, pull = jax.vjp(lambda *args: project(args + (half_height,), shift), *parts)
        back = pull([grads[c, chunk * 8 : chunk * 8 + 8, :] for c in range(PARAMS)])
        flat = back[0] + back[1] + back[2] + back[4]
        for k, value in enumerate(flat):
            dense_out[k * rows + chunk * 8 : k * rows + chunk * 8 + 8, :] = value
        logit_out[chunk * 8 : chunk * 8 + 8, :] = back[3]
    first = 0
    for ref in (centre_out, scale_out, rotation_out, colour_out):
        count = ref.shape[0]
        for row in range(rows):
            ref[:, row * 128 : row * 128 + 128] = dense_out[
                pl.ds(first + row, count, stride=rows), :
            ]
        first += count * rows


def exchange(table, peers, capacity):
    if capacity % 128 == 0:
        return lax.all_to_all(table, PEERS, split_axis=0, concat_axis=0, tiled=True)
    rows = table.shape[0]
    per = 128 // capacity
    chunks = table.reshape(rows, PARAMS, per, capacity).transpose(0, 2, 1, 3)
    chunks = chunks.reshape(peers, 1, PARAMS * capacity)
    moved = lax.all_to_all(chunks, PEERS, split_axis=0, concat_axis=0, tiled=True)
    moved = moved.reshape(rows, per, PARAMS, capacity).transpose(0, 2, 1, 3)
    return moved.reshape(rows, 1, ROW)


VMEM = pl.BlockSpec(memory_space=pltpu.VMEM)
SMEM = pl.BlockSpec(memory_space=pltpu.SMEM)
LIMIT = pltpu.CompilerParams(vmem_limit_bytes=40 * 1024 * 1024)


def shards(
    centres,
    log_scales,
    rotations,
    opacity_logits,
    colours,
    view_shift,
    tile_ids,
    tile_counts,
    tile_lists,
    send_index,
    image_cot,
):
    owned = centres.shape[1]
    rows = owned // 128
    peers, capacity = send_index.shape[1:]
    tiles, length = tile_lists.shape
    views = view_shift.shape[0]
    tiles_view = tiles * peers // views
    half_height = 8.0 * (tiles_view // TILES_X)
    assert peers * capacity == owned
    logits = opacity_logits.reshape(rows, 128)
    targets = send_index[0] if capacity % 128 == 0 else send_index.reshape(rows, 128)
    outgoing, inverse, view = pl.pallas_call(
        lambda *refs: pre_kernel(half_height, *refs),
        out_shape=(
            jax.ShapeDtypeStruct((rows, 1, ROW), F32),
            jax.ShapeDtypeStruct((rows, 128), jnp.int32),
            jax.ShapeDtypeStruct((rows, 128), jnp.int32),
        ),
        in_specs=[SMEM] + [VMEM] * 6,
        out_specs=(VMEM,) * 3,
        scratch_shapes=[
            pltpu.VMEM((13 * rows, 128), F32),
            pltpu.VMEM((rows, 128), jnp.int32),
            pltpu.VMEM((PARAMS * rows, 128), F32),
        ],
        compiler_params=LIMIT,
        name="project_and_pack",
    )(view_shift, centres, log_scales, rotations, logits, colours, targets)
    received = exchange(outgoing, peers, capacity)
    rendered, slot_grads = pl.pallas_call(
        lambda *refs: render_kernel(tiles_view, *refs),
        out_shape=(
            jax.ShapeDtypeStruct((3, tiles * 256), F32),
            jax.ShapeDtypeStruct((rows, 1, ROW), F32),
        ),
        in_specs=[SMEM] * 2 + [VMEM] * 3,
        out_specs=(VMEM,) * 2,
        scratch_shapes=[
            pltpu.VMEM((PARAMS, tiles, length), F32),
            pltpu.VMEM((tiles * length // 8, 128), F32),
            pltpu.VMEM((tiles * length // 8, 128), F32),
            pltpu.VMEM((tiles * length // 8, 128), F32),
            pltpu.VMEM((256, 256), BF16),
            pltpu.VMEM((256, 256), BF16),
            pltpu.VMEM((256, length), F32),
            pltpu.VMEM((256, length), F32),
            pltpu.VMEM((PARAMS * rows, 128), F32),
            pltpu.VMEM((tiles * length // 128, 128), jnp.int32),
        ],
        compiler_params=LIMIT,
        name="render",
    )(tile_counts, tile_ids, received, tile_lists, image_cot)
    returned = exchange(slot_grads, peers, capacity)
    shapes = [jax.ShapeDtypeStruct((n, owned), F32) for n in (3, 3, 4, 3)]
    shapes.insert(3, jax.ShapeDtypeStruct((rows, 128), F32))
    grads = pl.pallas_call(
        lambda *refs: post_kernel(half_height, *refs),
        out_shape=tuple(shapes),
        in_specs=[SMEM] + [VMEM] * 8,
        out_specs=(VMEM,) * 5,
        scratch_shapes=[
            pltpu.VMEM((13 * rows, 128), F32),
            pltpu.VMEM((PARAMS, rows, 128), F32),
            pltpu.VMEM((13 * rows, 128), F32),
        ],
        compiler_params=LIMIT,
        name="unpack_and_project_back",
    )(
        view_shift, centres, log_scales, rotations, logits, colours, inverse, view, returned
    )
    return (rendered, grads[0], grads[1], grads[2], grads[3].reshape(owned), grads[4])


def solution(mesh):
    wide = P(None, AXES)
    flat = P(AXES)
    return jax.shard_map(
        shards,
        mesh=mesh,
        in_specs=(
            wide,
            wide,
            wide,
            flat,
            wide,
            P("groups", None),
            flat,
            flat,
            P(AXES, None),
            P(AXES, None, None),
            wide,
        ),
        out_specs=(wide, wide, wide, wide, flat, wide),
        check_vma=False,
    )
```

```python
import math

import jax
import jax.numpy as jnp
from jax import lax
from jax.experimental import pallas as pl
from jax.experimental.pallas import tpu as pltpu
from jax.sharding import PartitionSpec as P

TILES_X = 32
FOCAL = 512.0
SH_ZERO = 0.28209479177387814
DILATION = 0.3
BACKGROUND = 1.0
DEPTH_OFFSET = 4.0
LOG2E = math.log2(math.e)
PARAMS = 9
ROW = PARAMS * 128
AXES = ("groups", "gs", "sub")
PEERS = ("gs", "sub")

BF16 = jnp.bfloat16
F32 = jnp.float32
NN = (((1,), (0,)), ((), ()))
NT = (((1,), (1,)), ((), ()))
TN = (((0,), (0,)), ((), ()))


def dot(lhs, rhs, dims=NN):
    return lax.dot_general(lhs, rhs, dims, preferred_element_type=F32)


def iota(shape, dim):
    return lax.broadcasted_iota(jnp.int32, shape, dim)


def halves(value):
    high = value.astype(BF16)
    return high, (value - high.astype(F32)).astype(BF16)


def lookup(row_of, index, rows):
    low = index & 127
    high = index >> 7
    found = jnp.zeros(index.shape, F32)
    for row in range(rows):
        spread = jnp.broadcast_to(row_of(row), index.shape)
        taken = jnp.take_along_axis(spread, low, axis=1, mode="promise_in_bounds")
        found = jnp.where(high == row, taken, found)
    return found


def project(raw, shift):
    centres, log_scales, rotations, logit, colours, half_height = raw
    half_width = 8.0 * TILES_X
    camera_x = centres[0] + shift[0]
    camera_y = centres[1] + shift[1]
    camera_z = centres[2] + shift[2] + DEPTH_OFFSET
    inv_norm = 1.0 / jnp.sqrt(sum(part * part for part in rotations))
    quat_w, quat_x, quat_y, quat_z = [part * inv_norm for part in rotations]
    rotation = [
        [
            1.0 - 2.0 * (quat_y * quat_y + quat_z * quat_z),
            2.0 * (quat_x * quat_y - quat_w * quat_z),
            2.0 * (quat_x * quat_z + quat_w * quat_y),
        ],
        [
            2.0 * (quat_x * quat_y + quat_w * quat_z),
            1.0 - 2.0 * (quat_x * quat_x + quat_z * quat_z),
            2.0 * (quat_y * quat_z - quat_w * quat_x),
        ],
        [
            2.0 * (quat_x * quat_z - quat_w * quat_y),
            2.0 * (quat_y * quat_z + quat_w * quat_x),
            1.0 - 2.0 * (quat_x * quat_x + quat_y * quat_y),
        ],
    ]
    scales = [jnp.exp(part) for part in log_scales]
    stretched = [[rotation[i][j] * scales[j] for j in range(3)] for i in range(3)]

    def covariance(i, j):
        return sum(stretched[i][mid] * stretched[j][mid] for mid in range(3))

    cov_xx, cov_xy, cov_xz = covariance(0, 0), covariance(0, 1), covariance(0, 2)
    cov_yy, cov_yz, cov_zz = covariance(1, 1), covariance(1, 2), covariance(2, 2)
    inv_z = 1.0 / camera_z
    focal_z = FOCAL * inv_z
    ratio_x = camera_x * inv_z
    ratio_y = camera_y * inv_z
    shear_x = -focal_z * ratio_x
    shear_y = -focal_z * ratio_y
    screen_xx = (
        focal_z * focal_z * cov_xx
        + 2.0 * focal_z * shear_x * cov_xz
        + shear_x * shear_x * cov_zz
        + DILATION
    )
    screen_yy = (
        focal_z * focal_z * cov_yy
        + 2.0 * focal_z * shear_y * cov_yz
        + shear_y * shear_y * cov_zz
        + DILATION
    )
    screen_xy = (
        focal_z * focal_z * cov_xy
        + focal_z * shear_y * cov_xz
        + shear_x * focal_z * cov_yz
        + shear_x * shear_y * cov_zz
    )
    inv_det = 1.0 / (screen_xx * screen_yy - screen_xy * screen_xy)
    return [
        FOCAL * ratio_x + half_width,
        FOCAL * ratio_y + half_height,
        screen_yy * inv_det,
        -screen_xy * inv_det,
        screen_xx * inv_det,
        1.0 / (1.0 + jnp.exp(-logit)),
    ] + [0.5 + SH_ZERO * part for part in colours]


def load_dense(ref, dense, first, rows):
    count = ref.shape[0]
    for row in range(rows):
        dense[pl.ds(first + row, count, stride=rows), :] = ref[:, row * 128 : row * 128 + 128]


def view_shifts(view, shift_ref):
    chosen = []
    for axis in range(3):
        value = jnp.full(view.shape, shift_ref[0, axis], F32)
        for other in range(1, shift_ref.shape[0]):
            value = jnp.where(view == other, shift_ref[other, axis], value)
        chosen.append(value)
    return chosen


def raw_rows(raw, rows, chunk):
    parts = [raw[i * rows + chunk * 8 : i * rows + chunk * 8 + 8, :] for i in range(14)]
    return parts[:3], parts[3:6], parts[6:10], parts[13], parts[10:13]


def pre_kernel(
    half_height,
    shift_ref,
    centre_hbm,
    scale_hbm,
    rotation_hbm,
    logit_hbm,
    colour_hbm,
    send_hbm,
    list_hbm,
    cot_hbm,
    out_ref,
    inverse_ref,
    view_ref,
    raw,
    slots,
    cot_ref,
    centre_ref,
    scale_ref,
    rotation_ref,
    colour_ref,
    send_ref,
    list_ref,
    index,
    table,
    arrived,
):
    rows = table.shape[0] // PARAMS
    owned = rows * 128
    logit_ref = raw.at[pl.ds(13 * rows, rows), :]
    pairs = [
        (send_hbm, send_ref),
        (centre_hbm, centre_ref),
        (scale_hbm, scale_ref),
        (rotation_hbm, rotation_ref),
        (colour_hbm, colour_ref),
        (logit_hbm, logit_ref),
        (list_hbm, list_ref),
        (cot_hbm, cot_ref),
    ]
    copies = [
        pltpu.make_async_copy(source, target, arrived.at[i])
        for i, (source, target) in enumerate(pairs)
    ]
    for copy in copies:
        copy.start()
    copies[0].wait()
    per = send_ref.shape[1] // 128
    peers = send_ref.shape[0]
    for part in range(per):
        index[pl.ds(part, peers, stride=per), :] = send_ref[:, part * 128 : part * 128 + 128]
    total = jnp.zeros((2 * rows, 128), F32)
    group = 8
    for start in range(0, rows, group):
        lefts, rights = [], []
        for row in range(start, start + group):
            entry = index[row : row + 1, :]
            local = entry % owned
            slot = row * 128 + iota((1, 128), 1)
            first = (slot >> 6).astype(F32)
            second = ((slot & 63) + 64 * (entry // owned)).astype(F32)
            match = jnp.broadcast_to(local >> 7, (rows, 128)) == iota((rows, 128), 0)
            lefts.append(
                jnp.concatenate([jnp.where(match, first, 0.0), jnp.where(match, second, 0.0)], 0)
            )
            rights.append(
                jnp.where(
                    jnp.broadcast_to(local & 127, (128, 128)) == iota((128, 128), 0), 1.0, 0.0
                )
            )
        left = jnp.concatenate(lefts, 1).astype(BF16)
        right = jnp.concatenate(rights, 1).astype(BF16)
        total = total + dot(left, right, NT)
    whole = (total + 0.5).astype(jnp.int32)
    second = whole[rows:]
    inverse_ref[...] = whole[:rows] * 64 + (second & 63)
    view_ref[...] = second >> 6
    for copy in copies[1:6]:
        copy.wait()
    first = 0
    for ref in (centre_ref, scale_ref, rotation_ref, colour_ref):
        load_dense(ref, raw, first, rows)
        first += ref.shape[0] * rows
    for chunk in range(rows // 8):
        parts = raw_rows(raw, rows, chunk)
        shift = view_shifts(view_ref[chunk * 8 : chunk * 8 + 8, :], shift_ref)
        for c, value in enumerate(project(parts + (half_height,), shift)):
            table[c * rows + chunk * 8 : c * rows + chunk * 8 + 8, :] = value
    local = [index[i * 8 : i * 8 + 8, :] % owned for i in range(rows // 8)]

    def gather(c, carry):
        lane = pl.multiple_of(c * 128, 128)
        for i in range(rows // 8):
            found = lookup(lambda row: table[pl.ds(c * rows + row, 1), :], local[i], rows)
            for s in range(8):
                out_ref[i * 8 + s, :, pl.ds(lane, 128)] = found[s : s + 1, :]
        return carry

    lax.fori_loop(0, PARAMS, gather, 0)
    copies[6].wait()
    tiles, length = list_ref.shape
    blocks = length // 128
    lane = iota((8, 128), 1)
    for b in range(blocks):
        entry = run_entry(lane, b, length)
        for i in range(tiles // 8):
            moved = jnp.zeros((8, 128), jnp.int32)
            for source in range(blocks):
                value = list_ref[i * 8 : i * 8 + 8, source * 128 : source * 128 + 128]
                taken = jnp.take_along_axis(
                    value, entry & 127, axis=1, mode="promise_in_bounds"
                )
                moved = jnp.where(entry >> 7 == source, taken, moved)
            slots[pl.ds(i * 8 * blocks + b, 8, stride=blocks), :] = moved
    copies[7].wait()


def run_entry(lane, block, length):
    return (lane & 7) * (length // 8) + block * 16 + (lane >> 3)


def render_kernel(
    tiles_view,
    length,
    count_ref,
    id_ref,
    table_ref,
    slots,
    cot_ref,
    image_ref,
    grad_ref,
    gathered,
    coefs,
    moments,
    grads,
    slot_ref,
    *buffers,
):
    blocks = length // 128
    tiles = slots.shape[0] // blocks
    rows = table_ref.shape[0]
    places = [(8 * i, b) for i in range(tiles // 8) for b in range(blocks)]
    stride = 16 * blocks

    def spot(first, b, k):
        return pl.ds((first * blocks + b) * 16 + k, 8, stride=stride)

    index = [slots[pl.ds(first * blocks + b, 8, stride=blocks), :] for first, b in places]

    def gather(c, carry):
        offset = pl.multiple_of(c * 128, 128)
        for pos, value in enumerate(index):
            gathered[c, pos] = lookup(
                lambda row: table_ref[row, :, pl.ds(offset, 128)], value, rows
            )
        return carry

    lax.fori_loop(0, PARAMS, gather, 0)

    sublane = iota((8, 128), 0)
    lane = iota((8, 128), 1)
    mid_x, mid_y, live = [], [], []
    for i in range(tiles // 8):
        x = jnp.zeros((8, 128), jnp.int32)
        y = x
        n = x
        for s in range(8):
            local = lax.rem(id_ref[i * 8 + s], tiles_view)
            x = jnp.where(sublane == s, 16 * lax.rem(local, TILES_X) + 8, x)
            y = jnp.where(sublane == s, 16 * lax.div(local, TILES_X) + 8, y)
            n = jnp.where(sublane == s, count_ref[i * 8 + s], n)
        mid_x.append(x.astype(F32))
        mid_y.append(y.astype(F32))
        live.append(n)

    def entry(pos):
        u, w, a, b, e, o = [gathered[c, pos] for c in range(6)]
        first = places[pos][0]
        return u - mid_x[first // 8], w - mid_y[first // 8], a, b, e, o

    coefs[...] = jnp.zeros(coefs.shape, F32)
    for pos, (first, block) in enumerate(places):
        du, dw, a, b, e, o = entry(pos)
        is_live = run_entry(lane, block, length) < live[first // 8]
        slope_x = a * du + b * dw
        slope_y = e * dw + b * du
        level = -0.5 * (du * slope_x + dw * slope_y) + jnp.log(o)
        values = [-0.5 * a, -0.5 * e, -b, slope_x, slope_y, level]
        for k, value in enumerate(values):
            dead = -1000.0 if k == 5 else 0.0
            coefs[spot(first, block, k), :] = jnp.where(is_live, value * LOG2E, dead)
        for k in range(3):
            coefs[spot(first, block, 8 + k), :] = gathered[6 + k, pos] - BACKGROUND

    feature = iota((8, 256), 0)
    pixel = iota((8, 256), 1)
    px = (pixel & 15).astype(F32) - 7.5
    py = (pixel >> 4).astype(F32) - 7.5
    features = jnp.where(feature == 0, px * px, 0.0)
    for k, value in enumerate([py * py, px * py, px, py, jnp.ones_like(px)]):
        features = jnp.where(feature == k + 1, value, features)
    blank = jnp.zeros((24, 256), F32)
    moment_rows = jnp.concatenate([features, jnp.zeros((8, 256), F32)], 0)
    moment_rows = jnp.concatenate([moment_rows, moment_rows], 1).astype(BF16)
    run_row = iota((8, 256), 0)

    def earlier_product(value):
        for step in (1, 2, 4):
            moved = pltpu.roll(value, step, 0)
            value = value * jnp.where(run_row >= step, moved, 1.0)
        return jnp.where(run_row >= 1, pltpu.roll(value, 1, 0), 1.0)

    def later_sum(value):
        for step in (1, 2, 4):
            moved = pltpu.roll(value, 8 - step, 0)
            value = value + jnp.where(run_row < 8 - step, moved, 0.0)
        return jnp.where(run_row < 7, pltpu.roll(value, 7, 0), 0.0)

    def render(t, alpha_ref, share_ref, weights, slopes):
        lanes = pl.ds(pl.multiple_of(t * 256, 256), 256)
        cot = jnp.concatenate([cot_ref[:, lanes], jnp.zeros((5, 256), F32)], 0)
        cot_high = cot.astype(BF16).astype(F32)
        cot_low = cot - cot_high
        right = jnp.concatenate(
            [
                jnp.concatenate([features, features, features, blank], 0),
                jnp.concatenate([blank, cot_high, cot_high, cot_low], 0),
            ],
            1,
        ).astype(BF16)
        cot_rows = jnp.concatenate([cot_high, cot_low], 0)
        cot_rows = jnp.concatenate([cot_rows, cot_rows], 1).astype(BF16)
        lefts, tints = [], []
        for b in range(blocks):
            base = pl.multiple_of((t * blocks + b) * 16, 16)
            coef = coefs[pl.ds(base, 8), :]
            tint = coefs[pl.ds(base + 8, 8), :]
            coef_high = coef.astype(BF16).astype(F32)
            rest = coef - coef_high
            coef_mid = rest.astype(BF16).astype(F32)
            tint_high = tint.astype(BF16).astype(F32)
            tint_low = tint - tint_high
            lefts.append(
                jnp.concatenate(
                    [coef_high, coef_mid, rest - coef_mid, tint_high, tint_low, tint_high], 0
                )
            )
            tints.append(jnp.concatenate([tint_high, tint_low], 0))
        left = jnp.concatenate(lefts, 1).astype(BF16)
        tint_rows = jnp.concatenate(tints, 1).astype(BF16)
        both = dot(left, right, TN)
        steps = length // 16
        left_over = jnp.ones((8, 256), F32)
        for step in range(steps):
            here = slice(step * 16, step * 16 + 16)
            alpha = jnp.exp2(both[here, :256])
            alpha_ref[here, :] = alpha
            keep = 1.0 - alpha
            left_over = left_over * (keep[:8] * keep[8:])
        through = earlier_product(left_over)
        total = jnp.zeros((8, 256), F32)
        for step in range(steps):
            here = slice(step * 16, step * 16 + 16)
            alpha = alpha_ref[here, :]
            first = alpha[:8] * through
            through = through - first
            second = alpha[8:] * through
            through = through - second
            weight = jnp.concatenate([first, second], 0)
            high, low = halves(weight)
            weights[here, :256] = high
            weights[here, 256:] = low
            share = weight * both[here, 256:]
            share_ref[here, :] = share
            total = total + (share[:8] + share[8:])
        image = dot(tint_rows, weights[:, :256])
        image_ref[:, lanes] = BACKGROUND + (image[:8] + image[8:])[:3]
        tint_grad = dot(cot_rows, weights[...], NT)
        tint_grad = tint_grad[:8] + tint_grad[8:]
        behind = later_sum(total)
        for step in reversed(range(steps)):
            here = slice(step * 16, step * 16 + 16)
            alpha = alpha_ref[here, :]
            share = share_ref[here, :]
            beta = alpha * (1.0 + alpha * (1.0 + alpha))
            second = share[8:] - beta[8:] * behind
            behind = behind + share[8:]
            first = share[:8] - beta[:8] * behind
            behind = behind + share[:8]
            high, low = halves(jnp.concatenate([first, second], 0))
            slopes[here, :256] = high
            slopes[here, 256:] = low
        summed = dot(moment_rows, slopes[...], NT)
        for b in range(blocks):
            base = pl.multiple_of((t * blocks + b) * 16, 16)
            here = slice(b * 128, b * 128 + 128)
            moments[pl.ds(base, 8), :] = summed[:8, here]
            moments[pl.ds(base + 8, 8), :] = tint_grad[:, here]

    def pair(t, carry):
        render(2 * t, *buffers[:4])
        render(2 * t + 1, *buffers[4:])
        return carry

    lax.fori_loop(0, tiles // 2, pair, 0)

    for pos, (first, block) in enumerate(places):
        du, dw, a, b, e, o = entry(pos)
        m_xx, m_yy, m_xy, m_x, m_y, m_one = [moments[spot(first, block, k), :] for k in range(6)]
        d_x = m_x - du * m_one
        d_y = m_y - dw * m_one
        values = [
            a * d_x + b * d_y,
            e * d_y + b * d_x,
            -0.5 * (m_xx - du * (m_x + d_x)),
            -(m_xy - dw * m_x - du * d_y),
            -0.5 * (m_yy - dw * (m_y + d_y)),
            m_one / o,
        ] + [moments[spot(first, block, 8 + k), :] for k in range(3)]
        for k, value in enumerate(values):
            grads[spot(first, block, k), :] = value

    slot_ref[...] = jnp.zeros(slot_ref.shape, F32)

    def scatter(t, carry):
        lefts, rights = [], []
        for b in range(blocks):
            base = pl.multiple_of((t * blocks + b) * 16, 16)
            entry_slot = slots[pl.ds(t * blocks + b, 1), :]
            match = jnp.broadcast_to(entry_slot >> 7, (rows, 128)) == iota((rows, 128), 0)
            where = jnp.broadcast_to(entry_slot & 127, (128, 128)) == iota((128, 128), 0)
            right = jnp.where(where, 1.0, 0.0).astype(BF16)
            high_rows, low_rows = [], []
            for c in range(PARAMS):
                value = grads[pl.ds(base + c, 1), :]
                value_high = value.astype(BF16).astype(F32)
                high_rows.append(jnp.where(match, value_high, 0.0))
                low_rows.append(jnp.where(match, value - value_high, 0.0))
            lefts.append(jnp.concatenate(high_rows, 0).astype(BF16))
            lefts.append(jnp.concatenate(low_rows, 0).astype(BF16))
            rights += [right, right]
        slot_ref[...] += dot(jnp.concatenate(lefts, 1), jnp.concatenate(rights, 1), NT)
        return carry

    lax.fori_loop(0, tiles, scatter, 0)

    for c in range(PARAMS):
        for row in range(rows):
            grad_ref[row, :, c * 128 : c * 128 + 128] = slot_ref[
                c * rows + row : c * rows + row + 1, :
            ]


def post_kernel(
    half_height,
    shift_ref,
    raw,
    inverse_ref,
    view_ref,
    table_ref,
    centre_out,
    scale_out,
    rotation_out,
    logit_out,
    colour_out,
    grads,
    dense_out,
):
    rows = logit_out.shape[0]
    index = [inverse_ref[i * 8 : i * 8 + 8, :] for i in range(rows // 8)]

    def gather(c, carry):
        offset = pl.multiple_of(c * 128, 128)
        for i in range(rows // 8):
            grads[c, i * 8 : i * 8 + 8, :] = lookup(
                lambda row: table_ref[row, :, pl.ds(offset, 128)], index[i], rows
            )
        return carry

    lax.fori_loop(0, PARAMS, gather, 0)
    for chunk in range(rows // 8):
        parts = raw_rows(raw, rows, chunk)
        shift = view_shifts(view_ref[chunk * 8 : chunk * 8 + 8, :], shift_ref)
        _, pull = jax.vjp(lambda *args: project(args + (half_height,), shift), *parts)
        back = pull([grads[c, chunk * 8 : chunk * 8 + 8, :] for c in range(PARAMS)])
        flat = back[0] + back[1] + back[2] + back[4]
        for k, value in enumerate(flat):
            dense_out[k * rows + chunk * 8 : k * rows + chunk * 8 + 8, :] = value
        logit_out[chunk * 8 : chunk * 8 + 8, :] = back[3]
    first = 0
    for ref in (centre_out, scale_out, rotation_out, colour_out):
        count = ref.shape[0]
        for row in range(rows):
            ref[:, row * 128 : row * 128 + 128] = dense_out[
                pl.ds(first + row, count, stride=rows), :
            ]
        first += count * rows


def exchange(table, peers, capacity):
    if capacity % 128 == 0:
        return lax.all_to_all(table, PEERS, split_axis=0, concat_axis=0, tiled=True)
    rows = table.shape[0]
    per = 128 // capacity
    chunks = table.reshape(rows, PARAMS, per, capacity).transpose(0, 2, 1, 3)
    chunks = chunks.reshape(peers, 1, PARAMS * capacity)
    moved = lax.all_to_all(chunks, PEERS, split_axis=0, concat_axis=0, tiled=True)
    moved = moved.reshape(rows, per, PARAMS, capacity).transpose(0, 2, 1, 3)
    return moved.reshape(rows, 1, ROW)


VMEM = pl.BlockSpec(memory_space=pltpu.VMEM)
SMEM = pl.BlockSpec(memory_space=pltpu.SMEM)
HBM = pl.BlockSpec(memory_space=pltpu.HBM)
LIMIT = pltpu.CompilerParams(vmem_limit_bytes=40 * 1024 * 1024)


def shards(
    centres,
    log_scales,
    rotations,
    opacity_logits,
    colours,
    view_shift,
    tile_ids,
    tile_counts,
    tile_lists,
    send_index,
    image_cot,
):
    owned = centres.shape[1]
    rows = owned // 128
    peers, capacity = send_index.shape[1:]
    tiles, length = tile_lists.shape
    views = view_shift.shape[0]
    tiles_view = tiles * peers // views
    half_height = 8.0 * (tiles_view // TILES_X)
    assert peers * capacity == owned
    logits = opacity_logits.reshape(rows, 128)
    targets = send_index[0] if capacity % 128 == 0 else send_index.reshape(rows, 128)
    table_shape = jax.ShapeDtypeStruct((rows, 1, ROW), F32)
    whole = jax.ShapeDtypeStruct((rows, 128), jnp.int32)
    outgoing, inverse, view, raw, slots, cot = pl.pallas_call(
        lambda *refs: pre_kernel(half_height, *refs),
        out_shape=(
            table_shape,
            whole,
            whole,
            jax.ShapeDtypeStruct((14 * rows, 128), F32),
            jax.ShapeDtypeStruct((tiles * length // 128, 128), jnp.int32),
            jax.ShapeDtypeStruct(image_cot.shape, F32),
        ),
        in_specs=[SMEM] + [HBM] * 8,
        out_specs=(VMEM,) * 6,
        scratch_shapes=[pltpu.VMEM((n, owned), F32) for n in (3, 3, 4, 3)]
        + [
            pltpu.VMEM(targets.shape, jnp.int32),
            pltpu.VMEM(tile_lists.shape, jnp.int32),
            pltpu.VMEM((rows, 128), jnp.int32),
            pltpu.VMEM((PARAMS * rows, 128), F32),
            pltpu.SemaphoreType.DMA((8,)),
        ],
        compiler_params=LIMIT,
        name="project_and_pack",
    )(
        view_shift,
        centres,
        log_scales,
        rotations,
        logits,
        colours,
        targets,
        tile_lists,
        image_cot,
    )
    received = exchange(outgoing, peers, capacity)
    rendered, slot_grads = pl.pallas_call(
        lambda *refs: render_kernel(tiles_view, length, *refs),
        out_shape=(jax.ShapeDtypeStruct((3, tiles * 256), F32), table_shape),
        in_specs=[SMEM] * 2 + [VMEM] * 3,
        out_specs=(VMEM,) * 2,
        scratch_shapes=[pltpu.VMEM((PARAMS, tiles * length // 1024, 8, 128), F32)]
        + [pltpu.VMEM((tiles * length // 8, 128), F32)] * 3
        + [pltpu.VMEM((PARAMS * rows, 128), F32)]
        + [
            pltpu.VMEM((length, 256), F32),
            pltpu.VMEM((length, 256), F32),
            pltpu.VMEM((length, 512), BF16),
            pltpu.VMEM((length, 512), BF16),
        ]
        * 2,
        compiler_params=LIMIT,
        name="render",
    )(tile_counts, tile_ids, received, slots, cot)
    returned = exchange(slot_grads, peers, capacity)
    shapes = [jax.ShapeDtypeStruct((n, owned), F32) for n in (3, 3, 4, 3)]
    shapes.insert(3, jax.ShapeDtypeStruct((rows, 128), F32))
    grads = pl.pallas_call(
        lambda *refs: post_kernel(half_height, *refs),
        out_shape=tuple(shapes),
        in_specs=[SMEM] + [VMEM] * 4,
        out_specs=(VMEM,) * 5,
        scratch_shapes=[
            pltpu.VMEM((PARAMS, rows, 128), F32),
            pltpu.VMEM((13 * rows, 128), F32),
        ],
        compiler_params=LIMIT,
        name="unpack_and_project_back",
    )(view_shift, raw, inverse, view, returned)
    return (rendered, grads[0], grads[1], grads[2], grads[3].reshape(owned), grads[4])


def solution(mesh):
    wide = P(None, AXES)
    flat = P(AXES)
    return jax.shard_map(
        shards,
        mesh=mesh,
        in_specs=(
            wide,
            wide,
            wide,
            flat,
            wide,
            P("groups", None),
            flat,
            flat,
            P(AXES, None),
            P(AXES, None, None),
            wide,
        ),
        out_specs=(wide, wide, wide, wide, flat, wide),
        check_vma=False,
    )
```

```python
import math

import jax
import jax.numpy as jnp
from jax import lax
from jax.experimental import pallas as pl
from jax.experimental.pallas import tpu as pltpu
from jax.sharding import PartitionSpec as P

TILES_X = 32
FOCAL = 512.0
SH_ZERO = 0.28209479177387814
DILATION = 0.3
BACKGROUND = 1.0
DEPTH_OFFSET = 4.0
LOG2E = math.log2(math.e)
PARAMS = 9
ROW = PARAMS * 128
AXES = ("groups", "gs", "sub")
PEERS = ("gs", "sub")

BF16 = jnp.bfloat16
F32 = jnp.float32
NN = (((1,), (0,)), ((), ()))
NT = (((1,), (1,)), ((), ()))
TN = (((0,), (0,)), ((), ()))


def dot(lhs, rhs, dims=NN):
    return lax.dot_general(lhs, rhs, dims, preferred_element_type=F32)


def iota(shape, dim):
    return lax.broadcasted_iota(jnp.int32, shape, dim)


def halves(value):
    high = value.astype(BF16)
    return high, (value - high.astype(F32)).astype(BF16)


def lookup(row_of, index, rows):
    low = index & 127
    high = index >> 7
    found = jnp.zeros(index.shape, F32)
    for row in range(rows):
        spread = jnp.broadcast_to(row_of(row), index.shape)
        taken = jnp.take_along_axis(spread, low, axis=1, mode="promise_in_bounds")
        found = jnp.where(high == row, taken, found)
    return found


def project(raw, shift):
    centres, log_scales, rotations, logit, colours, half_height = raw
    half_width = 8.0 * TILES_X
    camera_x = centres[0] + shift[0]
    camera_y = centres[1] + shift[1]
    camera_z = centres[2] + shift[2] + DEPTH_OFFSET
    inv_norm = 1.0 / jnp.sqrt(sum(part * part for part in rotations))
    quat_w, quat_x, quat_y, quat_z = [part * inv_norm for part in rotations]
    rotation = [
        [
            1.0 - 2.0 * (quat_y * quat_y + quat_z * quat_z),
            2.0 * (quat_x * quat_y - quat_w * quat_z),
            2.0 * (quat_x * quat_z + quat_w * quat_y),
        ],
        [
            2.0 * (quat_x * quat_y + quat_w * quat_z),
            1.0 - 2.0 * (quat_x * quat_x + quat_z * quat_z),
            2.0 * (quat_y * quat_z - quat_w * quat_x),
        ],
        [
            2.0 * (quat_x * quat_z - quat_w * quat_y),
            2.0 * (quat_y * quat_z + quat_w * quat_x),
            1.0 - 2.0 * (quat_x * quat_x + quat_y * quat_y),
        ],
    ]
    scales = [jnp.exp(part) for part in log_scales]
    stretched = [[rotation[i][j] * scales[j] for j in range(3)] for i in range(3)]

    def covariance(i, j):
        return sum(stretched[i][mid] * stretched[j][mid] for mid in range(3))

    cov_xx, cov_xy, cov_xz = covariance(0, 0), covariance(0, 1), covariance(0, 2)
    cov_yy, cov_yz, cov_zz = covariance(1, 1), covariance(1, 2), covariance(2, 2)
    inv_z = 1.0 / camera_z
    focal_z = FOCAL * inv_z
    ratio_x = camera_x * inv_z
    ratio_y = camera_y * inv_z
    shear_x = -focal_z * ratio_x
    shear_y = -focal_z * ratio_y
    screen_xx = (
        focal_z * focal_z * cov_xx
        + 2.0 * focal_z * shear_x * cov_xz
        + shear_x * shear_x * cov_zz
        + DILATION
    )
    screen_yy = (
        focal_z * focal_z * cov_yy
        + 2.0 * focal_z * shear_y * cov_yz
        + shear_y * shear_y * cov_zz
        + DILATION
    )
    screen_xy = (
        focal_z * focal_z * cov_xy
        + focal_z * shear_y * cov_xz
        + shear_x * focal_z * cov_yz
        + shear_x * shear_y * cov_zz
    )
    inv_det = 1.0 / (screen_xx * screen_yy - screen_xy * screen_xy)
    return [
        FOCAL * ratio_x + half_width,
        FOCAL * ratio_y + half_height,
        screen_yy * inv_det,
        -screen_xy * inv_det,
        screen_xx * inv_det,
        1.0 / (1.0 + jnp.exp(-logit)),
    ] + [0.5 + SH_ZERO * part for part in colours]


def load_dense(ref, dense, first, rows):
    count = ref.shape[0]
    for row in range(rows):
        dense[pl.ds(first + row, count, stride=rows), :] = ref[:, row * 128 : row * 128 + 128]


def view_shifts(view, shift_ref):
    chosen = []
    for axis in range(3):
        value = jnp.full(view.shape, shift_ref[0, axis], F32)
        for other in range(1, shift_ref.shape[0]):
            value = jnp.where(view == other, shift_ref[other, axis], value)
        chosen.append(value)
    return chosen


def raw_rows(raw, rows, chunk):
    parts = [raw[i * rows + chunk * 8 : i * rows + chunk * 8 + 8, :] for i in range(14)]
    return parts[:3], parts[3:6], parts[6:10], parts[13], parts[10:13]


def pre_kernel(
    half_height,
    tiles_view,
    shift_ref,
    count_ref,
    id_ref,
    centre_hbm,
    scale_hbm,
    rotation_hbm,
    logit_hbm,
    colour_hbm,
    send_hbm,
    list_hbm,
    out_ref,
    inverse_ref,
    view_ref,
    raw,
    slots,
    marks,
    centre_ref,
    scale_ref,
    rotation_ref,
    colour_ref,
    send_ref,
    list_ref,
    index,
    table,
    arrived,
):
    rows = table.shape[0] // PARAMS
    owned = rows * 128
    logit_ref = raw.at[pl.ds(13 * rows, rows), :]
    pairs = [
        (send_hbm, send_ref),
        (centre_hbm, centre_ref),
        (scale_hbm, scale_ref),
        (rotation_hbm, rotation_ref),
        (colour_hbm, colour_ref),
        (logit_hbm, logit_ref),
        (list_hbm, list_ref),
    ]
    copies = [
        pltpu.make_async_copy(source, target, arrived.at[i])
        for i, (source, target) in enumerate(pairs)
    ]
    for copy in copies:
        copy.start()
    copies[0].wait()
    per = send_ref.shape[1] // 128
    peers = send_ref.shape[0]
    for part in range(per):
        index[pl.ds(part, peers, stride=per), :] = send_ref[:, part * 128 : part * 128 + 128]
    total = jnp.zeros((2 * rows, 128), F32)
    group = 8
    for start in range(0, rows, group):
        lefts, rights = [], []
        for row in range(start, start + group):
            entry = index[row : row + 1, :]
            local = entry % owned
            slot = row * 128 + iota((1, 128), 1)
            first = (slot >> 6).astype(F32)
            second = ((slot & 63) + 64 * (entry // owned)).astype(F32)
            match = jnp.broadcast_to(local >> 7, (rows, 128)) == iota((rows, 128), 0)
            lefts.append(
                jnp.concatenate([jnp.where(match, first, 0.0), jnp.where(match, second, 0.0)], 0)
            )
            rights.append(
                jnp.where(
                    jnp.broadcast_to(local & 127, (128, 128)) == iota((128, 128), 0), 1.0, 0.0
                )
            )
        left = jnp.concatenate(lefts, 1).astype(BF16)
        right = jnp.concatenate(rights, 1).astype(BF16)
        total = total + dot(left, right, NT)
    whole = (total + 0.5).astype(jnp.int32)
    second = whole[rows:]
    inverse_ref[...] = whole[:rows] * 64 + (second & 63)
    view_ref[...] = second >> 6
    for copy in copies[1:6]:
        copy.wait()
    first = 0
    for ref in (centre_ref, scale_ref, rotation_ref, colour_ref):
        load_dense(ref, raw, first, rows)
        first += ref.shape[0] * rows
    for chunk in range(rows // 8):
        parts = raw_rows(raw, rows, chunk)
        shift = view_shifts(view_ref[chunk * 8 : chunk * 8 + 8, :], shift_ref)
        for c, value in enumerate(project(parts + (half_height,), shift)):
            table[c * rows + chunk * 8 : c * rows + chunk * 8 + 8, :] = value
    local = [index[i * 8 : i * 8 + 8, :] % owned for i in range(rows // 8)]

    def gather(c, carry):
        lane = pl.multiple_of(c * 128, 128)
        for i in range(rows // 8):
            found = lookup(lambda row: table[pl.ds(c * rows + row, 1), :], local[i], rows)
            for s in range(8):
                out_ref[i * 8 + s, :, pl.ds(lane, 128)] = found[s : s + 1, :]
        return carry

    lax.fori_loop(0, PARAMS, gather, 0)
    copies[6].wait()
    tiles, length = list_ref.shape
    blocks = length // 128
    lane = iota((8, 128), 1)
    for b in range(blocks):
        entry = run_entry(lane, b, length)
        for i in range(tiles // 8):
            moved = jnp.zeros((8, 128), jnp.int32)
            for source in range(blocks):
                value = list_ref[i * 8 : i * 8 + 8, source * 128 : source * 128 + 128]
                taken = jnp.take_along_axis(
                    value, entry & 127, axis=1, mode="promise_in_bounds"
                )
                moved = jnp.where(entry >> 7 == source, taken, moved)
            slots[pl.ds(i * 8 * blocks + b, 8, stride=blocks), :] = moved
    for t in range(tiles):
        local = lax.rem(id_ref[t], tiles_view)
        mark = count_ref[t] + 1024 * local
        marks[t * blocks : t * blocks + blocks, :] = jnp.full((blocks, 128), mark, jnp.int32)


def run_entry(lane, block, length):
    return (lane & 7) * (length // 8) + block * 16 + (lane >> 3)


def render_kernel(
    length,
    table_ref,
    slots,
    marks,
    cot_ref,
    image_ref,
    grad_ref,
    gathered,
    coefs,
    moments,
    grads,
    slot_ref,
    *buffers,
):
    blocks = length // 128
    tiles = slots.shape[0] // blocks
    rows = table_ref.shape[0]
    group = 8 // blocks
    steps = length // 16
    groups = tiles // group
    lane = iota((8, 128), 1)
    block_of = iota((8, 128), 0) % blocks

    feature = iota((8, 256), 0)
    pixel = iota((8, 256), 1)
    px = (pixel & 15).astype(F32) - 7.5
    py = (pixel >> 4).astype(F32) - 7.5
    features = jnp.where(feature == 0, px * px, 0.0)
    for k, value in enumerate([py * py, px * py, px, py, jnp.ones_like(px)]):
        features = jnp.where(feature == k + 1, value, features)
    blank = jnp.zeros((24, 256), F32)
    moment_rows = jnp.concatenate([features, jnp.zeros((8, 256), F32)], 0)
    moment_rows = jnp.concatenate([moment_rows, moment_rows], 1).astype(BF16)
    run_row = iota((8, 256), 0)

    def earlier_product(value):
        for step in (1, 2, 4):
            moved = pltpu.roll(value, step, 0)
            value = value * jnp.where(run_row >= step, moved, 1.0)
        return jnp.where(run_row >= 1, pltpu.roll(value, 1, 0), 1.0)

    def later_sum(value):
        for step in (1, 2, 4):
            moved = pltpu.roll(value, 8 - step, 0)
            value = value + jnp.where(run_row < 8 - step, moved, 0.0)
        return jnp.where(run_row < 7, pltpu.roll(value, 7, 0), 0.0)

    def spread(k):
        return pl.ds(k, 8, stride=16)

    def placed(g, params):
        u, w, a, b, e, o = params
        mark = marks[pl.ds(pl.multiple_of(g * 8, 8), 8), :]
        local = mark >> 10
        mid_x = (16 * lax.rem(local, TILES_X) + 8).astype(F32)
        mid_y = (16 * lax.div(local, TILES_X) + 8).astype(F32)
        return u - mid_x, w - mid_y, a, b, e, o, mark & 1023

    def gather(g):
        index = slots[pl.ds(pl.multiple_of(g * 8, 8), 8), :]
        low = index & 127
        high = index >> 7
        found = [jnp.zeros((8, 128), F32)] * PARAMS
        for row in range(rows):
            is_row = high == row
            for c in range(PARAMS):
                value = jnp.broadcast_to(table_ref[row, :, c * 128 : c * 128 + 128], (8, 128))
                value = jnp.take_along_axis(value, low, axis=1, mode="promise_in_bounds")
                found[c] = jnp.where(is_row, value, found[c])
        for c in range(6):
            gathered[g, c] = found[c]
        du, dw, a, b, e, o, live = placed(g, found[:6])
        entry = (lane & 7) * (length // 8) + block_of * 16 + (lane >> 3)
        is_live = entry < live
        slope_x = a * du + b * dw
        slope_y = e * dw + b * du
        level = -0.5 * (du * slope_x + dw * slope_y) + jnp.log(o)
        values = [-0.5 * a, -0.5 * e, -b, slope_x, slope_y, level]
        for k, value in enumerate(values):
            dead = -1000.0 if k == 5 else 0.0
            coefs[spread(k), :] = jnp.where(is_live, value * LOG2E, dead)
        for k in range(3):
            coefs[spread(8 + k), :] = found[6 + k] - BACKGROUND

    def chain(g):
        du, dw, a, b, e, o, _ = placed(g, [gathered[g, c] for c in range(6)])
        m_xx, m_yy, m_xy, m_x, m_y, m_one = [moments[spread(k), :] for k in range(6)]
        d_x = m_x - du * m_one
        d_y = m_y - dw * m_one
        values = [
            a * d_x + b * d_y,
            e * d_y + b * d_x,
            -0.5 * (m_xx - du * (m_x + d_x)),
            -(m_xy - dw * m_x - du * d_y),
            -0.5 * (m_yy - dw * (m_y + d_y)),
            m_one / o,
        ] + [moments[spread(8 + k), :] for k in range(3)]
        for c, value in enumerate(values):
            high = value.astype(BF16).astype(F32)
            grads[2 * c] = high
            grads[2 * c + 1] = value - high

    def scatter(g):
        index = slots[pl.ds(pl.multiple_of(g * 8, 8), 8), :]
        lefts, rights = [], []
        for r in range(8):
            slot = index[r : r + 1, :]
            match = jnp.broadcast_to(slot >> 8, (rows // 2, 128)) == iota((rows // 2, 128), 0)
            where = jnp.broadcast_to(slot & 255, (256, 128)) == iota((256, 128), 0)
            rights.append(jnp.where(where, 1.0, 0.0).astype(BF16))
            parts = [
                jnp.where(match, jnp.broadcast_to(grads[c, r : r + 1, :], match.shape), 0.0)
                for c in range(2 * PARAMS)
            ]
            lefts.append(jnp.concatenate(parts, 0).astype(BF16))
        slot_ref[...] += dot(jnp.concatenate(lefts, 1), jnp.concatenate(rights, 1), NT)

    def operands(t, i):
        lanes = pl.ds(pl.multiple_of(t * 256, 256), 256)
        cot = jnp.concatenate([cot_ref[:, lanes], jnp.zeros((5, 256), F32)], 0)
        cot_high = cot.astype(BF16).astype(F32)
        cot_low = cot - cot_high
        right = jnp.concatenate(
            [
                jnp.concatenate([features, features, features, blank], 0),
                jnp.concatenate([blank, cot_high, cot_high, cot_low], 0),
            ],
            1,
        ).astype(BF16)
        cot_rows = jnp.concatenate([cot_high, cot_low], 0)
        cot_rows = jnp.concatenate([cot_rows, cot_rows], 1).astype(BF16)
        lefts, tints = [], []
        for b in range(blocks):
            base = (i * blocks + b) * 16
            coef = coefs[base : base + 8, :]
            tint = coefs[base + 8 : base + 16, :]
            coef_high = coef.astype(BF16).astype(F32)
            rest = coef - coef_high
            coef_mid = rest.astype(BF16).astype(F32)
            tint_high = tint.astype(BF16).astype(F32)
            tint_low = tint - tint_high
            lefts.append(
                jnp.concatenate(
                    [coef_high, coef_mid, rest - coef_mid, tint_high, tint_low, tint_high], 0
                )
            )
            tints.append(jnp.concatenate([tint_high, tint_low], 0))
        left = jnp.concatenate(lefts, 1).astype(BF16)
        tint_rows = jnp.concatenate(tints, 1).astype(BF16)
        return lanes, cot_rows, tint_rows, dot(left, right, TN)

    def render(i, lanes, cot_rows, tint_rows, both, alpha_ref, share_ref, weights, slopes):
        left_over = jnp.ones((8, 256), F32)
        for step in range(steps):
            here = slice(step * 16, step * 16 + 16)
            alpha = jnp.exp2(both[here, :256])
            alpha_ref[here, :] = alpha
            keep = 1.0 - alpha
            left_over = left_over * (keep[:8] * keep[8:])
        through = earlier_product(left_over)
        total = jnp.zeros((8, 256), F32)
        for step in range(steps):
            here = slice(step * 16, step * 16 + 16)
            alpha = alpha_ref[here, :]
            first = alpha[:8] * through
            through = through - first
            second = alpha[8:] * through
            through = through - second
            weight = jnp.concatenate([first, second], 0)
            high, low = halves(weight)
            weights[here, :256] = high
            weights[here, 256:] = low
            share = weight * both[here, 256:]
            share_ref[here, :] = share
            total = total + (share[:8] + share[8:])
        image = dot(tint_rows, weights[:, :256])
        image_ref[:, lanes] = BACKGROUND + (image[:8] + image[8:])[:3]
        tint_grad = dot(cot_rows, weights[...], NT)
        tint_grad = tint_grad[:8] + tint_grad[8:]
        behind = later_sum(total)
        for step in reversed(range(steps)):
            here = slice(step * 16, step * 16 + 16)
            alpha = alpha_ref[here, :]
            share = share_ref[here, :]
            beta = alpha * (1.0 + alpha * (1.0 + alpha))
            second = share[8:] - beta[8:] * behind
            behind = behind + share[8:]
            first = share[:8] - beta[:8] * behind
            behind = behind + share[:8]
            high, low = halves(jnp.concatenate([first, second], 0))
            slopes[here, :256] = high
            slopes[here, 256:] = low
        summed = dot(moment_rows, slopes[...], NT)
        for b in range(blocks):
            base = (i * blocks + b) * 16
            here = slice(b * 128, b * 128 + 128)
            moments[base : base + 8, :] = summed[:8, here]
            moments[base + 8 : base + 16, :] = tint_grad[:, here]

    slot_ref[...] = jnp.zeros(slot_ref.shape, F32)
    moments[...] = jnp.zeros(moments.shape, F32)
    coefs[...] = jnp.zeros(coefs.shape, F32)
    gather(0)

    def step(g, carry):
        before = jnp.maximum(g - 1, 0)
        chain(before)
        ready = [operands(g * group + i, i) for i in range(group)]
        gather(jnp.minimum(g + 1, groups - 1))
        scatter(before)
        for i in range(group):
            render(i, *ready[i], *buffers[4 * i : 4 * i + 4])
        return carry

    lax.fori_loop(0, groups, step, 0)
    chain(groups - 1)
    scatter(groups - 1)

    half = rows // 2
    for c in range(PARAMS):
        high = slot_ref[2 * c * half : (2 * c + 1) * half, :]
        value = high + slot_ref[(2 * c + 1) * half : (2 * c + 2) * half, :]
        for row in range(rows):
            part = value[row // 2 : row // 2 + 1, row % 2 * 128 : row % 2 * 128 + 128]
            grad_ref[row, :, c * 128 : c * 128 + 128] = part


def post_kernel(
    half_height,
    shift_ref,
    raw,
    inverse_ref,
    view_ref,
    table_ref,
    centre_out,
    scale_out,
    rotation_out,
    logit_out,
    colour_out,
    grads,
    dense_out,
):
    rows = logit_out.shape[0]
    index = [inverse_ref[i * 8 : i * 8 + 8, :] for i in range(rows // 8)]

    def gather(c, carry):
        offset = pl.multiple_of(c * 128, 128)
        for i in range(rows // 8):
            grads[c, i * 8 : i * 8 + 8, :] = lookup(
                lambda row: table_ref[row, :, pl.ds(offset, 128)], index[i], rows
            )
        return carry

    lax.fori_loop(0, PARAMS, gather, 0)
    for chunk in range(rows // 8):
        parts = raw_rows(raw, rows, chunk)
        shift = view_shifts(view_ref[chunk * 8 : chunk * 8 + 8, :], shift_ref)
        _, pull = jax.vjp(lambda *args: project(args + (half_height,), shift), *parts)
        back = pull([grads[c, chunk * 8 : chunk * 8 + 8, :] for c in range(PARAMS)])
        flat = back[0] + back[1] + back[2] + back[4]
        for k, value in enumerate(flat):
            dense_out[k * rows + chunk * 8 : k * rows + chunk * 8 + 8, :] = value
        logit_out[chunk * 8 : chunk * 8 + 8, :] = back[3]
    first = 0
    for ref in (centre_out, scale_out, rotation_out, colour_out):
        count = ref.shape[0]
        for row in range(rows):
            ref[:, row * 128 : row * 128 + 128] = dense_out[
                pl.ds(first + row, count, stride=rows), :
            ]
        first += count * rows


def exchange(table, peers, capacity):
    if capacity % 128 == 0:
        return lax.all_to_all(table, PEERS, split_axis=0, concat_axis=0, tiled=True)
    rows = table.shape[0]
    per = 128 // capacity
    chunks = table.reshape(rows, PARAMS, per, capacity).transpose(0, 2, 1, 3)
    chunks = chunks.reshape(peers, 1, PARAMS * capacity)
    moved = lax.all_to_all(chunks, PEERS, split_axis=0, concat_axis=0, tiled=True)
    moved = moved.reshape(rows, per, PARAMS, capacity).transpose(0, 2, 1, 3)
    return moved.reshape(rows, 1, ROW)


VMEM = pl.BlockSpec(memory_space=pltpu.VMEM)
SMEM = pl.BlockSpec(memory_space=pltpu.SMEM)
HBM = pl.BlockSpec(memory_space=pltpu.HBM)
LIMIT = pltpu.CompilerParams(vmem_limit_bytes=40 * 1024 * 1024)
FULL = pltpu.CompilerParams(vmem_limit_bytes=60 * 1024 * 1024)


def shards(
    centres,
    log_scales,
    rotations,
    opacity_logits,
    colours,
    view_shift,
    tile_ids,
    tile_counts,
    tile_lists,
    send_index,
    image_cot,
):
    owned = centres.shape[1]
    rows = owned // 128
    peers, capacity = send_index.shape[1:]
    tiles, length = tile_lists.shape
    views = view_shift.shape[0]
    tiles_view = tiles * peers // views
    half_height = 8.0 * (tiles_view // TILES_X)
    assert peers * capacity == owned
    logits = opacity_logits.reshape(rows, 128)
    targets = send_index[0] if capacity % 128 == 0 else send_index.reshape(rows, 128)
    table_shape = jax.ShapeDtypeStruct((rows, 1, ROW), F32)
    whole = jax.ShapeDtypeStruct((rows, 128), jnp.int32)
    entry_shape = jax.ShapeDtypeStruct((tiles * length // 128, 128), jnp.int32)
    outgoing, inverse, view, raw, slots, marks = pl.pallas_call(
        lambda *refs: pre_kernel(half_height, tiles_view, *refs),
        out_shape=(
            table_shape,
            whole,
            whole,
            jax.ShapeDtypeStruct((14 * rows, 128), F32),
            entry_shape,
            entry_shape,
        ),
        in_specs=[SMEM] * 3 + [HBM] * 7,
        out_specs=(VMEM,) * 6,
        scratch_shapes=[pltpu.VMEM((n, owned), F32) for n in (3, 3, 4, 3)]
        + [
            pltpu.VMEM(targets.shape, jnp.int32),
            pltpu.VMEM(tile_lists.shape, jnp.int32),
            pltpu.VMEM((rows, 128), jnp.int32),
            pltpu.VMEM((PARAMS * rows, 128), F32),
            pltpu.SemaphoreType.DMA((7,)),
        ],
        compiler_params=FULL,
        name="project_and_pack",
    )(
        view_shift,
        tile_counts,
        tile_ids,
        centres,
        log_scales,
        rotations,
        logits,
        colours,
        targets,
        tile_lists,
    )
    received = exchange(outgoing, peers, capacity)
    rendered, slot_grads = pl.pallas_call(
        lambda *refs: render_kernel(length, *refs),
        out_shape=(jax.ShapeDtypeStruct((3, tiles * 256), F32), table_shape),
        in_specs=[VMEM] * 4,
        out_specs=(VMEM,) * 2,
        scratch_shapes=[
            pltpu.VMEM((tiles * length // 1024, 6, 8, 128), F32),
            pltpu.VMEM((128, 128), F32),
            pltpu.VMEM((128, 128), F32),
            pltpu.VMEM((2 * PARAMS, 8, 128), F32),
            pltpu.VMEM((PARAMS * rows, 256), F32),
        ]
        + [
            pltpu.VMEM((length, 256), F32),
            pltpu.VMEM((length, 256), F32),
            pltpu.VMEM((length, 512), BF16),
            pltpu.VMEM((length, 512), BF16),
        ]
        * (1024 // length),
        compiler_params=LIMIT,
        name="render",
    )(received, slots, marks, image_cot)
    returned = exchange(slot_grads, peers, capacity)
    shapes = [jax.ShapeDtypeStruct((n, owned), F32) for n in (3, 3, 4, 3)]
    shapes.insert(3, jax.ShapeDtypeStruct((rows, 128), F32))
    grads = pl.pallas_call(
        lambda *refs: post_kernel(half_height, *refs),
        out_shape=tuple(shapes),
        in_specs=[SMEM] + [VMEM] * 4,
        out_specs=(VMEM,) * 5,
        scratch_shapes=[
            pltpu.VMEM((PARAMS, rows, 128), F32),
            pltpu.VMEM((13 * rows, 128), F32),
        ],
        compiler_params=LIMIT,
        name="unpack_and_project_back",
    )(view_shift, raw, inverse, view, returned)
    return (rendered, grads[0], grads[1], grads[2], grads[3].reshape(owned), grads[4])


def solution(mesh):
    wide = P(None, AXES)
    flat = P(AXES)
    return jax.shard_map(
        shards,
        mesh=mesh,
        in_specs=(
            wide,
            wide,
            wide,
            flat,
            wide,
            P("groups", None),
            flat,
            flat,
            P(AXES, None),
            P(AXES, None, None),
            wide,
        ),
        out_specs=(wide, wide, wide, wide, flat, wide),
        check_vma=False,
    )
```

```python
import math

import jax
import jax.numpy as jnp
from jax import lax
from jax.experimental import pallas as pl
from jax.experimental.pallas import tpu as pltpu
from jax.sharding import PartitionSpec as P

TILES_X = 32
FOCAL = 512.0
SH_ZERO = 0.28209479177387814
DILATION = 0.3
BACKGROUND = 1.0
DEPTH_OFFSET = 4.0
LOG2E = math.log2(math.e)
PARAMS = 9
ROW = PARAMS * 128
AXES = ("groups", "gs", "sub")
PEERS = ("gs", "sub")

BF16 = jnp.bfloat16
F32 = jnp.float32
NN = (((1,), (0,)), ((), ()))
NT = (((1,), (1,)), ((), ()))
TN = (((0,), (0,)), ((), ()))


def dot(lhs, rhs, dims=NN):
    return lax.dot_general(lhs, rhs, dims, preferred_element_type=F32)


def iota(shape, dim):
    return lax.broadcasted_iota(jnp.int32, shape, dim)


def halves(value):
    high = value.astype(BF16)
    return high, (value - high.astype(F32)).astype(BF16)


def lookup(row_of, index, rows):
    low = index & 127
    high = index >> 7
    found = jnp.zeros(index.shape, F32)
    for row in range(rows):
        spread = jnp.broadcast_to(row_of(row), index.shape)
        taken = jnp.take_along_axis(spread, low, axis=1, mode="promise_in_bounds")
        found = jnp.where(high == row, taken, found)
    return found


def project(raw, shift):
    centres, log_scales, rotations, logit, colours, half_height = raw
    half_width = 8.0 * TILES_X
    camera_x = centres[0] + shift[0]
    camera_y = centres[1] + shift[1]
    camera_z = centres[2] + shift[2] + DEPTH_OFFSET
    inv_norm = 1.0 / jnp.sqrt(sum(part * part for part in rotations))
    quat_w, quat_x, quat_y, quat_z = [part * inv_norm for part in rotations]
    rotation = [
        [
            1.0 - 2.0 * (quat_y * quat_y + quat_z * quat_z),
            2.0 * (quat_x * quat_y - quat_w * quat_z),
            2.0 * (quat_x * quat_z + quat_w * quat_y),
        ],
        [
            2.0 * (quat_x * quat_y + quat_w * quat_z),
            1.0 - 2.0 * (quat_x * quat_x + quat_z * quat_z),
            2.0 * (quat_y * quat_z - quat_w * quat_x),
        ],
        [
            2.0 * (quat_x * quat_z - quat_w * quat_y),
            2.0 * (quat_y * quat_z + quat_w * quat_x),
            1.0 - 2.0 * (quat_x * quat_x + quat_y * quat_y),
        ],
    ]
    scales = [jnp.exp(part) for part in log_scales]
    stretched = [[rotation[i][j] * scales[j] for j in range(3)] for i in range(3)]

    def covariance(i, j):
        return sum(stretched[i][mid] * stretched[j][mid] for mid in range(3))

    cov_xx, cov_xy, cov_xz = covariance(0, 0), covariance(0, 1), covariance(0, 2)
    cov_yy, cov_yz, cov_zz = covariance(1, 1), covariance(1, 2), covariance(2, 2)
    inv_z = 1.0 / camera_z
    focal_z = FOCAL * inv_z
    ratio_x = camera_x * inv_z
    ratio_y = camera_y * inv_z
    shear_x = -focal_z * ratio_x
    shear_y = -focal_z * ratio_y
    screen_xx = (
        focal_z * focal_z * cov_xx
        + 2.0 * focal_z * shear_x * cov_xz
        + shear_x * shear_x * cov_zz
        + DILATION
    )
    screen_yy = (
        focal_z * focal_z * cov_yy
        + 2.0 * focal_z * shear_y * cov_yz
        + shear_y * shear_y * cov_zz
        + DILATION
    )
    screen_xy = (
        focal_z * focal_z * cov_xy
        + focal_z * shear_y * cov_xz
        + shear_x * focal_z * cov_yz
        + shear_x * shear_y * cov_zz
    )
    inv_det = 1.0 / (screen_xx * screen_yy - screen_xy * screen_xy)
    return [
        FOCAL * ratio_x + half_width,
        FOCAL * ratio_y + half_height,
        screen_yy * inv_det,
        -screen_xy * inv_det,
        screen_xx * inv_det,
        1.0 / (1.0 + jnp.exp(-logit)),
    ] + [0.5 + SH_ZERO * part for part in colours]


def load_dense(ref, dense, first, rows):
    count = ref.shape[0]
    for row in range(rows):
        dense[pl.ds(first + row, count, stride=rows), :] = ref[:, row * 128 : row * 128 + 128]


def view_shifts(view, shift_ref):
    chosen = []
    for axis in range(3):
        value = jnp.full(view.shape, shift_ref[0, axis], F32)
        for other in range(1, shift_ref.shape[0]):
            value = jnp.where(view == other, shift_ref[other, axis], value)
        chosen.append(value)
    return chosen


def raw_rows(raw, rows, chunk):
    parts = [raw[i * rows + chunk * 8 : i * rows + chunk * 8 + 8, :] for i in range(14)]
    return parts[:3], parts[3:6], parts[6:10], parts[13], parts[10:13]


def pre_kernel(
    half_height,
    tiles_view,
    shift_hbm,
    count_hbm,
    id_hbm,
    centre_hbm,
    scale_hbm,
    rotation_hbm,
    logit_hbm,
    colour_hbm,
    send_hbm,
    list_hbm,
    out_ref,
    inverse_ref,
    shifts,
    raw,
    slots,
    marks,
    shift_ref,
    count_ref,
    id_ref,
    centre_ref,
    scale_ref,
    rotation_ref,
    colour_ref,
    send_ref,
    list_ref,
    index,
    table,
    arrived,
):
    rows = table.shape[0] // PARAMS
    owned = rows * 128
    logit_ref = raw.at[pl.ds(13 * rows, rows), :]
    pairs = [
        (send_hbm, send_ref),
        (shift_hbm, shift_ref),
        (centre_hbm, centre_ref),
        (scale_hbm, scale_ref),
        (rotation_hbm, rotation_ref),
        (colour_hbm, colour_ref),
        (logit_hbm, logit_ref),
        (list_hbm, list_ref),
        (count_hbm, count_ref),
        (id_hbm, id_ref),
    ]
    copies = [
        pltpu.make_async_copy(source, target, arrived.at[i])
        for i, (source, target) in enumerate(pairs)
    ]
    for copy in copies:
        copy.start()
    copies[0].wait()
    per = send_ref.shape[1] // 128
    peers = send_ref.shape[0]
    for part in range(per):
        index[pl.ds(part, peers, stride=per), :] = send_ref[:, part * 128 : part * 128 + 128]
    total = jnp.zeros((2 * rows, 128), F32)
    group = 8
    for start in range(0, rows, group):
        lefts, rights = [], []
        for row in range(start, start + group):
            entry = index[row : row + 1, :]
            local = entry % owned
            slot = row * 128 + iota((1, 128), 1)
            first = (slot >> 6).astype(F32)
            second = ((slot & 63) + 64 * (entry // owned)).astype(F32)
            match = jnp.broadcast_to(local >> 7, (rows, 128)) == iota((rows, 128), 0)
            lefts.append(
                jnp.concatenate([jnp.where(match, first, 0.0), jnp.where(match, second, 0.0)], 0)
            )
            rights.append(
                jnp.where(
                    jnp.broadcast_to(local & 127, (128, 128)) == iota((128, 128), 0), 1.0, 0.0
                )
            )
        left = jnp.concatenate(lefts, 1).astype(BF16)
        right = jnp.concatenate(rights, 1).astype(BF16)
        total = total + dot(left, right, NT)
    whole = (total + 0.5).astype(jnp.int32)
    second = whole[rows:]
    inverse_ref[...] = whole[:rows] * 64 + (second & 63)
    view = second >> 6
    for copy in copies[1:7]:
        copy.wait()
    first = 0
    for ref in (centre_ref, scale_ref, rotation_ref, colour_ref):
        load_dense(ref, raw, first, rows)
        first += ref.shape[0] * rows
    for chunk in range(rows // 8):
        parts = raw_rows(raw, rows, chunk)
        shift = view_shifts(view[chunk * 8 : chunk * 8 + 8, :], shift_ref)
        for axis in range(3):
            shifts[axis * rows + chunk * 8 : axis * rows + chunk * 8 + 8, :] = shift[axis]
        for c, value in enumerate(project(parts + (half_height,), shift)):
            table[c * rows + chunk * 8 : c * rows + chunk * 8 + 8, :] = value
    local = [index[i * 8 : i * 8 + 8, :] % owned for i in range(rows // 8)]

    def gather(c, carry):
        lane = pl.multiple_of(c * 128, 128)
        for i in range(rows // 8):
            found = lookup(lambda row: table[pl.ds(c * rows + row, 1), :], local[i], rows)
            for s in range(8):
                out_ref[i * 8 + s, :, pl.ds(lane, 128)] = found[s : s + 1, :]
        return carry

    lax.fori_loop(0, PARAMS, gather, 0)
    for copy in copies[7:]:
        copy.wait()
    tiles, length = list_ref.shape
    blocks = length // 128
    lane = iota((8, 128), 1)
    for b in range(blocks):
        entry = run_entry(lane, b, length)
        for i in range(tiles // 8):
            moved = jnp.zeros((8, 128), jnp.int32)
            for source in range(blocks):
                value = list_ref[i * 8 : i * 8 + 8, source * 128 : source * 128 + 128]
                taken = jnp.take_along_axis(
                    value, entry & 127, axis=1, mode="promise_in_bounds"
                )
                moved = jnp.where(entry >> 7 == source, taken, moved)
            slots[pl.ds(i * 8 * blocks + b, 8, stride=blocks), :] = moved
    for t in range(tiles):
        local = lax.rem(id_ref[t], tiles_view)
        mark = count_ref[t] + 1024 * local
        marks[t * blocks : t * blocks + blocks, :] = jnp.full((blocks, 128), mark, jnp.int32)


def run_entry(lane, block, length):
    return (lane & 7) * (length // 8) + block * 16 + (lane >> 3)


def render_kernel(
    length,
    table_ref,
    slots,
    marks,
    cot_ref,
    image_ref,
    grad_ref,
    gathered,
    coefs,
    moments,
    grads,
    slot_ref,
    *buffers,
):
    blocks = length // 128
    tiles = slots.shape[0] // blocks
    rows = table_ref.shape[0]
    group = 8 // blocks
    steps = length // 16
    groups = tiles // group
    lane = iota((8, 128), 1)
    block_of = iota((8, 128), 0) % blocks

    feature = iota((8, 256), 0)
    pixel = iota((8, 256), 1)
    px = (pixel & 15).astype(F32) - 7.5
    py = (pixel >> 4).astype(F32) - 7.5
    features = jnp.where(feature == 0, px * px, 0.0)
    for k, value in enumerate([py * py, px * py, px, py, jnp.ones_like(px)]):
        features = jnp.where(feature == k + 1, value, features)
    blank = jnp.zeros((24, 256), F32)
    moment_rows = jnp.concatenate([features, jnp.zeros((8, 256), F32)], 0)
    moment_rows = jnp.concatenate([moment_rows, moment_rows], 1).astype(BF16)
    run_row = iota((8, 256), 0)

    def earlier_product(value):
        for step in (1, 2, 4):
            moved = pltpu.roll(value, step, 0)
            value = value * jnp.where(run_row >= step, moved, 1.0)
        return jnp.where(run_row >= 1, pltpu.roll(value, 1, 0), 1.0)

    def later_sum(value):
        for step in (1, 2, 4):
            moved = pltpu.roll(value, 8 - step, 0)
            value = value + jnp.where(run_row < 8 - step, moved, 0.0)
        return jnp.where(run_row < 7, pltpu.roll(value, 7, 0), 0.0)

    def spread(k):
        return pl.ds(k, 8, stride=16)

    def placed(g, params):
        u, w, a, b, e, o = params
        mark = marks[pl.ds(pl.multiple_of(g * 8, 8), 8), :]
        local = mark >> 10
        mid_x = (16 * lax.rem(local, TILES_X) + 8).astype(F32)
        mid_y = (16 * lax.div(local, TILES_X) + 8).astype(F32)
        return u - mid_x, w - mid_y, a, b, e, o, mark & 1023

    def gather(g):
        index = slots[pl.ds(pl.multiple_of(g * 8, 8), 8), :]
        low = index & 127
        high = index >> 7
        found = [jnp.zeros((8, 128), F32)] * PARAMS
        for row in range(rows):
            is_row = high == row
            for c in range(PARAMS):
                value = jnp.broadcast_to(table_ref[row, :, c * 128 : c * 128 + 128], (8, 128))
                value = jnp.take_along_axis(value, low, axis=1, mode="promise_in_bounds")
                found[c] = jnp.where(is_row, value, found[c])
        for c in range(6):
            gathered[g, c] = found[c]
        du, dw, a, b, e, o, live = placed(g, found[:6])
        entry = (lane & 7) * (length // 8) + block_of * 16 + (lane >> 3)
        is_live = entry < live
        slope_x = a * du + b * dw
        slope_y = e * dw + b * du
        level = -0.5 * (du * slope_x + dw * slope_y) + jnp.log(o)
        values = [-0.5 * a, -0.5 * e, -b, slope_x, slope_y, level]
        for k, value in enumerate(values):
            dead = -1000.0 if k == 5 else 0.0
            coefs[spread(k), :] = jnp.where(is_live, value * LOG2E, dead)
        for k in range(3):
            coefs[spread(8 + k), :] = found[6 + k] - BACKGROUND

    def chain(g):
        du, dw, a, b, e, o, _ = placed(g, [gathered[g, c] for c in range(6)])
        m_xx, m_yy, m_xy, m_x, m_y, m_one = [moments[spread(k), :] for k in range(6)]
        d_x = m_x - du * m_one
        d_y = m_y - dw * m_one
        values = [
            a * d_x + b * d_y,
            e * d_y + b * d_x,
            -0.5 * (m_xx - du * (m_x + d_x)),
            -(m_xy - dw * m_x - du * d_y),
            -0.5 * (m_yy - dw * (m_y + d_y)),
            m_one / o,
        ] + [moments[spread(8 + k), :] for k in range(3)]
        for c, value in enumerate(values):
            high = value.astype(BF16).astype(F32)
            grads[2 * c] = high
            grads[2 * c + 1] = value - high

    def scatter(g):
        index = slots[pl.ds(pl.multiple_of(g * 8, 8), 8), :]
        lefts, rights = [], []
        for r in range(8):
            slot = index[r : r + 1, :]
            match = jnp.broadcast_to(slot >> 8, (rows // 2, 128)) == iota((rows // 2, 128), 0)
            where = jnp.broadcast_to(slot & 255, (256, 128)) == iota((256, 128), 0)
            rights.append(jnp.where(where, 1.0, 0.0).astype(BF16))
            parts = [
                jnp.where(match, jnp.broadcast_to(grads[c, r : r + 1, :], match.shape), 0.0)
                for c in range(2 * PARAMS)
            ]
            lefts.append(jnp.concatenate(parts, 0).astype(BF16))
        slot_ref[...] += dot(jnp.concatenate(lefts, 1), jnp.concatenate(rights, 1), NT)

    def operands(t, i):
        lanes = pl.ds(pl.multiple_of(t * 256, 256), 256)
        cot = jnp.concatenate([cot_ref[:, lanes], jnp.zeros((5, 256), F32)], 0)
        cot_high = cot.astype(BF16).astype(F32)
        cot_low = cot - cot_high
        right = jnp.concatenate(
            [
                jnp.concatenate([features, features, features, blank], 0),
                jnp.concatenate([blank, cot_high, cot_high, cot_low], 0),
            ],
            1,
        ).astype(BF16)
        cot_rows = jnp.concatenate([cot_high, cot_low], 0)
        cot_rows = jnp.concatenate([cot_rows, cot_rows], 1).astype(BF16)
        lefts, tints = [], []
        for b in range(blocks):
            base = (i * blocks + b) * 16
            coef = coefs[base : base + 8, :]
            tint = coefs[base + 8 : base + 16, :]
            coef_high = coef.astype(BF16).astype(F32)
            rest = coef - coef_high
            coef_mid = rest.astype(BF16).astype(F32)
            tint_high = tint.astype(BF16).astype(F32)
            tint_low = tint - tint_high
            lefts.append(
                jnp.concatenate(
                    [coef_high, coef_mid, rest - coef_mid, tint_high, tint_low, tint_high], 0
                )
            )
            tints.append(jnp.concatenate([tint_high, tint_low], 0))
        left = jnp.concatenate(lefts, 1).astype(BF16)
        tint_rows = jnp.concatenate(tints, 1).astype(BF16)
        return lanes, cot_rows, tint_rows, dot(left, right, TN)

    def render(i, lanes, cot_rows, tint_rows, both, alpha_ref, share_ref, weights, slopes):
        left_over = jnp.ones((8, 256), F32)
        for step in range(steps):
            here = slice(step * 16, step * 16 + 16)
            alpha = jnp.exp2(both[here, :256])
            alpha_ref[here, :] = alpha
            keep = 1.0 - alpha
            left_over = left_over * (keep[:8] * keep[8:])
        through = earlier_product(left_over)
        total = jnp.zeros((8, 256), F32)
        for step in range(steps):
            here = slice(step * 16, step * 16 + 16)
            alpha = alpha_ref[here, :]
            first = alpha[:8] * through
            through = through - first
            second = alpha[8:] * through
            through = through - second
            weight = jnp.concatenate([first, second], 0)
            high, low = halves(weight)
            weights[here, :256] = high
            weights[here, 256:] = low
            share = weight * both[here, 256:]
            share_ref[here, :] = share
            total = total + (share[:8] + share[8:])
        image = dot(tint_rows, weights[:, :256])
        image_ref[:, lanes] = BACKGROUND + (image[:8] + image[8:])[:3]
        tint_grad = dot(cot_rows, weights[...], NT)
        tint_grad = tint_grad[:8] + tint_grad[8:]
        behind = later_sum(total)
        for step in reversed(range(steps)):
            here = slice(step * 16, step * 16 + 16)
            alpha = alpha_ref[here, :]
            share = share_ref[here, :]
            beta = alpha * (1.0 + alpha * (1.0 + alpha))
            second = share[8:] - beta[8:] * behind
            behind = behind + share[8:]
            first = share[:8] - beta[:8] * behind
            behind = behind + share[:8]
            high, low = halves(jnp.concatenate([first, second], 0))
            slopes[here, :256] = high
            slopes[here, 256:] = low
        summed = dot(moment_rows, slopes[...], NT)
        for b in range(blocks):
            base = (i * blocks + b) * 16
            here = slice(b * 128, b * 128 + 128)
            moments[base : base + 8, :] = summed[:8, here]
            moments[base + 8 : base + 16, :] = tint_grad[:, here]

    slot_ref[...] = jnp.zeros(slot_ref.shape, F32)
    moments[...] = jnp.zeros(moments.shape, F32)
    coefs[...] = jnp.zeros(coefs.shape, F32)
    gather(0)

    def step(g, carry):
        before = jnp.maximum(g - 1, 0)
        chain(before)
        ready = [operands(g * group + i, i) for i in range(group)]
        gather(jnp.minimum(g + 1, groups - 1))
        scatter(before)
        for i in range(group):
            render(i, *ready[i], *buffers[4 * i : 4 * i + 4])
        return carry

    lax.fori_loop(0, groups, step, 0)
    chain(groups - 1)
    scatter(groups - 1)

    half = rows // 2
    for c in range(PARAMS):
        high = slot_ref[2 * c * half : (2 * c + 1) * half, :]
        value = high + slot_ref[(2 * c + 1) * half : (2 * c + 2) * half, :]
        for row in range(rows):
            part = value[row // 2 : row // 2 + 1, row % 2 * 128 : row % 2 * 128 + 128]
            grad_ref[row, :, c * 128 : c * 128 + 128] = part


def post_kernel(
    half_height,
    raw,
    inverse_ref,
    shifts,
    table_ref,
    centre_out,
    scale_out,
    rotation_out,
    logit_out,
    colour_out,
    grads,
    dense_out,
):
    rows = logit_out.shape[0]
    index = [inverse_ref[i * 8 : i * 8 + 8, :] for i in range(rows // 8)]

    def gather(c, carry):
        offset = pl.multiple_of(c * 128, 128)
        for i in range(rows // 8):
            grads[c, i * 8 : i * 8 + 8, :] = lookup(
                lambda row: table_ref[row, :, pl.ds(offset, 128)], index[i], rows
            )
        return carry

    lax.fori_loop(0, PARAMS, gather, 0)
    for chunk in range(rows // 8):
        parts = raw_rows(raw, rows, chunk)
        shift = [
            shifts[axis * rows + chunk * 8 : axis * rows + chunk * 8 + 8, :] for axis in range(3)
        ]
        _, pull = jax.vjp(lambda *args: project(args + (half_height,), shift), *parts)
        back = pull([grads[c, chunk * 8 : chunk * 8 + 8, :] for c in range(PARAMS)])
        flat = back[0] + back[1] + back[2] + back[4]
        for k, value in enumerate(flat):
            dense_out[k * rows + chunk * 8 : k * rows + chunk * 8 + 8, :] = value
        logit_out[chunk * 8 : chunk * 8 + 8, :] = back[3]
    first = 0
    for ref in (centre_out, scale_out, rotation_out, colour_out):
        count = ref.shape[0]
        for row in range(rows):
            ref[:, row * 128 : row * 128 + 128] = dense_out[
                pl.ds(first + row, count, stride=rows), :
            ]
        first += count * rows


def exchange(table, peers, capacity):
    if capacity % 128 == 0:
        return lax.all_to_all(table, PEERS, split_axis=0, concat_axis=0, tiled=True)
    rows = table.shape[0]
    per = 128 // capacity
    chunks = table.reshape(rows, PARAMS, per, capacity).transpose(0, 2, 1, 3)
    chunks = chunks.reshape(peers, 1, PARAMS * capacity)
    moved = lax.all_to_all(chunks, PEERS, split_axis=0, concat_axis=0, tiled=True)
    moved = moved.reshape(rows, per, PARAMS, capacity).transpose(0, 2, 1, 3)
    return moved.reshape(rows, 1, ROW)


VMEM = pl.BlockSpec(memory_space=pltpu.VMEM)
HBM = pl.BlockSpec(memory_space=pltpu.HBM)
LIMIT = pltpu.CompilerParams(vmem_limit_bytes=40 * 1024 * 1024)


def shards(
    centres,
    log_scales,
    rotations,
    opacity_logits,
    colours,
    view_shift,
    tile_ids,
    tile_counts,
    tile_lists,
    send_index,
    image_cot,
):
    owned = centres.shape[1]
    rows = owned // 128
    peers, capacity = send_index.shape[1:]
    tiles, length = tile_lists.shape
    views = view_shift.shape[0]
    tiles_view = tiles * peers // views
    half_height = 8.0 * (tiles_view // TILES_X)
    assert peers * capacity == owned
    logits = opacity_logits.reshape(rows, 128)
    targets = send_index[0] if capacity % 128 == 0 else send_index.reshape(rows, 128)
    table_shape = jax.ShapeDtypeStruct((rows, 1, ROW), F32)
    whole = jax.ShapeDtypeStruct((rows, 128), jnp.int32)
    entry_shape = jax.ShapeDtypeStruct((tiles * length // 128, 128), jnp.int32)
    outgoing, inverse, shifts, raw, slots, marks = pl.pallas_call(
        lambda *refs: pre_kernel(half_height, tiles_view, *refs),
        out_shape=(
            table_shape,
            whole,
            jax.ShapeDtypeStruct((3 * rows, 128), F32),
            jax.ShapeDtypeStruct((14 * rows, 128), F32),
            entry_shape,
            entry_shape,
        ),
        in_specs=[HBM] * 10,
        out_specs=(VMEM,) * 6,
        scratch_shapes=[
            pltpu.SMEM(view_shift.shape, F32),
            pltpu.SMEM(tile_counts.shape, jnp.int32),
            pltpu.SMEM(tile_ids.shape, jnp.int32),
        ]
        + [pltpu.VMEM((n, owned), F32) for n in (3, 3, 4, 3)]
        + [
            pltpu.VMEM(targets.shape, jnp.int32),
            pltpu.VMEM(tile_lists.shape, jnp.int32),
            pltpu.VMEM((rows, 128), jnp.int32),
            pltpu.VMEM((PARAMS * rows, 128), F32),
            pltpu.SemaphoreType.DMA((10,)),
        ],
        compiler_params=LIMIT,
        name="project_and_pack",
    )(
        *[
            pltpu.with_memory_space_constraint(array, pltpu.HBM)
            for array in (
                view_shift,
                tile_counts,
                tile_ids,
                centres,
                log_scales,
                rotations,
                logits,
                colours,
                targets,
                tile_lists,
            )
        ],
    )
    received = exchange(outgoing, peers, capacity)
    rendered, slot_grads = pl.pallas_call(
        lambda *refs: render_kernel(length, *refs),
        out_shape=(jax.ShapeDtypeStruct((3, tiles * 256), F32), table_shape),
        in_specs=[VMEM] * 4,
        out_specs=(VMEM,) * 2,
        scratch_shapes=[
            pltpu.VMEM((tiles * length // 1024, 6, 8, 128), F32),
            pltpu.VMEM((128, 128), F32),
            pltpu.VMEM((128, 128), F32),
            pltpu.VMEM((2 * PARAMS, 8, 128), F32),
            pltpu.VMEM((PARAMS * rows, 256), F32),
        ]
        + [
            pltpu.VMEM((length, 256), F32),
            pltpu.VMEM((length, 256), F32),
            pltpu.VMEM((length, 512), BF16),
            pltpu.VMEM((length, 512), BF16),
        ]
        * (1024 // length),
        compiler_params=LIMIT,
        name="render",
    )(received, slots, marks, image_cot)
    returned = exchange(slot_grads, peers, capacity)
    shapes = [jax.ShapeDtypeStruct((n, owned), F32) for n in (3, 3, 4, 3)]
    shapes.insert(3, jax.ShapeDtypeStruct((rows, 128), F32))
    grads = pl.pallas_call(
        lambda *refs: post_kernel(half_height, *refs),
        out_shape=tuple(shapes),
        in_specs=[VMEM] * 4,
        out_specs=(VMEM,) * 5,
        scratch_shapes=[
            pltpu.VMEM((PARAMS, rows, 128), F32),
            pltpu.VMEM((13 * rows, 128), F32),
        ],
        compiler_params=LIMIT,
        name="unpack_and_project_back",
    )(raw, inverse, shifts, returned)
    return (rendered, grads[0], grads[1], grads[2], grads[3].reshape(owned), grads[4])


def solution(mesh):
    wide = P(None, AXES)
    flat = P(AXES)
    return jax.shard_map(
        shards,
        mesh=mesh,
        in_specs=(
            wide,
            wide,
            wide,
            flat,
            wide,
            P("groups", None),
            flat,
            flat,
            P(AXES, None),
            P(AXES, None, None),
            wide,
        ),
        out_specs=(wide, wide, wide, wide, flat, wide),
        check_vma=False,
    )
```

```python
import math

import jax
import jax.numpy as jnp
from jax import lax
from jax.experimental import pallas as pl
from jax.experimental.pallas import tpu as pltpu
from jax.sharding import PartitionSpec as P

TILES_X = 32
FOCAL = 512.0
SH_ZERO = 0.28209479177387814
DILATION = 0.3
BACKGROUND = 1.0
DEPTH_OFFSET = 4.0
LOG2E = math.log2(math.e)
PARAMS = 9
ROW = PARAMS * 128
AXES = ("groups", "gs", "sub")
PEERS = ("gs", "sub")

BF16 = jnp.bfloat16
F32 = jnp.float32
NN = (((1,), (0,)), ((), ()))
NT = (((1,), (1,)), ((), ()))
TN = (((0,), (0,)), ((), ()))


def dot(lhs, rhs, dims=NN):
    return lax.dot_general(lhs, rhs, dims, preferred_element_type=F32)


def iota(shape, dim):
    return lax.broadcasted_iota(jnp.int32, shape, dim)


def halves(value):
    high = value.astype(BF16)
    return high, (value - high.astype(F32)).astype(BF16)


def lookup(row_of, index, rows):
    low = index & 127
    high = index >> 7
    found = jnp.zeros(index.shape, F32)
    for row in range(rows):
        spread = jnp.broadcast_to(row_of(row), index.shape)
        taken = jnp.take_along_axis(spread, low, axis=1, mode="promise_in_bounds")
        found = jnp.where(high == row, taken, found)
    return found


def project(raw, shift):
    centres, log_scales, rotations, logit, colours, half_height = raw
    half_width = 8.0 * TILES_X
    camera_x = centres[0] + shift[0]
    camera_y = centres[1] + shift[1]
    camera_z = centres[2] + shift[2] + DEPTH_OFFSET
    inv_norm = 1.0 / jnp.sqrt(sum(part * part for part in rotations))
    quat_w, quat_x, quat_y, quat_z = [part * inv_norm for part in rotations]
    rotation = [
        [
            1.0 - 2.0 * (quat_y * quat_y + quat_z * quat_z),
            2.0 * (quat_x * quat_y - quat_w * quat_z),
            2.0 * (quat_x * quat_z + quat_w * quat_y),
        ],
        [
            2.0 * (quat_x * quat_y + quat_w * quat_z),
            1.0 - 2.0 * (quat_x * quat_x + quat_z * quat_z),
            2.0 * (quat_y * quat_z - quat_w * quat_x),
        ],
        [
            2.0 * (quat_x * quat_z - quat_w * quat_y),
            2.0 * (quat_y * quat_z + quat_w * quat_x),
            1.0 - 2.0 * (quat_x * quat_x + quat_y * quat_y),
        ],
    ]
    scales = [jnp.exp(part) for part in log_scales]
    stretched = [[rotation[i][j] * scales[j] for j in range(3)] for i in range(3)]

    def covariance(i, j):
        return sum(stretched[i][mid] * stretched[j][mid] for mid in range(3))

    cov_xx, cov_xy, cov_xz = covariance(0, 0), covariance(0, 1), covariance(0, 2)
    cov_yy, cov_yz, cov_zz = covariance(1, 1), covariance(1, 2), covariance(2, 2)
    inv_z = 1.0 / camera_z
    focal_z = FOCAL * inv_z
    ratio_x = camera_x * inv_z
    ratio_y = camera_y * inv_z
    shear_x = -focal_z * ratio_x
    shear_y = -focal_z * ratio_y
    screen_xx = (
        focal_z * focal_z * cov_xx
        + 2.0 * focal_z * shear_x * cov_xz
        + shear_x * shear_x * cov_zz
        + DILATION
    )
    screen_yy = (
        focal_z * focal_z * cov_yy
        + 2.0 * focal_z * shear_y * cov_yz
        + shear_y * shear_y * cov_zz
        + DILATION
    )
    screen_xy = (
        focal_z * focal_z * cov_xy
        + focal_z * shear_y * cov_xz
        + shear_x * focal_z * cov_yz
        + shear_x * shear_y * cov_zz
    )
    inv_det = 1.0 / (screen_xx * screen_yy - screen_xy * screen_xy)
    return [
        FOCAL * ratio_x + half_width,
        FOCAL * ratio_y + half_height,
        screen_yy * inv_det,
        -screen_xy * inv_det,
        screen_xx * inv_det,
        1.0 / (1.0 + jnp.exp(-logit)),
    ] + [0.5 + SH_ZERO * part for part in colours]


def load_dense(ref, dense, first, rows):
    count = ref.shape[0]
    for row in range(rows):
        dense[pl.ds(first + row, count, stride=rows), :] = ref[:, row * 128 : row * 128 + 128]


def view_shifts(view, shift_ref):
    chosen = []
    for axis in range(3):
        value = jnp.full(view.shape, shift_ref[0, axis], F32)
        for other in range(1, shift_ref.shape[0]):
            value = jnp.where(view == other, shift_ref[other, axis], value)
        chosen.append(value)
    return chosen


def raw_rows(raw, rows, chunk):
    parts = [raw[i * rows + chunk * 8 : i * rows + chunk * 8 + 8, :] for i in range(14)]
    return parts[:3], parts[3:6], parts[6:10], parts[13], parts[10:13]


def pre_kernel(
    half_height,
    tiles_view,
    shift_hbm,
    count_hbm,
    id_hbm,
    centre_hbm,
    scale_hbm,
    rotation_hbm,
    logit_hbm,
    colour_hbm,
    send_hbm,
    list_hbm,
    out_ref,
    inverse_ref,
    shifts,
    raw,
    slots,
    marks,
    shift_ref,
    count_ref,
    id_ref,
    centre_ref,
    scale_ref,
    rotation_ref,
    colour_ref,
    send_ref,
    list_ref,
    index,
    table,
    arrived,
):
    rows = table.shape[0] // PARAMS
    owned = rows * 128
    logit_ref = raw.at[pl.ds(13 * rows, rows), :]
    pairs = [
        (send_hbm, send_ref),
        (shift_hbm, shift_ref),
        (centre_hbm, centre_ref),
        (scale_hbm, scale_ref),
        (rotation_hbm, rotation_ref),
        (colour_hbm, colour_ref),
        (logit_hbm, logit_ref),
        (list_hbm, list_ref),
        (count_hbm, count_ref),
        (id_hbm, id_ref),
    ]
    copies = [
        pltpu.make_async_copy(source, target, arrived.at[i])
        for i, (source, target) in enumerate(pairs)
    ]
    for copy in copies:
        copy.start()
    copies[0].wait()
    per = send_ref.shape[1] // 128
    peers = send_ref.shape[0]
    for part in range(per):
        index[pl.ds(part, peers, stride=per), :] = send_ref[:, part * 128 : part * 128 + 128]
    total = jnp.zeros((2 * rows, 128), F32)
    group = 8
    for start in range(0, rows, group):
        lefts, rights = [], []
        for row in range(start, start + group):
            entry = index[row : row + 1, :]
            local = entry % owned
            slot = row * 128 + iota((1, 128), 1)
            first = (slot >> 6).astype(F32)
            second = ((slot & 63) + 64 * (entry // owned)).astype(F32)
            match = jnp.broadcast_to(local >> 7, (rows, 128)) == iota((rows, 128), 0)
            lefts.append(
                jnp.concatenate([jnp.where(match, first, 0.0), jnp.where(match, second, 0.0)], 0)
            )
            rights.append(
                jnp.where(
                    jnp.broadcast_to(local & 127, (128, 128)) == iota((128, 128), 0), 1.0, 0.0
                )
            )
        left = jnp.concatenate(lefts, 1).astype(BF16)
        right = jnp.concatenate(rights, 1).astype(BF16)
        total = total + dot(left, right, NT)
    whole = (total + 0.5).astype(jnp.int32)
    second = whole[rows:]
    inverse_ref[...] = whole[:rows] * 64 + (second & 63)
    view = second >> 6
    for copy in copies[1:7]:
        copy.wait()
    first = 0
    for ref in (centre_ref, scale_ref, rotation_ref, colour_ref):
        load_dense(ref, raw, first, rows)
        first += ref.shape[0] * rows
    for chunk in range(rows // 8):
        parts = raw_rows(raw, rows, chunk)
        shift = view_shifts(view[chunk * 8 : chunk * 8 + 8, :], shift_ref)
        for axis in range(3):
            shifts[axis * rows + chunk * 8 : axis * rows + chunk * 8 + 8, :] = shift[axis]
        for c, value in enumerate(project(parts + (half_height,), shift)):
            table[c * rows + chunk * 8 : c * rows + chunk * 8 + 8, :] = value
    local = [index[i * 8 : i * 8 + 8, :] % owned for i in range(rows // 8)]

    def gather(c, carry):
        lane = pl.multiple_of(c * 128, 128)
        for i in range(rows // 8):
            found = lookup(lambda row: table[pl.ds(c * rows + row, 1), :], local[i], rows)
            for s in range(8):
                out_ref[i * 8 + s, :, pl.ds(lane, 128)] = found[s : s + 1, :]
        return carry

    lax.fori_loop(0, PARAMS, gather, 0)
    for copy in copies[7:]:
        copy.wait()
    tiles, length = list_ref.shape
    blocks = length // 128
    lane = iota((8, 128), 1)
    for b in range(blocks):
        entry = run_entry(lane, b, length)
        for i in range(tiles // 8):
            moved = jnp.zeros((8, 128), jnp.int32)
            for source in range(blocks):
                value = list_ref[i * 8 : i * 8 + 8, source * 128 : source * 128 + 128]
                taken = jnp.take_along_axis(
                    value, entry & 127, axis=1, mode="promise_in_bounds"
                )
                moved = jnp.where(entry >> 7 == source, taken, moved)
            slots[pl.ds(i * 8 * blocks + b, 8, stride=blocks), :] = moved
    for t in range(tiles):
        local = lax.rem(id_ref[t], tiles_view)
        mark = count_ref[t] + 1024 * local
        marks[t * blocks : t * blocks + blocks, :] = jnp.full((blocks, 128), mark, jnp.int32)


def run_entry(lane, block, length):
    return (lane & 7) * (length // 8) + block * 16 + (lane >> 3)


def render_kernel(
    length,
    table_ref,
    slots,
    marks,
    cot_ref,
    image_ref,
    grad_ref,
    gathered,
    coefs,
    moments,
    grads,
    slot_ref,
    *buffers,
):
    blocks = length // 128
    tiles = slots.shape[0] // blocks
    rows = table_ref.shape[0]
    group = 8 // blocks
    steps = length // 16
    groups = tiles // group
    lane = iota((8, 128), 1)
    block_of = iota((8, 128), 0) % blocks

    feature = iota((8, 256), 0)
    pixel = iota((8, 256), 1)
    px = (pixel & 15).astype(F32) - 7.5
    py = (pixel >> 4).astype(F32) - 7.5
    features = jnp.where(feature == 0, px * px, 0.0)
    for k, value in enumerate([py * py, px * py, px, py, jnp.ones_like(px)]):
        features = jnp.where(feature == k + 1, value, features)
    blank = jnp.zeros((24, 256), F32)
    moment = iota((16, 96), 0)
    power = iota((16, 96), 1) % 48 // 16
    at = (iota((16, 96), 1) % 16).astype(F32) - 7.5
    moment_rows = jnp.zeros((16, 96), F32)
    for k, (y_power, value) in enumerate(
        [(0, at * at), (2, 1.0), (1, at), (0, at), (1, 1.0), (0, 1.0)]
    ):
        moment_rows = jnp.where((moment == k) & (power == y_power), value, moment_rows)
    moment_rows = moment_rows.astype(BF16)
    run_row = iota((8, 256), 0)

    def earlier_product(value):
        for step in (1, 2, 4):
            moved = pltpu.roll(value, step, 0)
            value = value * jnp.where(run_row >= step, moved, 1.0)
        return jnp.where(run_row >= 1, pltpu.roll(value, 1, 0), 1.0)

    def later_sum(value):
        for step in (1, 2, 4):
            moved = pltpu.roll(value, 8 - step, 0)
            value = value + jnp.where(run_row < 8 - step, moved, 0.0)
        return jnp.where(run_row < 7, pltpu.roll(value, 7, 0), 0.0)

    def spread(k):
        return pl.ds(k, 8, stride=16)

    def placed(g, params):
        u, w, a, b, e, o = params
        mark = marks[pl.ds(pl.multiple_of(g * 8, 8), 8), :]
        local = mark >> 10
        mid_x = (16 * lax.rem(local, TILES_X) + 8).astype(F32)
        mid_y = (16 * lax.div(local, TILES_X) + 8).astype(F32)
        return u - mid_x, w - mid_y, a, b, e, o, mark & 1023

    def gather(g):
        index = slots[pl.ds(pl.multiple_of(g * 8, 8), 8), :]
        low = index & 127
        high = index >> 7
        found = [jnp.zeros((8, 128), F32)] * PARAMS
        for row in range(rows):
            is_row = high == row
            for c in range(PARAMS):
                value = jnp.broadcast_to(table_ref[row, :, c * 128 : c * 128 + 128], (8, 128))
                value = jnp.take_along_axis(value, low, axis=1, mode="promise_in_bounds")
                found[c] = jnp.where(is_row, value, found[c])
        for c in range(6):
            gathered[g, c] = found[c]
        du, dw, a, b, e, o, live = placed(g, found[:6])
        entry = (lane & 7) * (length // 8) + block_of * 16 + (lane >> 3)
        is_live = entry < live
        slope_x = a * du + b * dw
        slope_y = e * dw + b * du
        level = -0.5 * (du * slope_x + dw * slope_y) + jnp.log(o)
        values = [-0.5 * a, -0.5 * e, -b, slope_x, slope_y, level]
        for k, value in enumerate(values):
            dead = -1000.0 if k == 5 else 0.0
            coefs[spread(k), :] = jnp.where(is_live, value * LOG2E, dead)
        for k in range(3):
            coefs[spread(8 + k), :] = found[6 + k] - BACKGROUND

    def chain(g):
        for i in range(group):
            summed = dot(moment_rows, buffers[5 * i + 4][...])
            for b in range(blocks):
                base = (i * blocks + b) * 16
                moments[base : base + 8, :] = summed[:8, b * 128 : b * 128 + 128]
        du, dw, a, b, e, o, _ = placed(g, [gathered[g, c] for c in range(6)])
        m_xx, m_yy, m_xy, m_x, m_y, m_one = [moments[spread(k), :] for k in range(6)]
        d_x = m_x - du * m_one
        d_y = m_y - dw * m_one
        values = [
            a * d_x + b * d_y,
            e * d_y + b * d_x,
            -0.5 * (m_xx - du * (m_x + d_x)),
            -(m_xy - dw * m_x - du * d_y),
            -0.5 * (m_yy - dw * (m_y + d_y)),
            m_one / o,
        ] + [moments[spread(8 + k), :] for k in range(3)]
        for c, value in enumerate(values):
            high = value.astype(BF16).astype(F32)
            grads[2 * c] = high
            grads[2 * c + 1] = value - high

    def scatter(g):
        index = slots[pl.ds(pl.multiple_of(g * 8, 8), 8), :]
        lefts, rights = [], []
        for r in range(8):
            slot = index[r : r + 1, :]
            match = jnp.broadcast_to(slot >> 8, (rows // 2, 128)) == iota((rows // 2, 128), 0)
            where = jnp.broadcast_to(slot & 255, (256, 128)) == iota((256, 128), 0)
            rights.append(jnp.where(where, 1.0, 0.0).astype(BF16))
            parts = [
                jnp.where(match, jnp.broadcast_to(grads[c, r : r + 1, :], match.shape), 0.0)
                for c in range(2 * PARAMS)
            ]
            lefts.append(jnp.concatenate(parts, 0).astype(BF16))
        slot_ref[...] += dot(jnp.concatenate(lefts, 1), jnp.concatenate(rights, 1), NT)

    def operands(t, i):
        lanes = pl.ds(pl.multiple_of(t * 256, 256), 256)
        cot = jnp.concatenate([cot_ref[:, lanes], jnp.zeros((5, 256), F32)], 0)
        cot_high = cot.astype(BF16).astype(F32)
        cot_low = cot - cot_high
        right = jnp.concatenate(
            [
                jnp.concatenate([features, features, features, blank], 0),
                jnp.concatenate([blank, cot_high, cot_high, cot_low], 0),
            ],
            1,
        ).astype(BF16)
        cot_rows = jnp.concatenate([cot_high, cot_low], 0)
        cot_rows = jnp.concatenate([cot_rows, cot_rows], 1).astype(BF16)
        lefts, tints = [], []
        for b in range(blocks):
            base = (i * blocks + b) * 16
            coef = coefs[base : base + 8, :]
            tint = coefs[base + 8 : base + 16, :]
            coef_high = coef.astype(BF16).astype(F32)
            rest = coef - coef_high
            coef_mid = rest.astype(BF16).astype(F32)
            tint_high = tint.astype(BF16).astype(F32)
            tint_low = tint - tint_high
            lefts.append(
                jnp.concatenate(
                    [coef_high, coef_mid, rest - coef_mid, tint_high, tint_low, tint_high], 0
                )
            )
            tints.append(jnp.concatenate([tint_high, tint_low], 0))
        left = jnp.concatenate(lefts, 1).astype(BF16)
        tint_rows = jnp.concatenate(tints, 1).astype(BF16)
        return lanes, cot_rows, tint_rows, dot(left, right, TN)

    def render(i, lanes, cot_rows, tint_rows, both, alpha_ref, share_ref, weights, slopes, column_ref):
        left_over = jnp.ones((8, 256), F32)
        for step in range(steps):
            here = slice(step * 16, step * 16 + 16)
            alpha = jnp.exp2(both[here, :256])
            alpha_ref[here, :] = alpha
            keep = 1.0 - alpha
            left_over = left_over * (keep[:8] * keep[8:])
        through = earlier_product(left_over)
        total = jnp.zeros((8, 256), F32)
        for step in range(steps):
            here = slice(step * 16, step * 16 + 16)
            alpha = alpha_ref[here, :]
            first = alpha[:8] * through
            through = through - first
            second = alpha[8:] * through
            through = through - second
            weight = jnp.concatenate([first, second], 0)
            high, low = halves(weight)
            weights[here, :256] = high
            weights[here, 256:] = low
            share = weight * both[here, 256:]
            share_ref[here, :] = share
            total = total + (share[:8] + share[8:])
        image = dot(tint_rows, weights[:, :256])
        image_ref[:, lanes] = BACKGROUND + (image[:8] + image[8:])[:3]
        tint_grad = dot(cot_rows, weights[...], NT)
        tint_grad = tint_grad[:8] + tint_grad[8:]
        behind = later_sum(total)
        for step in reversed(range(steps)):
            here = slice(step * 16, step * 16 + 16)
            alpha = alpha_ref[here, :]
            share = share_ref[here, :]
            beta = alpha * (1.0 + alpha * (1.0 + alpha))
            second = share[8:] - beta[8:] * behind
            behind = behind + share[8:]
            first = share[:8] - beta[:8] * behind
            behind = behind + share[:8]
            slopes[here, :] = jnp.concatenate([first, second], 0)
        sums = [[], []]
        for b in range(blocks):
            upper, lower = [
                slopes[b * 128 : b * 128 + 128, side * 128 : side * 128 + 128].T
                for side in range(2)
            ]
            columns = [[], [], []]
            for x in range(0, 16, 8):
                parts = [jnp.zeros((8, 128), F32)] * 3
                for y in range(8):
                    near = lower[y * 16 + x : y * 16 + x + 8, :]
                    far = upper[112 - y * 16 + x : 120 - y * 16 + x, :]
                    both_sides = near + far
                    parts[0] = parts[0] + both_sides
                    parts[1] = parts[1] + (y + 0.5) * (near - far)
                    parts[2] = parts[2] + (y + 0.5) ** 2 * both_sides
                for k in range(3):
                    columns[k].append(parts[k])
            column = jnp.concatenate(columns[0] + columns[1] + columns[2], 0)
            column_high = column.astype(BF16).astype(F32)
            sums[0].append(column_high)
            sums[1].append(column - column_high)
        summed = jnp.concatenate([jnp.concatenate(part, 1) for part in sums], 0)
        column_ref[...] = summed.astype(BF16)
        for b in range(blocks):
            base = (i * blocks + b) * 16
            moments[base + 8 : base + 16, :] = tint_grad[:, b * 128 : b * 128 + 128]

    slot_ref[...] = jnp.zeros(slot_ref.shape, F32)
    moments[...] = jnp.zeros(moments.shape, F32)
    coefs[...] = jnp.zeros(coefs.shape, F32)
    for i in range(group):
        buffers[5 * i + 4][...] = jnp.zeros((96, length), BF16)
    gather(0)

    def step(g, carry):
        before = jnp.maximum(g - 1, 0)
        chain(before)
        ready = [operands(g * group + i, i) for i in range(group)]
        gather(jnp.minimum(g + 1, groups - 1))
        scatter(before)
        for i in range(group):
            render(i, *ready[i], *buffers[5 * i : 5 * i + 5])
        return carry

    lax.fori_loop(0, groups, step, 0)
    chain(groups - 1)
    scatter(groups - 1)

    half = rows // 2
    for c in range(PARAMS):
        high = slot_ref[2 * c * half : (2 * c + 1) * half, :]
        value = high + slot_ref[(2 * c + 1) * half : (2 * c + 2) * half, :]
        for row in range(rows):
            part = value[row // 2 : row // 2 + 1, row % 2 * 128 : row % 2 * 128 + 128]
            grad_ref[row, :, c * 128 : c * 128 + 128] = part


def post_kernel(
    half_height,
    raw,
    inverse_ref,
    shifts,
    table_ref,
    centre_out,
    scale_out,
    rotation_out,
    logit_out,
    colour_out,
    grads,
    dense_out,
):
    rows = logit_out.shape[0]
    index = [inverse_ref[i * 8 : i * 8 + 8, :] for i in range(rows // 8)]

    def gather(c, carry):
        offset = pl.multiple_of(c * 128, 128)
        for i in range(rows // 8):
            grads[c, i * 8 : i * 8 + 8, :] = lookup(
                lambda row: table_ref[row, :, pl.ds(offset, 128)], index[i], rows
            )
        return carry

    lax.fori_loop(0, PARAMS, gather, 0)
    for chunk in range(rows // 8):
        parts = raw_rows(raw, rows, chunk)
        shift = [
            shifts[axis * rows + chunk * 8 : axis * rows + chunk * 8 + 8, :] for axis in range(3)
        ]
        _, pull = jax.vjp(lambda *args: project(args + (half_height,), shift), *parts)
        back = pull([grads[c, chunk * 8 : chunk * 8 + 8, :] for c in range(PARAMS)])
        flat = back[0] + back[1] + back[2] + back[4]
        for k, value in enumerate(flat):
            dense_out[k * rows + chunk * 8 : k * rows + chunk * 8 + 8, :] = value
        logit_out[chunk * 8 : chunk * 8 + 8, :] = back[3]
    first = 0
    for ref in (centre_out, scale_out, rotation_out, colour_out):
        count = ref.shape[0]
        for row in range(rows):
            ref[:, row * 128 : row * 128 + 128] = dense_out[
                pl.ds(first + row, count, stride=rows), :
            ]
        first += count * rows


def exchange(table, peers, capacity):
    if capacity % 128 == 0:
        return lax.all_to_all(table, PEERS, split_axis=0, concat_axis=0, tiled=True)
    rows = table.shape[0]
    per = 128 // capacity
    chunks = table.reshape(rows, PARAMS, per, capacity).transpose(0, 2, 1, 3)
    chunks = chunks.reshape(peers, 1, PARAMS * capacity)
    moved = lax.all_to_all(chunks, PEERS, split_axis=0, concat_axis=0, tiled=True)
    moved = moved.reshape(rows, per, PARAMS, capacity).transpose(0, 2, 1, 3)
    return moved.reshape(rows, 1, ROW)


VMEM = pl.BlockSpec(memory_space=pltpu.VMEM)
HBM = pl.BlockSpec(memory_space=pltpu.HBM)
LIMIT = pltpu.CompilerParams(vmem_limit_bytes=40 * 1024 * 1024)


def shards(
    centres,
    log_scales,
    rotations,
    opacity_logits,
    colours,
    view_shift,
    tile_ids,
    tile_counts,
    tile_lists,
    send_index,
    image_cot,
):
    owned = centres.shape[1]
    rows = owned // 128
    peers, capacity = send_index.shape[1:]
    tiles, length = tile_lists.shape
    views = view_shift.shape[0]
    tiles_view = tiles * peers // views
    half_height = 8.0 * (tiles_view // TILES_X)
    assert peers * capacity == owned
    logits = opacity_logits.reshape(rows, 128)
    targets = send_index[0] if capacity % 128 == 0 else send_index.reshape(rows, 128)
    table_shape = jax.ShapeDtypeStruct((rows, 1, ROW), F32)
    whole = jax.ShapeDtypeStruct((rows, 128), jnp.int32)
    entry_shape = jax.ShapeDtypeStruct((tiles * length // 128, 128), jnp.int32)
    outgoing, inverse, shifts, raw, slots, marks = pl.pallas_call(
        lambda *refs: pre_kernel(half_height, tiles_view, *refs),
        out_shape=(
            table_shape,
            whole,
            jax.ShapeDtypeStruct((3 * rows, 128), F32),
            jax.ShapeDtypeStruct((14 * rows, 128), F32),
            entry_shape,
            entry_shape,
        ),
        in_specs=[HBM] * 10,
        out_specs=(VMEM,) * 6,
        scratch_shapes=[
            pltpu.SMEM(view_shift.shape, F32),
            pltpu.SMEM(tile_counts.shape, jnp.int32),
            pltpu.SMEM(tile_ids.shape, jnp.int32),
        ]
        + [pltpu.VMEM((n, owned), F32) for n in (3, 3, 4, 3)]
        + [
            pltpu.VMEM(targets.shape, jnp.int32),
            pltpu.VMEM(tile_lists.shape, jnp.int32),
            pltpu.VMEM((rows, 128), jnp.int32),
            pltpu.VMEM((PARAMS * rows, 128), F32),
            pltpu.SemaphoreType.DMA((10,)),
        ],
        compiler_params=LIMIT,
        name="project_and_pack",
    )(
        *[
            pltpu.with_memory_space_constraint(array, pltpu.HBM)
            for array in (
                view_shift,
                tile_counts,
                tile_ids,
                centres,
                log_scales,
                rotations,
                logits,
                colours,
                targets,
                tile_lists,
            )
        ],
    )
    received = exchange(outgoing, peers, capacity)
    rendered, slot_grads = pl.pallas_call(
        lambda *refs: render_kernel(length, *refs),
        out_shape=(jax.ShapeDtypeStruct((3, tiles * 256), F32), table_shape),
        in_specs=[VMEM] * 4,
        out_specs=(VMEM,) * 2,
        scratch_shapes=[
            pltpu.VMEM((tiles * length // 1024, 6, 8, 128), F32),
            pltpu.VMEM((128, 128), F32),
            pltpu.VMEM((128, 128), F32),
            pltpu.VMEM((2 * PARAMS, 8, 128), F32),
            pltpu.VMEM((PARAMS * rows, 256), F32),
        ]
        + [
            pltpu.VMEM((length, 256), F32),
            pltpu.VMEM((length, 256), F32),
            pltpu.VMEM((length, 512), BF16),
            pltpu.VMEM((length, 256), F32),
            pltpu.VMEM((96, length), BF16),
        ]
        * (1024 // length),
        compiler_params=LIMIT,
        name="render",
    )(received, slots, marks, image_cot)
    returned = exchange(slot_grads, peers, capacity)
    shapes = [jax.ShapeDtypeStruct((n, owned), F32) for n in (3, 3, 4, 3)]
    shapes.insert(3, jax.ShapeDtypeStruct((rows, 128), F32))
    grads = pl.pallas_call(
        lambda *refs: post_kernel(half_height, *refs),
        out_shape=tuple(shapes),
        in_specs=[VMEM] * 4,
        out_specs=(VMEM,) * 5,
        scratch_shapes=[
            pltpu.VMEM((PARAMS, rows, 128), F32),
            pltpu.VMEM((13 * rows, 128), F32),
        ],
        compiler_params=LIMIT,
        name="unpack_and_project_back",
    )(raw, inverse, shifts, returned)
    return (rendered, grads[0], grads[1], grads[2], grads[3].reshape(owned), grads[4])


def solution(mesh):
    wide = P(None, AXES)
    flat = P(AXES)
    return jax.shard_map(
        shards,
        mesh=mesh,
        in_specs=(
            wide,
            wide,
            wide,
            flat,
            wide,
            P("groups", None),
            flat,
            flat,
            P(AXES, None),
            P(AXES, None, None),
            wide,
        ),
        out_specs=(wide, wide, wide, wide, flat, wide),
        check_vma=False,
    )
```

```python
import math

import jax
import jax.numpy as jnp
from jax import lax
from jax.experimental import pallas as pl
from jax.experimental.pallas import tpu as pltpu
from jax.sharding import PartitionSpec as P

TILES_X = 32
FOCAL = 512.0
SH_ZERO = 0.28209479177387814
DILATION = 0.3
BACKGROUND = 1.0
DEPTH_OFFSET = 4.0
LOG2E = math.log2(math.e)
PARAMS = 9
ROW = PARAMS * 128
AXES = ("groups", "gs", "sub")
PEERS = ("gs", "sub")

BF16 = jnp.bfloat16
F32 = jnp.float32
NN = (((1,), (0,)), ((), ()))
NT = (((1,), (1,)), ((), ()))
TN = (((0,), (0,)), ((), ()))


def dot(lhs, rhs, dims=NN):
    return lax.dot_general(lhs, rhs, dims, preferred_element_type=F32)


def iota(shape, dim):
    return lax.broadcasted_iota(jnp.int32, shape, dim)


def halves(value):
    high = value.astype(BF16)
    return high, (value - high.astype(F32)).astype(BF16)


def lookups(row_of, index, rows, channels):
    low = index & 127
    high = index >> 7
    found = [jnp.zeros(index.shape, F32) for _ in channels]
    for row in range(rows):
        is_row = high == row
        for at, c in enumerate(channels):
            value = jnp.broadcast_to(row_of(c, row), index.shape)
            value = jnp.take_along_axis(value, low, axis=1, mode="promise_in_bounds")
            found[at] = jnp.where(is_row, value, found[at])
    return found


def shown(logit):
    return 1.0 / (1.0 + jnp.exp(-logit))


def tint(colour):
    return 0.5 + SH_ZERO * colour


def project(raw, shift):
    centres, log_scales, rotations, logit, colours, half_height = raw
    half_width = 8.0 * TILES_X
    camera_x = centres[0] + shift[0]
    camera_y = centres[1] + shift[1]
    camera_z = centres[2] + shift[2] + DEPTH_OFFSET
    inv_norm = 1.0 / jnp.sqrt(sum(part * part for part in rotations))
    quat_w, quat_x, quat_y, quat_z = [part * inv_norm for part in rotations]
    rotation = [
        [
            1.0 - 2.0 * (quat_y * quat_y + quat_z * quat_z),
            2.0 * (quat_x * quat_y - quat_w * quat_z),
            2.0 * (quat_x * quat_z + quat_w * quat_y),
        ],
        [
            2.0 * (quat_x * quat_y + quat_w * quat_z),
            1.0 - 2.0 * (quat_x * quat_x + quat_z * quat_z),
            2.0 * (quat_y * quat_z - quat_w * quat_x),
        ],
        [
            2.0 * (quat_x * quat_z - quat_w * quat_y),
            2.0 * (quat_y * quat_z + quat_w * quat_x),
            1.0 - 2.0 * (quat_x * quat_x + quat_y * quat_y),
        ],
    ]
    scales = [jnp.exp(part) for part in log_scales]
    stretched = [[rotation[i][j] * scales[j] for j in range(3)] for i in range(3)]

    def covariance(i, j):
        return sum(stretched[i][mid] * stretched[j][mid] for mid in range(3))

    cov_xx, cov_xy, cov_xz = covariance(0, 0), covariance(0, 1), covariance(0, 2)
    cov_yy, cov_yz, cov_zz = covariance(1, 1), covariance(1, 2), covariance(2, 2)
    inv_z = 1.0 / camera_z
    focal_z = FOCAL * inv_z
    ratio_x = camera_x * inv_z
    ratio_y = camera_y * inv_z
    shear_x = -focal_z * ratio_x
    shear_y = -focal_z * ratio_y
    screen_xx = (
        focal_z * focal_z * cov_xx
        + 2.0 * focal_z * shear_x * cov_xz
        + shear_x * shear_x * cov_zz
        + DILATION
    )
    screen_yy = (
        focal_z * focal_z * cov_yy
        + 2.0 * focal_z * shear_y * cov_yz
        + shear_y * shear_y * cov_zz
        + DILATION
    )
    screen_xy = (
        focal_z * focal_z * cov_xy
        + focal_z * shear_y * cov_xz
        + shear_x * focal_z * cov_yz
        + shear_x * shear_y * cov_zz
    )
    inv_det = 1.0 / (screen_xx * screen_yy - screen_xy * screen_xy)
    return [
        FOCAL * ratio_x + half_width,
        FOCAL * ratio_y + half_height,
        screen_yy * inv_det,
        -screen_xy * inv_det,
        screen_xx * inv_det,
        shown(logit),
    ] + [tint(part) for part in colours]


def load_dense(ref, dense, first, rows):
    count = ref.shape[0]
    for row in range(rows):
        dense[pl.ds(first + row, count, stride=rows), :] = ref[:, row * 128 : row * 128 + 128]


def view_shifts(view, shift_ref):
    chosen = []
    for axis in range(3):
        value = jnp.full(view.shape, shift_ref[0, axis], F32)
        for other in range(1, shift_ref.shape[0]):
            value = jnp.where(view == other, shift_ref[other, axis], value)
        chosen.append(value)
    return chosen


def raw_rows(raw, rows, chunk):
    parts = [raw[i * rows + chunk * 8 : i * rows + chunk * 8 + 8, :] for i in range(14)]
    return parts[:3], parts[3:6], parts[6:10], parts[13], parts[10:13]


def pre_kernel(
    half_height,
    tiles_view,
    shift_hbm,
    count_hbm,
    id_hbm,
    centre_hbm,
    scale_hbm,
    rotation_hbm,
    logit_hbm,
    colour_hbm,
    send_hbm,
    list_hbm,
    out_ref,
    inverse_ref,
    shifts,
    raw,
    slots,
    marks,
    shift_ref,
    count_ref,
    id_ref,
    centre_ref,
    scale_ref,
    rotation_ref,
    colour_ref,
    send_ref,
    list_ref,
    index,
    table,
    arrived,
):
    rows = table.shape[0] // PARAMS
    owned = rows * 128
    logit_ref = raw.at[pl.ds(13 * rows, rows), :]
    pairs = [
        (send_hbm, send_ref),
        (shift_hbm, shift_ref),
        (centre_hbm, centre_ref),
        (scale_hbm, scale_ref),
        (rotation_hbm, rotation_ref),
        (colour_hbm, colour_ref),
        (logit_hbm, logit_ref),
        (list_hbm, list_ref),
        (count_hbm, count_ref),
        (id_hbm, id_ref),
    ]
    copies = [
        pltpu.make_async_copy(source, target, arrived.at[i])
        for i, (source, target) in enumerate(pairs)
    ]
    for copy in copies:
        copy.start()
    for copy in copies[:7]:
        copy.wait()
    per = send_ref.shape[1] // 128
    peers = send_ref.shape[0]
    for part in range(per):
        index[pl.ds(part, peers, stride=per), :] = send_ref[:, part * 128 : part * 128 + 128]
    first = 0
    for ref in (centre_ref, scale_ref, rotation_ref, colour_ref):
        load_dense(ref, raw, first, rows)
        first += ref.shape[0] * rows
    for chunk in range(rows // 8):
        _, _, _, logit, colours = raw_rows(raw, rows, chunk)
        for c, value in enumerate([shown(logit)] + [tint(part) for part in colours]):
            at = (5 + c) * rows + chunk * 8
            table[at : at + 8, :] = value

    def gather(channels):
        for i in range(rows // 8):
            local = index[i * 8 : i * 8 + 8, :] % owned
            found = lookups(
                lambda c, row: table[c * rows + row : c * rows + row + 1, :],
                local,
                rows,
                channels,
            )
            for value, c in zip(found, channels):
                for s in range(8):
                    out_ref[i * 8 + s, :, c * 128 : c * 128 + 128] = value[s : s + 1, :]

    gather(range(5, PARAMS))
    total = jnp.zeros((2 * rows, 128), F32)
    group = 8
    for start in range(0, rows, group):
        lefts, rights = [], []
        for row in range(start, start + group):
            entry = index[row : row + 1, :]
            local = entry % owned
            slot = row * 128 + iota((1, 128), 1)
            first = (slot >> 6).astype(F32)
            second = ((slot & 63) + 64 * (entry // owned)).astype(F32)
            match = jnp.broadcast_to(local >> 7, (rows, 128)) == iota((rows, 128), 0)
            lefts.append(
                jnp.concatenate([jnp.where(match, first, 0.0), jnp.where(match, second, 0.0)], 0)
            )
            rights.append(
                jnp.where(
                    jnp.broadcast_to(local & 127, (128, 128)) == iota((128, 128), 0), 1.0, 0.0
                )
            )
        left = jnp.concatenate(lefts, 1).astype(BF16)
        right = jnp.concatenate(rights, 1).astype(BF16)
        total = total + dot(left, right, NT)
    whole = (total + 0.5).astype(jnp.int32)
    second = whole[rows:]
    inverse_ref[...] = whole[:rows] * 64 + (second & 63)
    view = second >> 6
    for chunk in range(rows // 8):
        parts = raw_rows(raw, rows, chunk)
        shift = view_shifts(view[chunk * 8 : chunk * 8 + 8, :], shift_ref)
        for axis in range(3):
            shifts[axis * rows + chunk * 8 : axis * rows + chunk * 8 + 8, :] = shift[axis]
        for c, value in enumerate(project(parts + (half_height,), shift)[:5]):
            table[c * rows + chunk * 8 : c * rows + chunk * 8 + 8, :] = value
    gather(range(5))
    for copy in copies[7:]:
        copy.wait()
    tiles, length = list_ref.shape
    blocks = length // 128
    lane = iota((8, 128), 1)
    for b in range(blocks):
        entry = run_entry(lane, b, length)
        for i in range(tiles // 8):
            moved = jnp.zeros((8, 128), jnp.int32)
            for source in range(blocks):
                value = list_ref[i * 8 : i * 8 + 8, source * 128 : source * 128 + 128]
                taken = jnp.take_along_axis(
                    value, entry & 127, axis=1, mode="promise_in_bounds"
                )
                moved = jnp.where(entry >> 7 == source, taken, moved)
            slots[pl.ds(i * 8 * blocks + b, 8, stride=blocks), :] = moved
    for t in range(tiles):
        local = lax.rem(id_ref[t], tiles_view)
        mark = count_ref[t] + 1024 * local
        marks[t * blocks : t * blocks + blocks, :] = jnp.full((blocks, 128), mark, jnp.int32)


def run_entry(lane, block, length):
    return (lane & 7) * (length // 8) + block * 16 + (lane >> 3)


def render_kernel(
    length,
    table_ref,
    slots,
    marks,
    cot_ref,
    image_ref,
    grad_ref,
    gathered,
    coefs,
    moments,
    grads,
    slot_ref,
    *buffers,
):
    blocks = length // 128
    tiles = slots.shape[0] // blocks
    rows = table_ref.shape[0]
    group = 8 // blocks
    steps = length // 16
    groups = tiles // group
    lane = iota((8, 128), 1)
    block_of = iota((8, 128), 0) % blocks

    feature = iota((8, 256), 0)
    pixel = iota((8, 256), 1)
    px = (pixel & 15).astype(F32) - 7.5
    py = (pixel >> 4).astype(F32) - 7.5
    features = jnp.where(feature == 0, px * px, 0.0)
    for k, value in enumerate([py * py, px * py, px, py, jnp.ones_like(px)]):
        features = jnp.where(feature == k + 1, value, features)
    blank = jnp.zeros((24, 256), F32)
    moment = iota((16, 96), 0)
    power = iota((16, 96), 1) % 48 // 16
    at = (iota((16, 96), 1) % 16).astype(F32) - 7.5
    moment_rows = jnp.zeros((16, 96), F32)
    for k, (y_power, value) in enumerate(
        [(0, at * at), (2, 1.0), (1, at), (0, at), (1, 1.0), (0, 1.0)]
    ):
        moment_rows = jnp.where((moment == k) & (power == y_power), value, moment_rows)
    moment_rows = moment_rows.astype(BF16)
    run_row = iota((8, 256), 0)

    def earlier_product(value):
        for step in (1, 2, 4):
            moved = pltpu.roll(value, step, 0)
            value = value * jnp.where(run_row >= step, moved, 1.0)
        return jnp.where(run_row >= 1, pltpu.roll(value, 1, 0), 1.0)

    def later_sum(value):
        for step in (1, 2, 4):
            moved = pltpu.roll(value, 8 - step, 0)
            value = value + jnp.where(run_row < 8 - step, moved, 0.0)
        return jnp.where(run_row < 7, pltpu.roll(value, 7, 0), 0.0)

    def spread(k):
        return pl.ds(k, 8, stride=16)

    def placed(g, params):
        u, w, a, b, e, o = params
        mark = marks[pl.ds(pl.multiple_of(g * 8, 8), 8), :]
        local = mark >> 10
        mid_x = (16 * lax.rem(local, TILES_X) + 8).astype(F32)
        mid_y = (16 * lax.div(local, TILES_X) + 8).astype(F32)
        return u - mid_x, w - mid_y, a, b, e, o, mark & 1023

    def gather(g):
        index = slots[pl.ds(pl.multiple_of(g * 8, 8), 8), :]
        found = lookups(
            lambda c, row: table_ref[row, :, c * 128 : c * 128 + 128],
            index,
            rows,
            range(PARAMS),
        )
        for c in range(6):
            gathered[g, c] = found[c]
        du, dw, a, b, e, o, live = placed(g, found[:6])
        entry = (lane & 7) * (length // 8) + block_of * 16 + (lane >> 3)
        is_live = entry < live
        slope_x = a * du + b * dw
        slope_y = e * dw + b * du
        level = -0.5 * (du * slope_x + dw * slope_y) + jnp.log(o)
        values = [-0.5 * a, -0.5 * e, -b, slope_x, slope_y, level]
        for k, value in enumerate(values):
            dead = -1000.0 if k == 5 else 0.0
            coefs[spread(k), :] = jnp.where(is_live, value * LOG2E, dead)
        for k in range(3):
            coefs[spread(8 + k), :] = found[6 + k] - BACKGROUND

    def chain(g):
        for i in range(group):
            summed = dot(moment_rows, buffers[5 * i + 4][...])
            for b in range(blocks):
                base = (i * blocks + b) * 16
                moments[base : base + 8, :] = summed[:8, b * 128 : b * 128 + 128]
        du, dw, a, b, e, o, _ = placed(g, [gathered[g, c] for c in range(6)])
        m_xx, m_yy, m_xy, m_x, m_y, m_one = [moments[spread(k), :] for k in range(6)]
        d_x = m_x - du * m_one
        d_y = m_y - dw * m_one
        values = [
            a * d_x + b * d_y,
            e * d_y + b * d_x,
            -0.5 * (m_xx - du * (m_x + d_x)),
            -(m_xy - dw * m_x - du * d_y),
            -0.5 * (m_yy - dw * (m_y + d_y)),
            m_one / o,
        ] + [moments[spread(8 + k), :] for k in range(3)]
        for c, value in enumerate(values):
            high = value.astype(BF16).astype(F32)
            grads[2 * c] = high
            grads[2 * c + 1] = value - high

    def scatter(g):
        index = slots[pl.ds(pl.multiple_of(g * 8, 8), 8), :]
        lefts, rights = [], []
        number = iota((256, 128), 0).astype(F32).astype(BF16)
        for r in range(8):
            slot = index[r : r + 1, :]
            match = jnp.broadcast_to(slot >> 8, (rows // 2, 128)) == iota((rows // 2, 128), 0)
            low = (slot & 255).astype(F32).astype(BF16)
            where = jnp.broadcast_to(low, (256, 128)) == number
            rights.append(jnp.where(where, jnp.ones((), BF16), jnp.zeros((), BF16)))
            parts = [
                jnp.where(match, jnp.broadcast_to(grads[c, r : r + 1, :], match.shape), 0.0)
                for c in range(2 * PARAMS)
            ]
            lefts.append(jnp.concatenate(parts, 0).astype(BF16))
        slot_ref[...] += dot(jnp.concatenate(lefts, 1), jnp.concatenate(rights, 1), NT)

    def operands(t, i):
        lanes = pl.ds(pl.multiple_of(t * 256, 256), 256)
        cot = jnp.concatenate([cot_ref[:, lanes], jnp.zeros((5, 256), F32)], 0)
        cot_high = cot.astype(BF16).astype(F32)
        cot_low = cot - cot_high
        right = jnp.concatenate(
            [
                jnp.concatenate([features, features, features, blank], 0),
                jnp.concatenate([blank, cot_high, cot_high, cot_low], 0),
            ],
            1,
        ).astype(BF16)
        cot_rows = jnp.concatenate([cot_high, cot_low], 0)
        cot_rows = jnp.concatenate([cot_rows, cot_rows], 1).astype(BF16)
        lefts, tints = [], []
        for b in range(blocks):
            base = (i * blocks + b) * 16
            coef = coefs[base : base + 8, :]
            tint = coefs[base + 8 : base + 16, :]
            coef_high = coef.astype(BF16).astype(F32)
            rest = coef - coef_high
            coef_mid = rest.astype(BF16).astype(F32)
            tint_high = tint.astype(BF16).astype(F32)
            tint_low = tint - tint_high
            lefts.append(
                jnp.concatenate(
                    [coef_high, coef_mid, rest - coef_mid, tint_high, tint_low, tint_high], 0
                )
            )
            tints.append(jnp.concatenate([tint_high, tint_low], 0))
        left = jnp.concatenate(lefts, 1).astype(BF16)
        tint_rows = jnp.concatenate(tints, 1).astype(BF16)
        return lanes, cot_rows, tint_rows, dot(left, right, TN)

    def render(i, lanes, cot_rows, tint_rows, both, alpha_ref, weight_ref, weights, slopes, column_ref):
        left_over = jnp.ones((8, 256), F32)
        for step in range(steps):
            here = slice(step * 16, step * 16 + 16)
            alpha = jnp.exp2(both[here, :256])
            alpha_ref[here, :] = alpha
            keep = 1.0 - alpha
            left_over = left_over * (keep[:8] * keep[8:])
        through = earlier_product(left_over)
        total = jnp.zeros((8, 256), F32)
        for step in range(steps):
            here = slice(step * 16, step * 16 + 16)
            alpha = alpha_ref[here, :]
            first = alpha[:8] * through
            through = through - first
            second = alpha[8:] * through
            through = through - second
            weight = jnp.concatenate([first, second], 0)
            high, low = halves(weight)
            weights[here, :256] = high
            weights[here, 256:] = low
            weight_ref[here, :] = weight
            share = weight * both[here, 256:]
            total = total + (share[:8] + share[8:])
        image = dot(tint_rows, weights[:, :256])
        image_ref[:, lanes] = BACKGROUND + (image[:8] + image[8:])[:3]
        tint_grad = dot(cot_rows, weights[...], NT)
        tint_grad = tint_grad[:8] + tint_grad[8:]
        behind = later_sum(total) / through
        for step in reversed(range(steps)):
            here = slice(step * 16, step * 16 + 16)
            alpha = alpha_ref[here, :]
            weight = weight_ref[here, :]
            shade = both[here, 256:]
            second = shade[8:] - behind
            behind = behind + alpha[8:] * second
            first = shade[:8] - behind
            behind = behind + alpha[:8] * first
            first = weight[:8] * first
            second = weight[8:] * second
            slopes[here, :] = jnp.concatenate([first, second], 0)
        sums = [[], []]
        for b in range(blocks):
            upper, lower = [
                slopes[b * 128 : b * 128 + 128, side * 128 : side * 128 + 128].T
                for side in range(2)
            ]
            columns = [[], [], []]
            for x in range(0, 16, 8):
                parts = [jnp.zeros((8, 128), F32)] * 3
                for y in range(8):
                    near = lower[y * 16 + x : y * 16 + x + 8, :]
                    far = upper[112 - y * 16 + x : 120 - y * 16 + x, :]
                    both_sides = near + far
                    parts[0] = parts[0] + both_sides
                    parts[1] = parts[1] + (y + 0.5) * (near - far)
                    parts[2] = parts[2] + (y + 0.5) ** 2 * both_sides
                for k in range(3):
                    columns[k].append(parts[k])
            column = jnp.concatenate(columns[0] + columns[1] + columns[2], 0)
            column_high = column.astype(BF16).astype(F32)
            sums[0].append(column_high)
            sums[1].append(column - column_high)
        summed = jnp.concatenate([jnp.concatenate(part, 1) for part in sums], 0)
        column_ref[...] = summed.astype(BF16)
        for b in range(blocks):
            base = (i * blocks + b) * 16
            moments[base + 8 : base + 16, :] = tint_grad[:, b * 128 : b * 128 + 128]

    slot_ref[...] = jnp.zeros(slot_ref.shape, F32)
    moments[...] = jnp.zeros(moments.shape, F32)
    coefs[...] = jnp.zeros(coefs.shape, F32)
    for i in range(group):
        buffers[5 * i + 4][...] = jnp.zeros((96, length), BF16)
    gather(0)

    def step(g, carry):
        before = jnp.maximum(g - 1, 0)
        chain(before)
        ready = [operands(g * group + i, i) for i in range(group)]
        gather(jnp.minimum(g + 1, groups - 1))
        scatter(before)
        for i in range(group):
            render(i, *ready[i], *buffers[5 * i : 5 * i + 5])
        return carry

    lax.fori_loop(0, groups, step, 0)
    chain(groups - 1)
    scatter(groups - 1)

    half = rows // 2
    for c in range(PARAMS):
        high = slot_ref[2 * c * half : (2 * c + 1) * half, :]
        value = high + slot_ref[(2 * c + 1) * half : (2 * c + 2) * half, :]
        for row in range(rows):
            part = value[row // 2 : row // 2 + 1, row % 2 * 128 : row % 2 * 128 + 128]
            grad_ref[row, :, c * 128 : c * 128 + 128] = part


def post_kernel(
    half_height,
    raw,
    inverse_ref,
    shifts,
    table_ref,
    centre_out,
    scale_out,
    rotation_out,
    logit_out,
    colour_out,
    dense_out,
):
    rows = logit_out.shape[0]
    for chunk in range(rows // 8):
        parts = raw_rows(raw, rows, chunk)
        shift = [
            shifts[axis * rows + chunk * 8 : axis * rows + chunk * 8 + 8, :] for axis in range(3)
        ]
        _, pull = jax.vjp(lambda *args: project(args + (half_height,), shift), *parts)
        found = lookups(
            lambda c, row: table_ref[row, :, c * 128 : c * 128 + 128],
            inverse_ref[chunk * 8 : chunk * 8 + 8, :],
            rows,
            range(PARAMS),
        )
        back = pull(found)
        flat = back[0] + back[1] + back[2] + back[4]
        for k, value in enumerate(flat):
            dense_out[k * rows + chunk * 8 : k * rows + chunk * 8 + 8, :] = value
        logit_out[chunk * 8 : chunk * 8 + 8, :] = back[3]
    first = 0
    for ref in (centre_out, scale_out, rotation_out, colour_out):
        count = ref.shape[0]
        for row in range(rows):
            ref[:, row * 128 : row * 128 + 128] = dense_out[
                pl.ds(first + row, count, stride=rows), :
            ]
        first += count * rows


def exchange(table, peers, capacity):
    if capacity % 128 == 0:
        return lax.all_to_all(table, PEERS, split_axis=0, concat_axis=0, tiled=True)
    rows = table.shape[0]
    per = 128 // capacity
    chunks = table.reshape(rows, PARAMS, per, capacity).transpose(0, 2, 1, 3)
    chunks = chunks.reshape(peers, 1, PARAMS * capacity)
    moved = lax.all_to_all(chunks, PEERS, split_axis=0, concat_axis=0, tiled=True)
    moved = moved.reshape(rows, per, PARAMS, capacity).transpose(0, 2, 1, 3)
    return moved.reshape(rows, 1, ROW)


VMEM = pl.BlockSpec(memory_space=pltpu.VMEM)
HBM = pl.BlockSpec(memory_space=pltpu.HBM)
LIMIT = pltpu.CompilerParams(vmem_limit_bytes=40 * 1024 * 1024)


def shards(
    centres,
    log_scales,
    rotations,
    opacity_logits,
    colours,
    view_shift,
    tile_ids,
    tile_counts,
    tile_lists,
    send_index,
    image_cot,
):
    owned = centres.shape[1]
    rows = owned // 128
    peers, capacity = send_index.shape[1:]
    tiles, length = tile_lists.shape
    views = view_shift.shape[0]
    tiles_view = tiles * peers // views
    half_height = 8.0 * (tiles_view // TILES_X)
    assert peers * capacity == owned
    logits = opacity_logits.reshape(rows, 128)
    targets = send_index[0] if capacity % 128 == 0 else send_index.reshape(rows, 128)
    table_shape = jax.ShapeDtypeStruct((rows, 1, ROW), F32)
    whole = jax.ShapeDtypeStruct((rows, 128), jnp.int32)
    entry_shape = jax.ShapeDtypeStruct((tiles * length // 128, 128), jnp.int32)
    outgoing, inverse, shifts, raw, slots, marks = pl.pallas_call(
        lambda *refs: pre_kernel(half_height, tiles_view, *refs),
        out_shape=(
            table_shape,
            whole,
            jax.ShapeDtypeStruct((3 * rows, 128), F32),
            jax.ShapeDtypeStruct((14 * rows, 128), F32),
            entry_shape,
            entry_shape,
        ),
        in_specs=[HBM] * 10,
        out_specs=(VMEM,) * 6,
        scratch_shapes=[
            pltpu.SMEM(view_shift.shape, F32),
            pltpu.SMEM(tile_counts.shape, jnp.int32),
            pltpu.SMEM(tile_ids.shape, jnp.int32),
        ]
        + [pltpu.VMEM((n, owned), F32) for n in (3, 3, 4, 3)]
        + [
            pltpu.VMEM(targets.shape, jnp.int32),
            pltpu.VMEM(tile_lists.shape, jnp.int32),
            pltpu.VMEM((rows, 128), jnp.int32),
            pltpu.VMEM((PARAMS * rows, 128), F32),
            pltpu.SemaphoreType.DMA((10,)),
        ],
        compiler_params=LIMIT,
        name="project_and_pack",
    )(
        *[
            pltpu.with_memory_space_constraint(array, pltpu.HBM)
            for array in (
                view_shift,
                tile_counts,
                tile_ids,
                centres,
                log_scales,
                rotations,
                logits,
                colours,
                targets,
                tile_lists,
            )
        ],
    )
    received = exchange(outgoing, peers, capacity)
    rendered, slot_grads = pl.pallas_call(
        lambda *refs: render_kernel(length, *refs),
        out_shape=(jax.ShapeDtypeStruct((3, tiles * 256), F32), table_shape),
        in_specs=[VMEM] * 4,
        out_specs=(VMEM,) * 2,
        scratch_shapes=[
            pltpu.VMEM((tiles * length // 1024, 6, 8, 128), F32),
            pltpu.VMEM((128, 128), F32),
            pltpu.VMEM((128, 128), F32),
            pltpu.VMEM((2 * PARAMS, 8, 128), F32),
            pltpu.VMEM((PARAMS * rows, 256), F32),
        ]
        + [
            pltpu.VMEM((length, 256), F32),
            pltpu.VMEM((length, 256), F32),
            pltpu.VMEM((length, 512), BF16),
            pltpu.VMEM((length, 256), F32),
            pltpu.VMEM((96, length), BF16),
        ]
        * (1024 // length),
        compiler_params=LIMIT,
        name="render",
    )(received, slots, marks, image_cot)
    returned = exchange(slot_grads, peers, capacity)
    shapes = [jax.ShapeDtypeStruct((n, owned), F32) for n in (3, 3, 4, 3)]
    shapes.insert(3, jax.ShapeDtypeStruct((rows, 128), F32))
    grads = pl.pallas_call(
        lambda *refs: post_kernel(half_height, *refs),
        out_shape=tuple(shapes),
        in_specs=[VMEM] * 4,
        out_specs=(VMEM,) * 5,
        scratch_shapes=[pltpu.VMEM((13 * rows, 128), F32)],
        compiler_params=LIMIT,
        name="unpack_and_project_back",
    )(raw, inverse, shifts, returned)
    return (rendered, grads[0], grads[1], grads[2], grads[3].reshape(owned), grads[4])


def solution(mesh):
    wide = P(None, AXES)
    flat = P(AXES)
    return jax.shard_map(
        shards,
        mesh=mesh,
        in_specs=(
            wide,
            wide,
            wide,
            flat,
            wide,
            P("groups", None),
            flat,
            flat,
            P(AXES, None),
            P(AXES, None, None),
            wide,
        ),
        out_specs=(wide, wide, wide, wide, flat, wide),
        check_vma=False,
    )
```

```python
import math

import jax
import jax.numpy as jnp
from jax import lax
from jax.experimental import pallas as pl
from jax.experimental.pallas import tpu as pltpu
from jax.sharding import PartitionSpec as P

TILES_X = 32
FOCAL = 512.0
SH_ZERO = 0.28209479177387814
DILATION = 0.3
BACKGROUND = 1.0
DEPTH_OFFSET = 4.0
LOG2E = math.log2(math.e)
PARAMS = 9
ROW = PARAMS * 128
AXES = ("groups", "gs", "sub")
PEERS = ("gs", "sub")

BF16 = jnp.bfloat16
F32 = jnp.float32
NN = (((1,), (0,)), ((), ()))
NT = (((1,), (1,)), ((), ()))
TN = (((0,), (0,)), ((), ()))


def dot(lhs, rhs, dims=NN):
    return lax.dot_general(lhs, rhs, dims, preferred_element_type=F32)


def iota(shape, dim):
    return lax.broadcasted_iota(jnp.int32, shape, dim)


def halves(value):
    high = value.astype(BF16)
    return high, (value - high.astype(F32)).astype(BF16)


def lookups(row_of, index, rows, channels):
    low = index & 127
    high = index >> 7
    found = [jnp.zeros(index.shape, F32) for _ in channels]
    for row in range(rows):
        is_row = high == row
        for at, c in enumerate(channels):
            value = jnp.broadcast_to(row_of(c, row), index.shape)
            value = jnp.take_along_axis(value, low, axis=1, mode="promise_in_bounds")
            found[at] = jnp.where(is_row, value, found[at])
    return found


def shown(logit):
    return 1.0 / (1.0 + jnp.exp(-logit))


def tint(colour):
    return 0.5 + SH_ZERO * colour


def project(raw, shift):
    centres, log_scales, rotations, logit, colours, half_height = raw
    half_width = 8.0 * TILES_X
    camera_x = centres[0] + shift[0]
    camera_y = centres[1] + shift[1]
    camera_z = centres[2] + shift[2] + DEPTH_OFFSET
    inv_norm = 1.0 / jnp.sqrt(sum(part * part for part in rotations))
    quat_w, quat_x, quat_y, quat_z = [part * inv_norm for part in rotations]
    rotation = [
        [
            1.0 - 2.0 * (quat_y * quat_y + quat_z * quat_z),
            2.0 * (quat_x * quat_y - quat_w * quat_z),
            2.0 * (quat_x * quat_z + quat_w * quat_y),
        ],
        [
            2.0 * (quat_x * quat_y + quat_w * quat_z),
            1.0 - 2.0 * (quat_x * quat_x + quat_z * quat_z),
            2.0 * (quat_y * quat_z - quat_w * quat_x),
        ],
        [
            2.0 * (quat_x * quat_z - quat_w * quat_y),
            2.0 * (quat_y * quat_z + quat_w * quat_x),
            1.0 - 2.0 * (quat_x * quat_x + quat_y * quat_y),
        ],
    ]
    scales = [jnp.exp(part) for part in log_scales]
    stretched = [[rotation[i][j] * scales[j] for j in range(3)] for i in range(3)]

    def covariance(i, j):
        return sum(stretched[i][mid] * stretched[j][mid] for mid in range(3))

    cov_xx, cov_xy, cov_xz = covariance(0, 0), covariance(0, 1), covariance(0, 2)
    cov_yy, cov_yz, cov_zz = covariance(1, 1), covariance(1, 2), covariance(2, 2)
    inv_z = 1.0 / camera_z
    focal_z = FOCAL * inv_z
    ratio_x = camera_x * inv_z
    ratio_y = camera_y * inv_z
    shear_x = -focal_z * ratio_x
    shear_y = -focal_z * ratio_y
    screen_xx = (
        focal_z * focal_z * cov_xx
        + 2.0 * focal_z * shear_x * cov_xz
        + shear_x * shear_x * cov_zz
        + DILATION
    )
    screen_yy = (
        focal_z * focal_z * cov_yy
        + 2.0 * focal_z * shear_y * cov_yz
        + shear_y * shear_y * cov_zz
        + DILATION
    )
    screen_xy = (
        focal_z * focal_z * cov_xy
        + focal_z * shear_y * cov_xz
        + shear_x * focal_z * cov_yz
        + shear_x * shear_y * cov_zz
    )
    inv_det = 1.0 / (screen_xx * screen_yy - screen_xy * screen_xy)
    return [
        FOCAL * ratio_x + half_width,
        FOCAL * ratio_y + half_height,
        screen_yy * inv_det,
        -screen_xy * inv_det,
        screen_xx * inv_det,
        shown(logit),
    ] + [tint(part) for part in colours]


def load_dense(ref, dense, first, rows):
    count = ref.shape[0]
    for row in range(rows):
        dense[pl.ds(first + row, count, stride=rows), :] = ref[:, row * 128 : row * 128 + 128]


def view_shifts(view, shift_ref):
    chosen = []
    for axis in range(3):
        value = jnp.full(view.shape, shift_ref[0, axis], F32)
        for other in range(1, shift_ref.shape[0]):
            value = jnp.where(view == other, shift_ref[other, axis], value)
        chosen.append(value)
    return chosen


def raw_rows(raw, rows, chunk):
    parts = [raw[i * rows + chunk * 8 : i * rows + chunk * 8 + 8, :] for i in range(14)]
    return parts[:3], parts[3:6], parts[6:10], parts[13], parts[10:13]


def pre_kernel(
    half_height,
    tiles_view,
    shift_hbm,
    count_hbm,
    id_hbm,
    centre_hbm,
    scale_hbm,
    rotation_hbm,
    logit_hbm,
    colour_hbm,
    send_hbm,
    list_hbm,
    out_ref,
    inverse_ref,
    shifts,
    raw,
    slots,
    marks,
    shift_ref,
    count_ref,
    id_ref,
    centre_ref,
    scale_ref,
    rotation_ref,
    colour_ref,
    send_ref,
    list_ref,
    index,
    table,
    arrived,
):
    rows = table.shape[0] // PARAMS
    owned = rows * 128
    logit_ref = raw.at[pl.ds(13 * rows, rows), :]
    pairs = [
        (send_hbm, send_ref),
        (shift_hbm, shift_ref),
        (centre_hbm, centre_ref),
        (scale_hbm, scale_ref),
        (rotation_hbm, rotation_ref),
        (colour_hbm, colour_ref),
        (logit_hbm, logit_ref),
        (list_hbm, list_ref),
        (count_hbm, count_ref),
        (id_hbm, id_ref),
    ]
    copies = [
        pltpu.make_async_copy(source, target, arrived.at[i])
        for i, (source, target) in enumerate(pairs)
    ]
    for copy in copies:
        copy.start()
    for copy in copies[:7]:
        copy.wait()
    per = send_ref.shape[1] // 128
    peers = send_ref.shape[0]
    for part in range(per):
        index[pl.ds(part, peers, stride=per), :] = send_ref[:, part * 128 : part * 128 + 128]
    first = 0
    for ref in (centre_ref, scale_ref, rotation_ref, colour_ref):
        load_dense(ref, raw, first, rows)
        first += ref.shape[0] * rows
    for chunk in range(rows // 8):
        _, _, _, logit, colours = raw_rows(raw, rows, chunk)
        for c, value in enumerate([shown(logit)] + [tint(part) for part in colours]):
            at = (5 + c) * rows + chunk * 8
            table[at : at + 8, :] = value

    def gather(channels):
        for i in range(rows // 8):
            local = index[i * 8 : i * 8 + 8, :] % owned
            found = lookups(
                lambda c, row: table[c * rows + row : c * rows + row + 1, :],
                local,
                rows,
                channels,
            )
            for value, c in zip(found, channels):
                for s in range(8):
                    out_ref[i * 8 + s, :, c * 128 : c * 128 + 128] = value[s : s + 1, :]

    gather(range(5, PARAMS))
    total = jnp.zeros((2 * rows, 128), F32)
    group = 8
    for start in range(0, rows, group):
        lefts, rights = [], []
        for row in range(start, start + group):
            entry = index[row : row + 1, :]
            local = entry % owned
            slot = row * 128 + iota((1, 128), 1)
            first = (slot >> 6).astype(F32)
            second = ((slot & 63) + 64 * (entry // owned)).astype(F32)
            match = jnp.broadcast_to(local >> 7, (rows, 128)) == iota((rows, 128), 0)
            lefts.append(
                jnp.concatenate([jnp.where(match, first, 0.0), jnp.where(match, second, 0.0)], 0)
            )
            rights.append(
                jnp.where(
                    jnp.broadcast_to(local & 127, (128, 128)) == iota((128, 128), 0), 1.0, 0.0
                )
            )
        left = jnp.concatenate(lefts, 1).astype(BF16)
        right = jnp.concatenate(rights, 1).astype(BF16)
        total = total + dot(left, right, NT)
    whole = (total + 0.5).astype(jnp.int32)
    second = whole[rows:]
    inverse_ref[...] = whole[:rows] * 64 + (second & 63)
    view = second >> 6
    for chunk in range(rows // 8):
        parts = raw_rows(raw, rows, chunk)
        shift = view_shifts(view[chunk * 8 : chunk * 8 + 8, :], shift_ref)
        for axis in range(3):
            shifts[axis * rows + chunk * 8 : axis * rows + chunk * 8 + 8, :] = shift[axis]
        for c, value in enumerate(project(parts + (half_height,), shift)[:5]):
            table[c * rows + chunk * 8 : c * rows + chunk * 8 + 8, :] = value
    gather(range(5))
    for copy in copies[7:]:
        copy.wait()
    tiles, length = list_ref.shape
    blocks = length // 128
    lane = iota((8, 128), 1)
    for b in range(blocks):
        entry = run_entry(lane, b, length)
        for i in range(tiles // 8):
            moved = jnp.zeros((8, 128), jnp.int32)
            for source in range(blocks):
                value = list_ref[i * 8 : i * 8 + 8, source * 128 : source * 128 + 128]
                taken = jnp.take_along_axis(
                    value, entry & 127, axis=1, mode="promise_in_bounds"
                )
                moved = jnp.where(entry >> 7 == source, taken, moved)
            slots[pl.ds(i * 8 * blocks + b, 8, stride=blocks), :] = moved
    for t in range(tiles):
        local = lax.rem(id_ref[t], tiles_view)
        mark = count_ref[t] + 1024 * local
        marks[t * blocks : t * blocks + blocks, :] = jnp.full((blocks, 128), mark, jnp.int32)


def run_entry(lane, block, length):
    return (lane & 7) * (length // 8) + block * 16 + (lane >> 3)


def render_kernel(
    length,
    table_ref,
    slots,
    marks,
    cot_ref,
    image_ref,
    grad_ref,
    gathered,
    coefs,
    moments,
    grads,
    slot_ref,
    *buffers,
):
    blocks = length // 128
    tiles = slots.shape[0] // blocks
    rows = table_ref.shape[0]
    group = 8 // blocks
    steps = length // 16
    groups = tiles // group
    lane = iota((8, 128), 1)
    block_of = iota((8, 128), 0) % blocks

    feature = iota((8, 256), 0)
    pixel = iota((8, 256), 1)
    px = (pixel & 15).astype(F32) - 7.5
    py = (pixel >> 4).astype(F32) - 7.5
    features = jnp.where(feature == 0, px * px, 0.0)
    for k, value in enumerate([py * py, px * py, px, py, jnp.ones_like(px)]):
        features = jnp.where(feature == k + 1, value, features)
    blank = jnp.zeros((24, 256), F32)
    moment = iota((16, 96), 0)
    power = iota((16, 96), 1) % 48 // 16
    at = (iota((16, 96), 1) % 16).astype(F32) - 7.5
    moment_rows = jnp.zeros((16, 96), F32)
    for k, (y_power, value) in enumerate(
        [(0, at * at), (2, 1.0), (1, at), (0, at), (1, 1.0), (0, 1.0)]
    ):
        moment_rows = jnp.where((moment == k) & (power == y_power), value, moment_rows)
    moment_rows = moment_rows.astype(BF16)
    run_row = iota((8, 256), 0)

    def earlier_product(value):
        for step in (1, 2, 4):
            moved = pltpu.roll(value, step, 0)
            value = value * jnp.where(run_row >= step, moved, 1.0)
        return jnp.where(run_row >= 1, pltpu.roll(value, 1, 0), 1.0)

    def later_sum(value):
        for step in (1, 2, 4):
            moved = pltpu.roll(value, 8 - step, 0)
            value = value + jnp.where(run_row < 8 - step, moved, 0.0)
        return jnp.where(run_row < 7, pltpu.roll(value, 7, 0), 0.0)

    def spread(k):
        return pl.ds(k, 8, stride=16)

    def placed(g, params):
        u, w, a, b, e, o = params
        mark = marks[pl.ds(pl.multiple_of(g * 8, 8), 8), :]
        local = mark >> 10
        mid_x = (16 * lax.rem(local, TILES_X) + 8).astype(F32)
        mid_y = (16 * lax.div(local, TILES_X) + 8).astype(F32)
        return u - mid_x, w - mid_y, a, b, e, o, mark & 1023

    def gather(g):
        index = slots[pl.ds(pl.multiple_of(g * 8, 8), 8), :]
        found = lookups(
            lambda c, row: table_ref[row, :, c * 128 : c * 128 + 128],
            index,
            rows,
            range(PARAMS),
        )
        for c in range(6):
            gathered[g, c] = found[c]
        du, dw, a, b, e, o, live = placed(g, found[:6])
        entry = (lane & 7) * (length // 8) + block_of * 16 + (lane >> 3)
        is_live = entry < live
        slope_x = a * du + b * dw
        slope_y = e * dw + b * du
        level = -0.5 * (du * slope_x + dw * slope_y) + jnp.log(o)
        values = [-0.5 * a, -0.5 * e, -b, slope_x, slope_y, level]
        for k, value in enumerate(values):
            dead = -1000.0 if k == 5 else 0.0
            coefs[spread(k), :] = jnp.where(is_live, value * LOG2E, dead)
        for k in range(3):
            coefs[spread(8 + k), :] = found[6 + k] - BACKGROUND

    def chain(g):
        for i in range(group):
            summed = dot(moment_rows, buffers[5 * i + 4][...])
            for b in range(blocks):
                base = (i * blocks + b) * 16
                moments[base : base + 8, :] = summed[:8, b * 128 : b * 128 + 128]
        du, dw, a, b, e, o, _ = placed(g, [gathered[g, c] for c in range(6)])
        m_xx, m_yy, m_xy, m_x, m_y, m_one = [moments[spread(k), :] for k in range(6)]
        d_x = m_x - du * m_one
        d_y = m_y - dw * m_one
        values = [
            a * d_x + b * d_y,
            e * d_y + b * d_x,
            -0.5 * (m_xx - du * (m_x + d_x)),
            -(m_xy - dw * m_x - du * d_y),
            -0.5 * (m_yy - dw * (m_y + d_y)),
            m_one / o,
        ] + [moments[spread(8 + k), :] for k in range(3)]
        for c, value in enumerate(values):
            high = value.astype(BF16).astype(F32)
            grads[2 * c] = high
            grads[2 * c + 1] = value - high

    def scatter(g):
        index = slots[pl.ds(pl.multiple_of(g * 8, 8), 8), :]
        lefts, rights = [], []
        number = iota((256, 128), 0).astype(F32).astype(BF16)
        for r in range(8):
            slot = index[r : r + 1, :]
            match = jnp.broadcast_to(slot >> 8, (rows // 2, 128)) == iota((rows // 2, 128), 0)
            low = (slot & 255).astype(F32).astype(BF16)
            where = jnp.broadcast_to(low, (256, 128)) == number
            rights.append(jnp.where(where, jnp.ones((), BF16), jnp.zeros((), BF16)))
            parts = [
                jnp.where(match, jnp.broadcast_to(grads[c, r : r + 1, :], match.shape), 0.0)
                for c in range(2 * PARAMS)
            ]
            lefts.append(jnp.concatenate(parts, 0).astype(BF16))
        slot_ref[...] += dot(jnp.concatenate(lefts, 1), jnp.concatenate(rights, 1), NT)

    def operands(t, i):
        lanes = pl.ds(pl.multiple_of(t * 256, 256), 256)
        cot = jnp.concatenate([cot_ref[:, lanes], jnp.zeros((5, 256), F32)], 0)
        cot_high = cot.astype(BF16).astype(F32)
        cot_low = cot - cot_high
        right = jnp.concatenate(
            [
                jnp.concatenate([features, features, features, blank], 0),
                jnp.concatenate([blank, cot_high, cot_high, cot_low], 0),
            ],
            1,
        ).astype(BF16)
        cot_rows = jnp.concatenate([cot_high, cot_low], 0)
        cot_rows = jnp.concatenate([cot_rows, cot_rows], 1).astype(BF16)
        lefts, tints = [], []
        for b in range(blocks):
            base = (i * blocks + b) * 16
            coef = coefs[base : base + 8, :]
            tint = coefs[base + 8 : base + 16, :]
            coef_high = coef.astype(BF16).astype(F32)
            rest = coef - coef_high
            coef_mid = rest.astype(BF16).astype(F32)
            tint_high = tint.astype(BF16).astype(F32)
            tint_low = tint - tint_high
            lefts.append(
                jnp.concatenate(
                    [coef_high, coef_mid, rest - coef_mid, tint_high, tint_low, tint_high], 0
                )
            )
            tints.append(jnp.concatenate([tint_high, tint_low], 0))
        left = jnp.concatenate(lefts, 1).astype(BF16)
        tint_rows = jnp.concatenate(tints, 1).astype(BF16)
        return lanes, cot_rows, tint_rows, dot(left, right, TN)

    def render(i, lanes, cot_rows, tint_rows, both, alpha_ref, weight_ref, weights, slopes, column_ref):
        through = jnp.ones((8, 256), F32)
        total = jnp.zeros((8, 256), F32)
        for step in range(steps):
            here = slice(step * 16, step * 16 + 16)
            alpha = jnp.exp2(both[here, :256])
            alpha_ref[here, :] = alpha
            first = alpha[:8] * through
            through = through - first
            second = alpha[8:] * through
            through = through - second
            weight = jnp.concatenate([first, second], 0)
            weight_ref[here, :] = weight
            share = weight * both[here, 256:]
            total = total + (share[:8] + share[8:])
        reach = earlier_product(through)
        behind = later_sum(total * reach) / (reach * through)
        for step in reversed(range(steps)):
            here = slice(step * 16, step * 16 + 16)
            alpha = alpha_ref[here, :]
            shade = both[here, 256:]
            weight = weight_ref[here, :]
            weight = jnp.concatenate([weight[:8] * reach, weight[8:] * reach], 0)
            high, low = halves(weight)
            weights[here, :256] = high
            weights[here, 256:] = low
            second = shade[8:] - behind
            behind = behind + alpha[8:] * second
            first = shade[:8] - behind
            behind = behind + alpha[:8] * first
            slopes[here, :] = jnp.concatenate([weight[:8] * first, weight[8:] * second], 0)
        image = dot(tint_rows, weights[:, :256])
        image_ref[:, lanes] = BACKGROUND + (image[:8] + image[8:])[:3]
        tint_grad = dot(cot_rows, weights[...], NT)
        tint_grad = tint_grad[:8] + tint_grad[8:]
        sums = [[], []]
        for b in range(blocks):
            upper, lower = [
                slopes[b * 128 : b * 128 + 128, side * 128 : side * 128 + 128].T
                for side in range(2)
            ]
            columns = [[], [], []]
            for x in range(0, 16, 8):
                parts = [jnp.zeros((8, 128), F32)] * 3
                for y in range(8):
                    near = lower[y * 16 + x : y * 16 + x + 8, :]
                    far = upper[112 - y * 16 + x : 120 - y * 16 + x, :]
                    both_sides = near + far
                    parts[0] = parts[0] + both_sides
                    parts[1] = parts[1] + (y + 0.5) * (near - far)
                    parts[2] = parts[2] + (y + 0.5) ** 2 * both_sides
                for k in range(3):
                    columns[k].append(parts[k])
            column = jnp.concatenate(columns[0] + columns[1] + columns[2], 0)
            column_high = column.astype(BF16).astype(F32)
            sums[0].append(column_high)
            sums[1].append(column - column_high)
        summed = jnp.concatenate([jnp.concatenate(part, 1) for part in sums], 0)
        column_ref[...] = summed.astype(BF16)
        for b in range(blocks):
            base = (i * blocks + b) * 16
            moments[base + 8 : base + 16, :] = tint_grad[:, b * 128 : b * 128 + 128]

    slot_ref[...] = jnp.zeros(slot_ref.shape, F32)
    moments[...] = jnp.zeros(moments.shape, F32)
    coefs[...] = jnp.zeros(coefs.shape, F32)
    for i in range(group):
        buffers[5 * i + 4][...] = jnp.zeros((96, length), BF16)
    gather(0)

    def step(g, carry):
        before = jnp.maximum(g - 1, 0)
        chain(before)
        ready = [operands(g * group + i, i) for i in range(group)]
        gather(jnp.minimum(g + 1, groups - 1))
        scatter(before)
        for i in range(group):
            render(i, *ready[i], *buffers[5 * i : 5 * i + 5])
        return carry

    lax.fori_loop(0, groups, step, 0)
    chain(groups - 1)
    scatter(groups - 1)

    half = rows // 2
    for c in range(PARAMS):
        high = slot_ref[2 * c * half : (2 * c + 1) * half, :]
        value = high + slot_ref[(2 * c + 1) * half : (2 * c + 2) * half, :]
        for row in range(rows):
            part = value[row // 2 : row // 2 + 1, row % 2 * 128 : row % 2 * 128 + 128]
            grad_ref[row, :, c * 128 : c * 128 + 128] = part


def post_kernel(
    half_height,
    raw,
    inverse_ref,
    shifts,
    table_ref,
    centre_out,
    scale_out,
    rotation_out,
    logit_out,
    colour_out,
    dense_out,
):
    rows = logit_out.shape[0]
    for chunk in range(rows // 8):
        parts = raw_rows(raw, rows, chunk)
        shift = [
            shifts[axis * rows + chunk * 8 : axis * rows + chunk * 8 + 8, :] for axis in range(3)
        ]
        _, pull = jax.vjp(lambda *args: project(args + (half_height,), shift), *parts)
        found = lookups(
            lambda c, row: table_ref[row, :, c * 128 : c * 128 + 128],
            inverse_ref[chunk * 8 : chunk * 8 + 8, :],
            rows,
            range(PARAMS),
        )
        back = pull(found)
        flat = back[0] + back[1] + back[2] + back[4]
        for k, value in enumerate(flat):
            dense_out[k * rows + chunk * 8 : k * rows + chunk * 8 + 8, :] = value
        logit_out[chunk * 8 : chunk * 8 + 8, :] = back[3]
    first = 0
    for ref in (centre_out, scale_out, rotation_out, colour_out):
        count = ref.shape[0]
        for row in range(rows):
            ref[:, row * 128 : row * 128 + 128] = dense_out[
                pl.ds(first + row, count, stride=rows), :
            ]
        first += count * rows


def exchange(table, peers, capacity):
    if capacity % 128 == 0:
        return lax.all_to_all(table, PEERS, split_axis=0, concat_axis=0, tiled=True)
    rows = table.shape[0]
    per = 128 // capacity
    chunks = table.reshape(rows, PARAMS, per, capacity).transpose(0, 2, 1, 3)
    chunks = chunks.reshape(peers, 1, PARAMS * capacity)
    moved = lax.all_to_all(chunks, PEERS, split_axis=0, concat_axis=0, tiled=True)
    moved = moved.reshape(rows, per, PARAMS, capacity).transpose(0, 2, 1, 3)
    return moved.reshape(rows, 1, ROW)


VMEM = pl.BlockSpec(memory_space=pltpu.VMEM)
HBM = pl.BlockSpec(memory_space=pltpu.HBM)
LIMIT = pltpu.CompilerParams(vmem_limit_bytes=40 * 1024 * 1024)


def shards(
    centres,
    log_scales,
    rotations,
    opacity_logits,
    colours,
    view_shift,
    tile_ids,
    tile_counts,
    tile_lists,
    send_index,
    image_cot,
):
    owned = centres.shape[1]
    rows = owned // 128
    peers, capacity = send_index.shape[1:]
    tiles, length = tile_lists.shape
    views = view_shift.shape[0]
    tiles_view = tiles * peers // views
    half_height = 8.0 * (tiles_view // TILES_X)
    assert peers * capacity == owned
    logits = opacity_logits.reshape(rows, 128)
    targets = send_index[0] if capacity % 128 == 0 else send_index.reshape(rows, 128)
    table_shape = jax.ShapeDtypeStruct((rows, 1, ROW), F32)
    whole = jax.ShapeDtypeStruct((rows, 128), jnp.int32)
    entry_shape = jax.ShapeDtypeStruct((tiles * length // 128, 128), jnp.int32)
    outgoing, inverse, shifts, raw, slots, marks = pl.pallas_call(
        lambda *refs: pre_kernel(half_height, tiles_view, *refs),
        out_shape=(
            table_shape,
            whole,
            jax.ShapeDtypeStruct((3 * rows, 128), F32),
            jax.ShapeDtypeStruct((14 * rows, 128), F32),
            entry_shape,
            entry_shape,
        ),
        in_specs=[HBM] * 10,
        out_specs=(VMEM,) * 6,
        scratch_shapes=[
            pltpu.SMEM(view_shift.shape, F32),
            pltpu.SMEM(tile_counts.shape, jnp.int32),
            pltpu.SMEM(tile_ids.shape, jnp.int32),
        ]
        + [pltpu.VMEM((n, owned), F32) for n in (3, 3, 4, 3)]
        + [
            pltpu.VMEM(targets.shape, jnp.int32),
            pltpu.VMEM(tile_lists.shape, jnp.int32),
            pltpu.VMEM((rows, 128), jnp.int32),
            pltpu.VMEM((PARAMS * rows, 128), F32),
            pltpu.SemaphoreType.DMA((10,)),
        ],
        compiler_params=LIMIT,
        name="project_and_pack",
    )(
        *[
            pltpu.with_memory_space_constraint(array, pltpu.HBM)
            for array in (
                view_shift,
                tile_counts,
                tile_ids,
                centres,
                log_scales,
                rotations,
                logits,
                colours,
                targets,
                tile_lists,
            )
        ],
    )
    received = exchange(outgoing, peers, capacity)
    rendered, slot_grads = pl.pallas_call(
        lambda *refs: render_kernel(length, *refs),
        out_shape=(jax.ShapeDtypeStruct((3, tiles * 256), F32), table_shape),
        in_specs=[VMEM] * 4,
        out_specs=(VMEM,) * 2,
        scratch_shapes=[
            pltpu.VMEM((tiles * length // 1024, 6, 8, 128), F32),
            pltpu.VMEM((128, 128), F32),
            pltpu.VMEM((128, 128), F32),
            pltpu.VMEM((2 * PARAMS, 8, 128), F32),
            pltpu.VMEM((PARAMS * rows, 256), F32),
        ]
        + [
            pltpu.VMEM((length, 256), F32),
            pltpu.VMEM((length, 256), F32),
            pltpu.VMEM((length, 512), BF16),
            pltpu.VMEM((length, 256), F32),
            pltpu.VMEM((96, length), BF16),
        ]
        * (1024 // length),
        compiler_params=LIMIT,
        name="render",
    )(received, slots, marks, image_cot)
    returned = exchange(slot_grads, peers, capacity)
    shapes = [jax.ShapeDtypeStruct((n, owned), F32) for n in (3, 3, 4, 3)]
    shapes.insert(3, jax.ShapeDtypeStruct((rows, 128), F32))
    grads = pl.pallas_call(
        lambda *refs: post_kernel(half_height, *refs),
        out_shape=tuple(shapes),
        in_specs=[VMEM] * 4,
        out_specs=(VMEM,) * 5,
        scratch_shapes=[pltpu.VMEM((13 * rows, 128), F32)],
        compiler_params=LIMIT,
        name="unpack_and_project_back",
    )(raw, inverse, shifts, returned)
    return (rendered, grads[0], grads[1], grads[2], grads[3].reshape(owned), grads[4])


def solution(mesh):
    wide = P(None, AXES)
    flat = P(AXES)
    return jax.shard_map(
        shards,
        mesh=mesh,
        in_specs=(
            wide,
            wide,
            wide,
            flat,
            wide,
            P("groups", None),
            flat,
            flat,
            P(AXES, None),
            P(AXES, None, None),
            wide,
        ),
        out_specs=(wide, wide, wide, wide, flat, wide),
        check_vma=False,
    )
```
